32 devices in a mesh: dp: 4 (over y, x), ctx: 8 (over z, core).
Axes of the slice: x: 2, y: 2, z: 4, core: 2. Of those that a mesh axis runs over, the one named last changes fastest.
Arguments:
- tokens: bfloat16 [8192, 2048], P(('dp', 'ctx')), may hold values from -6 to 6
- in_weight: bfloat16 [3, 2048, 2048], P(None, ('dp', 'ctx')), may hold values from -0.125 to 0.125
- short_taps: float32 [7, 3, 2048], replicated, may hold values from -2.4 to 2.4
- long_taps: bfloat16 [128, 128], replicated, may hold values from -0.5 to 0.5
- out_weight: bfloat16 [2048, 2048], P(('dp', 'ctx')), may hold values from -0.125 to 0.125
Outputs:
- block_out: bfloat16 [8192, 2048], P(('dp', 'ctx'))
The draws below stay inside these ranges and needn't reach their ends.
All inputs are finite; a program needn't handle non-finite values.
Results may differ from the reference program's by a relative error of at most 0.0076.
Values may be sent and summed in bfloat16 or wider, within the bound.
No kernel may reach another device: no remote copies, remote signals or barrier semaphores. Data moves between devices by JAX's collectives and lax.ppermute only.
A program may use at most 128 MiB of HBM per device.

```python
import jax
import jax.numpy as jnp
from jax import lax

DIN = 2048
CH = 2048
DOUT = 2048
GSIZE = 16
SHORT = 7
TAPS = 128
GROUPS = 128
SEQS = 4
LEN = 2048
TOKENS = 8192


def levels(own_key, extent, split, low, high):
    factor_of, own = 1.0, jax.random.fold_in(own_key, 6)
    for dim, shards_of in split:
        steps = jnp.exp(jax.random.uniform(jax.random.fold_in(own, dim), (shards_of,), jnp.float32, low / len(split), high / len(split)))
        factor_of = factor_of * jnp.repeat(steps, extent[dim] // shards_of).reshape([-1 if axis == dim else 1 for axis in range(len(extent))])
    return factor_of


def centred(own_key, extent, spread, reach, cuts=(), kind=jnp.bfloat16):
    loudness = levels(own_key, extent, cuts, -0.22, 0.18) if cuts else 1.0
    result = jax.random.normal(own_key, extent, jnp.float32) * spread * loudness
    return jnp.minimum(jnp.maximum(result, -reach), reach).astype(kind)


def setup_inputs(seed: int = 0) -> dict:
    key_list = jax.random.split(jax.random.key(seed), 6)
    tokens = centred(key_list[0], (TOKENS, DIN), 1.0, 6.0, ((0, 32),))
    in_weight = centred(key_list[1], (3, CH, DIN), DIN ** -0.5, 0.125, ((1, 32),))
    short_taps = centred(key_list[2], (SHORT, 3, CH), 0.4, 2.4, (), jnp.float32)
    long_taps = centred(key_list[3], (GROUPS, TAPS), TAPS ** -0.5, 0.5)
    out_weight = centred(key_list[4], (CH, DOUT), CH ** -0.5, 0.125, ((0, 32),))
    return {"tokens": tokens, "in_weight": in_weight, "short_taps": short_taps, "long_taps": long_taps, "out_weight": out_weight}


def reference(tokens, in_weight, short_taps, long_taps, out_weight):
    seqs = tokens.reshape(SEQS, LEN, DIN)
    flat_in = in_weight.reshape(3 * CH, DIN)
    chan_filter = jnp.repeat(long_taps.astype(jnp.float32), GSIZE, axis=0)

    def one_sequence(seq):
        streams = jnp.dot(seq, flat_in.T, preferred_element_type=jnp.float32).astype(jnp.bfloat16)
        streams = lax.optimization_barrier(streams).astype(jnp.float32).reshape(LEN, 3, CH)
        padded = jnp.concatenate([jnp.zeros((SHORT - 1, 3, CH), jnp.float32), streams], axis=0)
        feat = jnp.zeros((LEN, 3, CH), jnp.float32)
        for j in range(SHORT):
            feat = feat + short_taps[j] * padded[SHORT - 1 - j:SHORT - 1 - j + LEN]
        gated = (feat[:, 1] * feat[:, 2]).astype(jnp.bfloat16)
        gated = lax.optimization_barrier(gated).astype(jnp.float32)
        padkv = jnp.concatenate([jnp.zeros((TAPS - 1, CH), jnp.float32), gated], axis=0)

        def tap_step(j, acc):
            start = (TAPS - 1 - j).astype(jnp.int32)
            window = lax.dynamic_slice_in_dim(padkv, start, LEN, 0)
            return acc + chan_filter[:, j] * window

        longconv = lax.fori_loop(0, TAPS, tap_step, jnp.zeros((LEN, CH), jnp.float32))
        mixed = (feat[:, 0] * longconv).astype(jnp.bfloat16)
        return jnp.dot(mixed, out_weight, preferred_element_type=jnp.float32).astype(jnp.bfloat16)

    outcome = lax.map(one_sequence, seqs)
    return outcome.reshape(TOKENS, DOUT)
```

```python
import functools

import jax
import jax.numpy as jnp
from jax import lax
from jax.experimental import pallas as pl
from jax.experimental.pallas import tpu as pltpu
from jax.sharding import Mesh
from jax.sharding import PartitionSpec as P

GSIZE = 16
SHORT = 7
TAPS = 128
EDGE = 144
LANES = 128
LEAD = 256


def ring_of(count):
    order = [i for i in range(count) if i == 0 or i % 2 == 1]
    order += [i for i in reversed(range(1, count)) if i % 2 == 0]
    return [(order[i], order[(i + 1) % count]) for i in range(count)]


def previous_of(count):
    table = [0] * count
    for source, target in ring_of(count):
        table[target] = source
    return table


def swap(block):
    return lax.ppermute(block, "core", [(0, 1), (1, 0)])


def nt(a, b):
    return lax.dot_general(a, b, (((1,), (1,)), ((), ())), preferred_element_type=jnp.float32)


def rounded(x):
    return x.astype(jnp.bfloat16).astype(jnp.float32)


def mix_kernel(
    core_ref, w_ref, own_ref, sib_ref, own_edge_ref, sib_edge_ref, taps_ref, long_ref, out_ref,
    streams, edge, tiles, gated,
):
    width = out_ref.shape[0]
    rows = own_ref.shape[1]
    half = own_edge_ref.shape[2]
    size = min(width, GSIZE)
    count = width // size
    core = core_ref[0]

    @pl.when(pl.program_id(0) == 0)
    def _():
        for g in range(count):
            line = jnp.concatenate(
                [jnp.zeros((1, TAPS), jnp.float32), long_ref[g : g + 1, :]], axis=1
            )
            square = pltpu.roll(
                jnp.broadcast_to(line, (2 * TAPS, 2 * TAPS)), 0, 1, stride=1, stride_axis=0
            )
            tiles[g] = square[:, :TAPS].astype(jnp.bfloat16)
        edge[...] = jnp.zeros_like(edge)

    w = w_ref[...]
    mine = pl.multiple_of(LEAD + core * rows, LANES)
    theirs = pl.multiple_of(LEAD + (1 - core) * rows, LANES)
    streams[:, pl.ds(mine, rows)] = rounded(nt(w, own_ref[0]))
    streams[:, pl.ds(theirs, rows)] = rounded(nt(w, sib_ref[0]))
    w_mine = w_ref[:, pl.ds(pl.multiple_of(core * half, LANES), half)]
    w_theirs = w_ref[:, pl.ds(pl.multiple_of((1 - core) * half, LANES), half)]
    edge[:, :EDGE] = rounded(nt(w_mine, own_edge_ref[0]) + nt(w_theirs, sib_edge_ref[0]))
    streams[:, :LEAD] = pltpu.roll(edge[...], LEAD - EDGE, 1)

    total = LEAD + 2 * rows
    step = min(8, width)

    def feat(k, r, first):
        base = k * width + r
        x = streams[base : base + step, first - LANES : total]
        taps = taps_ref[base : base + step, :]
        acc = None
        for j in range(SHORT):
            term = taps[:, j : j + 1] * (x if j == 0 else pltpu.roll(x, j, 1))
            acc = term if acc is None else acc + term
        return acc[:, LANES:]

    blocks = 2 * rows // TAPS
    for r in range(0, width, step):
        both = feat(1, r, LANES) * feat(2, r, LANES)
        gated[r : r + step, :] = both
    for g in range(count):
        at = g * size
        part = gated[at : at + size, :].astype(jnp.bfloat16)
        window = jnp.concatenate(
            [part[:, b * TAPS : b * TAPS + 2 * TAPS] for b in range(blocks)], axis=0
        )
        conv = jnp.dot(window, tiles[g], preferred_element_type=jnp.float32)
        wide = jnp.concatenate([conv[b * size : (b + 1) * size] for b in range(blocks)], axis=1)
        query = jnp.concatenate([feat(0, at + r, LEAD) for r in range(0, size, step)], axis=0)
        out_ref[at : at + size, 0, :] = (query * wide).astype(jnp.bfloat16)


def mix_chunk(core, w, own, sib, own_edge, sib_edge, taps, filters):
    lines, features = w.shape
    width = lines // 3
    seqs, rows, _ = own.shape
    half = own_edge.shape[2]
    count = filters.shape[0]
    block = lambda shape: pl.BlockSpec(shape, lambda s: (s, 0, 0))
    full = lambda shape: pl.BlockSpec(shape, lambda s: (0,) * len(shape))
    return pl.pallas_call(
        mix_kernel,
        grid=(seqs,),
        out_shape=jax.ShapeDtypeStruct((seqs, width, 1, 2 * rows), jnp.bfloat16),
        in_specs=[
            pl.BlockSpec(memory_space=pltpu.SMEM),
            full((lines, features)),
            block((1, rows, features)),
            block((1, rows, features)),
            block((1, EDGE, half)),
            block((1, EDGE, half)),
            full(taps.shape),
            full(filters.shape),
        ],
        out_specs=pl.BlockSpec((None, width, 1, 2 * rows), lambda s: (s, 0, 0, 0)),
        scratch_shapes=[
            pltpu.VMEM((lines, LEAD + 2 * rows), jnp.float32),
            pltpu.VMEM((lines, LEAD), jnp.float32),
            pltpu.VMEM((count, 2 * TAPS, TAPS), jnp.bfloat16),
            pltpu.VMEM((width, LANES + 2 * rows), jnp.float32),
        ],
        compiler_params=pltpu.CompilerParams(vmem_limit_bytes=40 * 1024 * 1024),
        cost_estimate=pl.CostEstimate(
            flops=2 * seqs * 2 * rows * lines * features,
            bytes_accessed=2 * seqs * 2 * rows * features,
            transcendentals=0,
        ),
    )(core, w, own, sib, own_edge, sib_edge, taps, filters)


def shards(chips, tokens, in_weight, short_taps, long_taps, out_weight):
    _, width, features = in_weight.shape
    rows = tokens.shape[0]
    half = features // 2
    dp = lax.axis_index("dp")
    z = lax.axis_index("z")
    core = lax.axis_index("core")
    ring = ring_of(chips)

    pairs = lambda c: [(2 * i + 1, 2 * (i + 1) + c) for i in range(chips - 1)]
    last = tokens[rows - EDGE :]
    edge = lax.ppermute(last[:, :half], ("z", "core"), pairs(0)) + lax.ppermute(
        last[:, half:], ("z", "core"), pairs(1)
    )
    own = lax.all_gather(tokens, "dp")
    own_edge = lax.all_gather(edge, "dp")
    sib = swap(own)
    sib_edge = swap(own_edge)

    table = jnp.array(previous_of(chips), jnp.int32)
    w = in_weight
    v = out_weight
    outs = [v]
    mixed = []
    origin = z
    core_arg = core.reshape(1).astype(jnp.int32)
    for s in range(chips):
        base = ((dp * chips + origin) * 2 + core) * width
        taps = lax.dynamic_slice_in_dim(short_taps, base, width, 2)
        taps = jnp.pad(taps.reshape(SHORT, 3 * width).T, ((0, 0), (0, 1)))
        filters = lax.dynamic_slice_in_dim(
            long_taps, base // GSIZE, max(1, width // GSIZE), 0
        ).astype(jnp.float32)
        mixed.append(
            mix_chunk(
                core_arg, w.reshape(3 * width, features), own, sib, own_edge, sib_edge, taps, filters
            )
        )
        if s < chips - 1:
            v = lax.ppermute(v, "z", ring)
            w = lax.ppermute(w, "z", ring)
            outs.append(v)
            origin = table[origin]
    weights = lax.all_gather(jnp.stack(outs), "dp")
    stacked = jnp.concatenate(mixed, axis=2).reshape(-1, width, chips, 2 * rows)
    moved = lax.all_to_all(stacked, "dp", 0, 0, tiled=True)
    moved = jnp.swapaxes(moved, 1, 2).reshape(-1, 2 * rows)
    weights = weights.reshape(moved.shape[0], -1)
    part = lax.dot_general(
        moved, weights, (((0,), (0,)), ((), ())), preferred_element_type=jnp.float32
    ).reshape(2, rows, -1)
    mine = lax.dynamic_index_in_dim(part, core, 0, False)
    other = lax.dynamic_index_in_dim(part, 1 - core, 0, False).astype(jnp.bfloat16)
    return (mine + swap(other).astype(jnp.float32)).astype(jnp.bfloat16)


def solution(mesh):
    count = mesh.shape["dp"]
    chips = mesh.shape["ctx"] // 2
    fine = Mesh(mesh.devices.reshape(count, chips, 2), ("dp", "z", "core"))
    every = ("dp", "z", "core")
    in_specs = (P(every, None), P(None, every, None), P(), P(), P(every, None))
    return jax.shard_map(
        functools.partial(shards, chips),
        mesh=fine,
        in_specs=in_specs,
        out_specs=P(every, None),
        check_vma=False,
    )
```

```python
import functools

import jax
import jax.numpy as jnp
from jax import lax
from jax.experimental import pallas as pl
from jax.experimental.pallas import tpu as pltpu
from jax.sharding import Mesh
from jax.sharding import PartitionSpec as P

GSIZE = 16
SHORT = 7
TAPS = 128
EDGE = 144
LANES = 128
LEAD = 256
ANY = pl.BlockSpec(memory_space=pl.ANY)
SMEM = pl.BlockSpec(memory_space=pltpu.SMEM)
VMEM = pl.BlockSpec(memory_space=pltpu.VMEM)


def ring_of(count):
    order = [i for i in range(count) if i == 0 or i % 2 == 1]
    order += [i for i in reversed(range(1, count)) if i % 2 == 0]
    return [(order[i], order[(i + 1) % count]) for i in range(count)]


def origins_of(count):
    previous = dict((target, source) for source, target in ring_of(count))
    table = [list(range(count))]
    for _ in range(count - 1):
        table.append([previous[i] for i in table[-1]])
    return table


def swap(block):
    return lax.ppermute(block, "core", [(0, 1), (1, 0)])


def across(block, r):
    count = lax.axis_size("dp")
    return lax.ppermute(block, "dp", [(i, i ^ r) for i in range(count)])


def nt(a, b):
    return lax.dot_general(a, b, (((1,), (1,)), ((), ())), preferred_element_type=jnp.float32)


def tn(a, b):
    return lax.dot_general(a, b, (((0,), (0,)), ((), ())), preferred_element_type=jnp.float32)


def rounded(x):
    return x.astype(jnp.bfloat16).astype(jnp.float32)


def mix_kernel(places, slots, core_ref, w_ref, taps_ref, long_ref, *rest):
    pieces, rest = rest[: len(places)], rest[len(places) :]
    edges, rest = rest[:2], rest[2:]
    outs, rest = rest[:slots], rest[slots:]
    tokens, edge_tokens, streams, edge, tiles, gated, mixed, sems, edge_sems = rest
    lines = w_ref.shape[0]
    width = lines // 3
    rows = tokens.shape[2]
    half = edge_tokens.shape[3]
    size = min(width, GSIZE)
    count = width // size
    core = core_ref[0]

    copies = []
    for n, (slot, side, row) in enumerate(places):
        part = pieces[n]
        copies.append(
            (
                slot,
                pltpu.make_async_copy(
                    part, tokens.at[slot, side, pl.ds(row, part.shape[0])], sems.at[n]
                ),
            )
        )
    edge_copies = [
        pltpu.make_async_copy(edges[side], edge_tokens.at[side], edge_sems.at[side])
        for side in range(2)
    ]
    for copy in edge_copies:
        copy.start()
    for slot in range(slots):
        for owner, copy in copies:
            if owner == slot:
                copy.start()

    for g in range(count):
        line = jnp.concatenate(
            [jnp.zeros((1, TAPS), jnp.float32), long_ref[g : g + 1, :]], axis=1
        )
        square = pltpu.roll(
            jnp.broadcast_to(line, (2 * TAPS, 2 * TAPS)), 0, 1, stride=1, stride_axis=0
        )
        tiles[g] = square[:, :TAPS].astype(jnp.bfloat16)
    edge[...] = jnp.zeros_like(edge)
    for copy in edge_copies:
        copy.wait()

    total = LEAD + 2 * rows
    step = min(8, width)
    blocks = 2 * rows // TAPS
    mine = pl.multiple_of(LEAD + core * rows, LANES)
    theirs = pl.multiple_of(LEAD + (1 - core) * rows, LANES)
    w_mine = pl.ds(pl.multiple_of(core * half, LANES), half)
    w_theirs = pl.ds(pl.multiple_of((1 - core) * half, LANES), half)

    def feat(k, r, first):
        base = k * width + r
        x = streams[base : base + step, first - LANES : total]
        taps = taps_ref[base : base + step, :]
        acc = None
        for j in range(SHORT):
            term = taps[:, j : j + 1] * (x if j == 0 else pltpu.roll(x, j, 1))
            acc = term if acc is None else acc + term
        return acc[:, LANES:]

    def one(slot, carry):
        for k in range(slots):

            @pl.when(slot == k)
            def _():
                for owner, copy in copies:
                    if owner == k:
                        copy.wait()

        w = w_ref[...]
        streams[:, pl.ds(mine, rows)] = rounded(nt(w, tokens[slot, 0]))
        streams[:, pl.ds(theirs, rows)] = rounded(nt(w, tokens[slot, 1]))
        edge[:, :EDGE] = rounded(
            nt(w_ref[:, w_mine], edge_tokens[0, slot])
            + nt(w_ref[:, w_theirs], edge_tokens[1, slot])
        )
        streams[:, :LEAD] = pltpu.roll(edge[...], LEAD - EDGE, 1)
        for r in range(0, width, step):
            gated[r : r + step, :] = feat(1, r, LANES) * feat(2, r, LANES)
        for g in range(count):
            at = g * size
            part = gated[at : at + size, :].astype(jnp.bfloat16)
            window = jnp.concatenate(
                [part[:, b * TAPS : b * TAPS + 2 * TAPS] for b in range(blocks)], axis=0
            )
            conv = jnp.dot(window, tiles[g], preferred_element_type=jnp.float32)
            wide = jnp.concatenate([conv[b * size : (b + 1) * size] for b in range(blocks)], axis=1)
            query = jnp.concatenate([feat(0, at + r, LEAD) for r in range(0, size, step)], axis=0)
            mixed[at : at + size, :] = (query * wide).astype(jnp.bfloat16)
        for k in range(slots):

            @pl.when(slot == k)
            def _():
                outs[k][...] = mixed[...]

        return carry

    lax.fori_loop(0, slots, one, 0)


def mix_chunk(core, w, taps, filters, places, pieces, edges):
    lines, features = w.shape
    width = lines // 3
    slots, _, half = edges[0].shape
    rows = max(row + p.shape[0] for (_, _, row), p in zip(places, pieces))
    count = filters.shape[0]
    return pl.pallas_call(
        functools.partial(mix_kernel, places, slots),
        out_shape=[jax.ShapeDtypeStruct((width, 2 * rows), jnp.bfloat16)] * slots,
        in_specs=[SMEM, VMEM, VMEM, VMEM] + [ANY] * (len(pieces) + 2),
        out_specs=[VMEM] * slots,
        scratch_shapes=[
            pltpu.VMEM((slots, 2, rows, features), jnp.bfloat16),
            pltpu.VMEM((2, slots, EDGE, half), jnp.bfloat16),
            pltpu.VMEM((lines, LEAD + 2 * rows), jnp.float32),
            pltpu.VMEM((lines, LEAD), jnp.float32),
            pltpu.VMEM((count, 2 * TAPS, TAPS), jnp.bfloat16),
            pltpu.VMEM((width, LANES + 2 * rows), jnp.float32),
            pltpu.VMEM((width, 2 * rows), jnp.bfloat16),
            pltpu.SemaphoreType.DMA((len(pieces),)),
            pltpu.SemaphoreType.DMA((2,)),
        ],
        compiler_params=pltpu.CompilerParams(vmem_limit_bytes=44 * 1024 * 1024),
        cost_estimate=pl.CostEstimate(
            flops=2 * slots * 2 * rows * lines * features,
            bytes_accessed=2 * slots * 2 * rows * features,
            transcendentals=0,
        ),
    )(core, w, taps, filters, *pieces, *edges)


def out_kernel(count, core_ref, *refs):
    parts, weights = refs[:count], refs[count : 2 * count]
    out_ref, left, right, sems = refs[2 * count :]
    depth = parts[0].shape[0]
    rows = out_ref.shape[0]
    copies = []
    for n in range(count):
        here = pl.ds(n * depth, depth)
        copies.append(pltpu.make_async_copy(parts[n], left.at[here], sems.at[0, n]))
        copies.append(pltpu.make_async_copy(weights[n], right.at[here], sems.at[1, n]))
    for copy in copies:
        copy.start()
    for copy in copies:
        copy.wait()
    at = pl.multiple_of(core_ref[0] * rows, LANES)
    a = left[:, pl.ds(at, rows)].T
    tile = 512
    for t in range(0, out_ref.shape[1], tile):
        out_ref[:, t : t + tile] = jnp.dot(
            a, right[:, t : t + tile], preferred_element_type=jnp.float32
        ).astype(out_ref.dtype)


def project(which, parts, weights, dtype):
    count = len(parts)
    depth, span = parts[0].shape
    width = weights[0].shape[1]
    rows = span // 2
    return pl.pallas_call(
        functools.partial(out_kernel, count),
        out_shape=jax.ShapeDtypeStruct((rows, width), dtype),
        in_specs=[SMEM] + [ANY] * (2 * count),
        out_specs=VMEM,
        scratch_shapes=[
            pltpu.VMEM((count * depth, span), jnp.bfloat16),
            pltpu.VMEM((count * depth, width), jnp.bfloat16),
            pltpu.SemaphoreType.DMA((2, count)),
        ],
        compiler_params=pltpu.CompilerParams(vmem_limit_bytes=44 * 1024 * 1024),
        cost_estimate=pl.CostEstimate(
            flops=2 * rows * width * count * depth,
            bytes_accessed=2 * count * depth * (width + span),
            transcendentals=0,
        ),
    )(which, *parts, *weights)


def tie(*groups):
    return lax.optimization_barrier(groups)


def shards(chips, tokens, in_weight, short_taps, long_taps, out_weight):
    _, width, features = in_weight.shape
    rows = tokens.shape[0]
    half = features // 2
    slots = lax.axis_size("dp")
    dp = lax.axis_index("dp")
    z = lax.axis_index("z")
    core = lax.axis_index("core")
    ring = ring_of(chips)
    forward = lambda block: lax.ppermute(block, "z", ring)

    table = jnp.array(origins_of(chips), jnp.int32)
    origins = lax.dynamic_index_in_dim(table, z, 1, False)
    core_arg = core.reshape(1).astype(jnp.int32)
    taps, filters = [], []
    for s in range(chips):
        base = ((dp * chips + origins[s]) * 2 + core) * width
        part = lax.dynamic_slice_in_dim(short_taps, base, width, 2)
        taps.append(jnp.pad(part.reshape(SHORT, 3 * width).T, ((0, 0), (0, 1))))
        filters.append(
            lax.dynamic_slice_in_dim(
                long_taps, base // GSIZE, max(1, width // GSIZE), 0
            ).astype(jnp.float32)
        )

    pairs = lambda c: [(2 * i + 1, 2 * (i + 1) + c) for i in range(chips - 1)]
    last = tokens[rows - EDGE :]
    edge = lax.ppermute(last[:, :half], ("z", "core"), pairs(0)) + lax.ppermute(
        last[:, half:], ("z", "core"), pairs(1)
    )
    ws, vs = [in_weight], [out_weight]
    ws.append(forward(ws[0]))
    vs.append(forward(vs[0]))
    blocks = [tokens] + [None] * (slots - 1)
    twins = [swap(tokens)] + [None] * (slots - 1)
    quick = slots == 4
    for r in range(1, slots):
        if not (quick and r == 3):
            blocks[r] = across(tokens, r)
    near = jnp.stack([edge] + [across(edge, r) for r in range(1, slots)])
    (blocks, twins, ws, vs, near) = tie(blocks[:3] if quick else blocks, twins[:1], ws, vs, near)

    places = [(r, 0, 0) for r in range(3 if quick else slots)]
    pieces = list(blocks)
    ws.append(forward(ws[1]))
    vs.append(forward(vs[1]))
    twins = list(twins) + [swap(block) for block in blocks[1:]]
    halves = []
    if quick:
        halves = [across(blocks[2][: rows // 2], 1), across(blocks[1][rows // 2 :], 2)]
    far = swap(near)
    spread = lambda v: [v] + [across(v, r) for r in range(1, slots)]
    wide = [None] * chips
    wide[1] = spread(vs[1])
    (twins, halves, ws, vs, far, wide[1]) = tie(twins, halves, ws, vs, far, wide[1])

    if quick:
        places += [(3, 0, 0), (3, 0, rows // 2)]
        pieces += list(halves)
    places += [(r, 1, 0) for r in range(len(twins))]
    pieces += list(twins)
    if quick:
        places += [(3, 1, 0), (3, 1, rows // 2)]
        pieces += [swap(block) for block in halves]
    for s in range(3, chips):
        ws.append(forward(ws[s - 1]))
        vs.append(forward(vs[s - 1]))
    wide[0] = spread(vs[0])
    mix = lambda s: mix_chunk(
        core_arg,
        ws[s].reshape(3 * width, features),
        taps[s],
        filters[s],
        places,
        pieces,
        (near, far),
    )
    mixed = [mix(s) for s in range(3)]
    wide[2] = spread(vs[2])
    (mixed, ws, wide[0], wide[2]) = tie(mixed, ws, wide[0], wide[2])
    mixed = list(mixed) + [mix(s) for s in range(3, chips)]
    for s in range(3, chips):
        wide[s] = spread(vs[s])
    moved = [
        [m[0]] + [across(m[r], r) for r in range(1, slots)] for m in mixed
    ]
    if width % 16:
        join = lambda lists: [jnp.concatenate([one[r] for one in lists]) for r in range(slots)]
    else:
        join = lambda lists: [one[r] for one in lists for r in range(slots)]
    parts, weights = join(moved), join(wide)
    theirs = swap(project(1 - core_arg, parts, weights, jnp.bfloat16))
    mine = project(core_arg, parts, weights, jnp.float32)
    return (mine + theirs.astype(jnp.float32)).astype(jnp.bfloat16)


def solution(mesh):
    count = mesh.shape["dp"]
    chips = mesh.shape["ctx"] // 2
    fine = Mesh(mesh.devices.reshape(count, chips, 2), ("dp", "z", "core"))
    every = ("dp", "z", "core")
    in_specs = (P(every, None), P(None, every, None), P(), P(), P(every, None))
    return jax.shard_map(
        functools.partial(shards, chips),
        mesh=fine,
        in_specs=in_specs,
        out_specs=P(every, None),
        check_vma=False,
    )
```

```python
import functools

import jax
import jax.numpy as jnp
from jax import lax
from jax.experimental import pallas as pl
from jax.experimental.pallas import tpu as pltpu
from jax.sharding import Mesh
from jax.sharding import PartitionSpec as P

GSIZE = 16
SHORT = 7
TAPS = 128
EDGE = 144
LANES = 128
WIDE = 64
ANY = pl.BlockSpec(memory_space=pl.ANY)
SMEM = pl.BlockSpec(memory_space=pltpu.SMEM)
VMEM = pl.BlockSpec(memory_space=pltpu.VMEM)


def ring_of(count):
    order = [i for i in range(count) if i == 0 or i % 2 == 1]
    order += [i for i in reversed(range(1, count)) if i % 2 == 0]
    return [(order[i], order[(i + 1) % count]) for i in range(count)]


def origins_of(count):
    previous = dict((target, source) for source, target in ring_of(count))
    table = [list(range(count))]
    for _ in range(count - 1):
        table.append([previous[i] for i in table[-1]])
    return table


def swap(block):
    return lax.ppermute(block, "core", [(0, 1), (1, 0)])


def across(block, r):
    count = lax.axis_size("dp")
    return lax.ppermute(block, "dp", [(i, i ^ r) for i in range(count)])


def tn(a, b):
    return lax.dot_general(a, b, (((0,), (0,)), ((), ())), preferred_element_type=jnp.float32)


def rounded(x):
    return x.astype(jnp.bfloat16).astype(jnp.float32)


def dot(a, b):
    return jnp.dot(a, b, preferred_element_type=jnp.float32)


def mix_kernel(step, slots, place_ref, w_ref, taps_ref, long_ref, *rest):
    own_ref, sib_ref, near_ref, far_ref = rest[:4]
    outs, rest = rest[4 : 4 + slots], rest[4 + slots :]
    tokens, edges, wide_w, streams, query, gated, tiles, mixed, sems = rest
    rows = tokens.shape[2]
    half = edges.shape[3]
    core = place_ref[0]
    origin = place_ref[2 + step]
    count = WIDE // GSIZE

    copies = []
    for slot in range(slots):
        copies.append(
            [
                pltpu.make_async_copy(ref.at[at], dst.at[slot, side], sems.at[slot, n])
                for n, (ref, dst, side, at) in enumerate(
                    [
                        (near_ref, edges, 0, slot),
                        (far_ref, edges, 1, slot),
                        (own_ref, tokens, 0, lax.bitwise_xor(place_ref[1], slot)),
                        (sib_ref, tokens, 1, lax.bitwise_xor(place_ref[1], slot)),
                    ]
                )
            ]
        )
    for group in copies:
        for copy in group:
            copy.start()

    w = w_ref[...]
    pad = jnp.zeros((WIDE, w.shape[1]), w.dtype)
    wide_w[...] = jnp.concatenate([w[: 2 * WIDE], pad, w[2 * WIDE :]], axis=0).T
    filters = long_ref[origin]
    for g in range(count):
        line = jnp.concatenate([jnp.zeros((1, TAPS), jnp.float32), filters[g : g + 1, :]], axis=1)
        square = pltpu.roll(
            jnp.broadcast_to(line, (2 * TAPS, 2 * TAPS)), 0, 1, stride=1, stride_axis=0
        )
        tiles[g] = square[:, :TAPS].astype(jnp.bfloat16)
    taps = taps_ref[origin]

    blocks = 2 * rows // TAPS
    mine = pl.multiple_of(EDGE + core * rows, 16)
    theirs = pl.multiple_of(EDGE + (1 - core) * rows, 16)
    w_mine = pl.ds(pl.multiple_of(core * half, LANES), half)
    w_theirs = pl.ds(pl.multiple_of((1 - core) * half, LANES), half)
    band = 64

    def feat(at, lanes):
        total = None
        for j in range(SHORT):
            term = taps[j : j + 1, lanes] * streams[at - j : at - j + band, lanes]
            total = term if total is None else total + term
        return total

    def one(slot, carry):
        for k in range(slots):

            @pl.when(slot == k)
            def _():
                for copy in copies[k]:
                    copy.wait()

        streams[:EDGE, :] = rounded(
            dot(edges[slot, 0], wide_w[w_mine, :]) + dot(edges[slot, 1], wide_w[w_theirs, :])
        )
        streams[pl.ds(mine, rows), :] = rounded(dot(tokens[slot, 0], wide_w[...]))
        streams[pl.ds(theirs, rows), :] = rounded(dot(tokens[slot, 1], wide_w[...]))
        for at in range(EDGE - TAPS, EDGE + 2 * rows, band):
            first = feat(at, slice(0, LANES))
            second = feat(at, slice(LANES, 2 * LANES))
            here = at - (EDGE - TAPS)
            gated[here : here + band, :] = (first * second).astype(jnp.bfloat16)
            if at >= EDGE:
                query[at - EDGE : at - EDGE + band, :] = first
        turned = gated[...].T
        queries = query[...].T
        for g in range(count):
            part = turned[WIDE + g * GSIZE : WIDE + (g + 1) * GSIZE, :]
            window = jnp.concatenate(
                [part[:, b * TAPS : b * TAPS + 2 * TAPS] for b in range(blocks)], axis=0
            )
            conv = dot(window, tiles[g])
            row = jnp.concatenate(
                [conv[b * GSIZE : (b + 1) * GSIZE] for b in range(blocks)], axis=1
            )
            mixed[g * GSIZE : (g + 1) * GSIZE, :] = (
                queries[g * GSIZE : (g + 1) * GSIZE, :] * row
            ).astype(jnp.bfloat16)
        for k in range(slots):

            @pl.when(slot == k)
            def _():
                outs[k][...] = mixed[...]

        return carry

    lax.fori_loop(0, slots, one, 0)


def mix_chunk(step, place, w, taps, filters, own, sib, near, far):
    features = w.shape[1]
    slots, rows, _ = own.shape
    half = near.shape[2]
    count = WIDE // GSIZE
    return pl.pallas_call(
        functools.partial(mix_kernel, step, slots),
        out_shape=[jax.ShapeDtypeStruct((WIDE, 2 * rows), jnp.bfloat16)] * slots,
        in_specs=[SMEM, VMEM, VMEM, VMEM] + [ANY] * 4,
        out_specs=[VMEM] * slots,
        scratch_shapes=[
            pltpu.VMEM((slots, 2, rows, features), jnp.bfloat16),
            pltpu.VMEM((slots, 2, EDGE, half), jnp.bfloat16),
            pltpu.VMEM((features, 4 * WIDE), jnp.bfloat16),
            pltpu.VMEM((EDGE + 2 * rows, 4 * WIDE), jnp.float32),
            pltpu.VMEM((2 * rows, LANES), jnp.float32),
            pltpu.VMEM((TAPS + 2 * rows, LANES), jnp.bfloat16),
            pltpu.VMEM((count, 2 * TAPS, TAPS), jnp.bfloat16),
            pltpu.VMEM((WIDE, 2 * rows), jnp.bfloat16),
            pltpu.SemaphoreType.DMA((slots, 4)),
        ],
        compiler_params=pltpu.CompilerParams(vmem_limit_bytes=44 * 1024 * 1024),
        cost_estimate=pl.CostEstimate(
            flops=4 * slots * 2 * rows * 4 * WIDE * features,
            bytes_accessed=2 * slots * 2 * rows * features,
            transcendentals=0,
        ),
    )(place, w, taps, filters, own, sib, near, far)


def out_kernel(counts, core_ref, *refs):
    parts, refs = refs[: counts[0]], refs[counts[0] :]
    weights, refs = refs[: counts[1]], refs[counts[1] :]
    out_ref, left, right, sems = refs
    rows = out_ref.shape[0]
    copies = []
    for kind, (group, whole) in enumerate(((parts, left), (weights, right))):
        at = 0
        for n, ref in enumerate(group):
            here = pl.ds(at, ref.shape[0])
            copies.append(pltpu.make_async_copy(ref, whole.at[here], sems.at[kind, n]))
            at += ref.shape[0]
    for copy in copies:
        copy.start()
    for copy in copies:
        copy.wait()
    at = pl.multiple_of(core_ref[0] * rows, LANES)
    a = left[:, pl.ds(at, rows)].T
    tile = 512
    for t in range(0, out_ref.shape[1], tile):
        out_ref[:, t : t + tile] = dot(a, right[:, t : t + tile]).astype(out_ref.dtype)


def project(which, parts, weights, dtype):
    counts = (len(parts), len(weights))
    depth = sum(w.shape[0] for w in weights)
    span, width = parts[0].shape[1], weights[0].shape[1]
    rows = span // 2
    return pl.pallas_call(
        functools.partial(out_kernel, counts),
        out_shape=jax.ShapeDtypeStruct((rows, width), dtype),
        in_specs=[SMEM] + [ANY] * sum(counts),
        out_specs=VMEM,
        scratch_shapes=[
            pltpu.VMEM((depth, span), jnp.bfloat16),
            pltpu.VMEM((depth, width), jnp.bfloat16),
            pltpu.SemaphoreType.DMA((2, max(counts))),
        ],
        compiler_params=pltpu.CompilerParams(vmem_limit_bytes=44 * 1024 * 1024),
        cost_estimate=pl.CostEstimate(
            flops=4 * rows * width * depth,
            bytes_accessed=2 * depth * (width + span),
            transcendentals=0,
        ),
    )(which, *parts, *weights)


def tie(*groups):
    return lax.optimization_barrier(groups)


def shards(chips, tokens, in_weight, short_taps, long_taps, out_weight):
    _, width, features = in_weight.shape
    rows = tokens.shape[0]
    half = features // 2
    slots = lax.axis_size("dp")
    dp = lax.axis_index("dp")
    z = lax.axis_index("z")
    core = lax.axis_index("core")
    ring = ring_of(chips)
    forward = lambda block: lax.ppermute(block, "z", ring)

    table = jnp.array(origins_of(chips), jnp.int32)
    origins = lax.dynamic_index_in_dim(table, z, 1, False)
    place = jnp.concatenate([jnp.stack([core, dp]).astype(jnp.int32), origins])
    first = dp * chips * 2
    part = short_taps.reshape(SHORT, 3, -1, 2, width)
    part = lax.dynamic_slice(
        part, (0, 0, dp * chips, core, 0), (SHORT, 3, chips, 1, width)
    ).reshape(SHORT, 3, chips, width)
    part = jnp.pad(part, ((0, 1), (0, 0), (0, 0), (0, WIDE - width)))
    part = jnp.transpose(part, (2, 0, 1, 3))
    taps = jnp.concatenate(
        [part[:, :, 0], part[:, :, 1], jnp.zeros_like(part[:, :, 0]), part[:, :, 2]], axis=2
    )
    groups = max(1, width // GSIZE)
    each = jnp.stack(
        [
            lax.dynamic_slice_in_dim(
                long_taps, (first + 2 * i + core) * width // GSIZE, groups, 0
            )
            for i in range(chips)
        ]
    ).astype(jnp.float32)
    filters = jnp.pad(each, ((0, 0), (0, WIDE // GSIZE - groups), (0, 0)))

    own = lax.all_gather(tokens, "dp")
    pairs = lambda c: [(2 * i + 1, 2 * (i + 1) + c) for i in range(chips - 1)]
    last = tokens[rows - EDGE :]
    edge = lax.ppermute(last[:, :half], ("z", "core"), pairs(0)) + lax.ppermute(
        last[:, half:], ("z", "core"), pairs(1)
    )
    near = jnp.stack([edge] + [across(edge, r) for r in range(1, slots)])
    far = swap(near)

    ws, vs = [in_weight], [out_weight]
    for s in range(1, chips):
        ws.append(forward(ws[-1]))
        vs.append(forward(vs[-1]))
    every_v = jnp.concatenate(vs)

    own, far, every_v, ws[chips - 2] = tie(own, far, every_v, ws[chips - 2])
    if chips > 3:
        ws[chips - 1] = forward(ws[chips - 2])
    sib = swap(own)
    if slots == 4:
        v_x, v_y = across(every_v, 1), across(every_v, 2)
        cut = every_v.shape[0] // 2
        wide = [every_v, v_x, v_y, (across(v_y[:cut], 1), across(v_x[cut:], 2))]
    else:
        wide = [every_v] + [across(every_v, r) for r in range(1, slots)]
    lists = []
    for s in range(chips):
        w = ws[s]
        if width < WIDE:
            w = jnp.pad(w, ((0, 0), (0, WIDE - width), (0, 0)))
        mixed = mix_chunk(
            s, place, w.reshape(3 * WIDE, features), taps, filters, own, sib, near, far
        )
        mixed = [m[:width] for m in mixed]
        lists.append([mixed[0]] + [across(mixed[r], r) for r in range(1, slots)])
    parts, weights = [], []
    for r in range(slots):
        column = [one[r] for one in lists]
        parts += [jnp.concatenate(column)] if width < WIDE else column
        weights += list(wide[r]) if isinstance(wide[r], tuple) else [wide[r]]
    here = core.reshape(1).astype(jnp.int32)
    theirs = swap(project(1 - here, parts, weights, jnp.bfloat16))
    mine = project(here, parts, weights, jnp.float32)
    return (mine + theirs.astype(jnp.float32)).astype(jnp.bfloat16)


def solution(mesh):
    count = mesh.shape["dp"]
    chips = mesh.shape["ctx"] // 2
    fine = Mesh(mesh.devices.reshape(count, chips, 2), ("dp", "z", "core"))
    every = ("dp", "z", "core")
    in_specs = (P(every, None), P(None, every, None), P(), P(), P(every, None))
    return jax.shard_map(
        functools.partial(shards, chips),
        mesh=fine,
        in_specs=in_specs,
        out_specs=P(every, None),
        check_vma=False,
    )
```

```python
import functools

import jax
import jax.numpy as jnp
from jax import lax
from jax.experimental import pallas as pl
from jax.experimental.pallas import tpu as pltpu
from jax.sharding import Mesh
from jax.sharding import PartitionSpec as P

GSIZE = 16
SHORT = 7
TAPS = 128
LANES = 128
WIDE = 64
HALO = 160
ANY = pl.BlockSpec(memory_space=pl.ANY)
SMEM = pl.BlockSpec(memory_space=pltpu.SMEM)
VMEM = pl.BlockSpec(memory_space=pltpu.VMEM)
LIMIT = pltpu.CompilerParams(vmem_limit_bytes=48 * 1024 * 1024)


def ring_of(count):
    order = [i for i in range(count) if i == 0 or i % 2 == 1]
    order += [i for i in reversed(range(1, count)) if i % 2 == 0]
    return [(order[i], order[(i + 1) % count]) for i in range(count)]


def origins_of(count):
    previous = dict((target, source) for source, target in ring_of(count))
    table = [list(range(count))]
    for _ in range(count - 1):
        table.append([previous[i] for i in table[-1]])
    return table


def swap(block):
    return lax.ppermute(block, "core", [(0, 1), (1, 0)])


def across(block, r):
    count = lax.axis_size("dp")
    return lax.ppermute(block, "dp", [(i, i ^ r) for i in range(count)])


def tie(*groups):
    return lax.optimization_barrier(groups)


def dot(a, b):
    return jnp.dot(a, b, preferred_element_type=jnp.float32)


def nt(a, b):
    return lax.dot_general(a, b, (((1,), (1,)), ((), ())), preferred_element_type=jnp.float32)


def mix_kernel(step, slots, parts, place_ref, taps_ref, long_ref, wa_ref, wb_ref, *rest):
    pieces, rest = rest[: len(parts)], rest[len(parts) :]
    outs, rest = rest[:slots], rest[slots:]
    tokens, w, first, second, packed, turned, tiles, sems, w_sems = rest
    span = tokens.shape[1] - HALO
    rows = span // 2
    core = place_ref[0]
    origin = place_ref[2 + step]
    count = WIDE // GSIZE

    cut = wa_ref.shape[0]
    w_copies = [
        pltpu.make_async_copy(wa_ref, w.at[pl.ds(0, cut)], w_sems.at[0]),
        pltpu.make_async_copy(
            wb_ref.at[pl.ds(0, 2 * WIDE - cut)], w.at[pl.ds(cut, 2 * WIDE - cut)], w_sems.at[1]
        ),
        pltpu.make_async_copy(
            wb_ref.at[pl.ds(2 * WIDE - cut, WIDE)], w.at[pl.ds(3 * WIDE, WIDE)], w_sems.at[2]
        ),
    ]
    for copy in w_copies:
        copy.start()
    copies = [[] for _ in range(slots)]
    number = 0
    for ref, (slot, side, start) in zip(pieces, parts):
        owner = core if side == 0 else 1 - core
        end = start + ref.shape[0]
        bounds = []
        if start < rows:
            bounds.append((start, min(end, rows), HALO + owner * rows + start))
        if end > rows:
            low = max(start, rows)
            bounds.append((low, end, owner * (HALO // 2) + low - rows))
        for low, high, at in bounds:
            copies[slot].append(
                pltpu.make_async_copy(
                    ref.at[pl.ds(low - start, high - low)],
                    tokens.at[slot, pl.ds(pl.multiple_of(at, 16), high - low)],
                    sems.at[number],
                )
            )
            number += 1
    for group in copies:
        for copy in group:
            copy.start()

    w[2 * WIDE : 3 * WIDE, :] = jnp.zeros((WIDE, w.shape[1]), w.dtype)
    filters = long_ref[origin]
    for g in range(count):
        line = jnp.concatenate([jnp.zeros((1, TAPS), jnp.float32), filters[g : g + 1, :]], axis=1)
        square = pltpu.roll(
            jnp.broadcast_to(line, (2 * TAPS, 2 * TAPS)), 0, 1, stride=1, stride_axis=0
        )
        tiles[g] = square[:, :TAPS].astype(jnp.bfloat16)
    taps = taps_ref[origin]
    band = 64
    blocks = span // TAPS
    lower = lax.broadcasted_iota(jnp.int32, (band, LANES), 1) < WIDE

    def project_slot(slot):
        result = nt(tokens[slot], w[...]).astype(jnp.bfloat16).astype(jnp.float32)
        first[slot % 2] = result[:, :LANES]
        second[slot % 2] = result[:, LANES:]

    def feat(ref, slot, at, lanes):
        total = None
        for j in range(SHORT):
            term = taps[j : j + 1, lanes] * ref[slot % 2, at - j : at - j + band, :]
            total = term if total is None else total + term
        return total

    for copy in w_copies + copies[0]:
        copy.wait()
    project_slot(0)
    for slot in range(slots):
        if slot + 1 < slots:
            for copy in copies[slot + 1]:
                copy.wait()
            project_slot(slot + 1)
        for n in range((TAPS + span) // band):
            at = HALO - TAPS + n * band
            a = feat(first, slot, at, slice(0, LANES))
            b = feat(second, slot, at, slice(LANES, 2 * LANES))
            packed[slot % 2, n * band : (n + 1) * band, :] = jnp.where(lower, a, a * b).astype(
                jnp.bfloat16
            )
        turned[slot] = packed[slot % 2].T

    for g in range(count):
        channels = slice(WIDE + g * GSIZE, WIDE + (g + 1) * GSIZE)
        window = jnp.concatenate(
            [
                turned[slot, channels, b * TAPS : (b + 2) * TAPS]
                for slot in range(slots)
                for b in range(blocks)
            ],
            axis=0,
        )
        conv = dot(window, tiles[g])
        for slot in range(slots):
            row = jnp.concatenate(
                [
                    conv[(slot * blocks + b) * GSIZE : (slot * blocks + b + 1) * GSIZE]
                    for b in range(blocks)
                ],
                axis=1,
            )
            query = turned[slot, g * GSIZE : (g + 1) * GSIZE, TAPS:].astype(jnp.float32)
            outs[slot][g * GSIZE : (g + 1) * GSIZE, :] = (query * row).astype(jnp.bfloat16)


def mix_chunk(step, rows, slots, place, taps, filters, wa, wb, parts, pieces):
    features = wa.shape[1]
    count = WIDE // GSIZE
    return pl.pallas_call(
        functools.partial(mix_kernel, step, slots, parts),
        out_shape=[jax.ShapeDtypeStruct((WIDE, 2 * rows), jnp.bfloat16)] * slots,
        in_specs=[SMEM, VMEM, VMEM] + [ANY] * (2 + len(pieces)),
        out_specs=[VMEM] * slots,
        scratch_shapes=[
            pltpu.VMEM((slots, HALO + 2 * rows, features), jnp.bfloat16),
            pltpu.VMEM((4 * WIDE, features), jnp.bfloat16),
            pltpu.VMEM((2, HALO + 2 * rows, LANES), jnp.float32),
            pltpu.VMEM((2, HALO + 2 * rows, LANES), jnp.float32),
            pltpu.VMEM((2, TAPS + 2 * rows, LANES), jnp.bfloat16),
            pltpu.VMEM((slots, LANES, TAPS + 2 * rows), jnp.bfloat16),
            pltpu.VMEM((count, 2 * TAPS, TAPS), jnp.bfloat16),
            pltpu.SemaphoreType.DMA((2 * len(pieces),)),
            pltpu.SemaphoreType.DMA((3,)),
        ],
        compiler_params=LIMIT,
        cost_estimate=pl.CostEstimate(
            flops=4 * slots * 2 * rows * 4 * WIDE * features,
            bytes_accessed=2 * slots * 2 * rows * features,
            transcendentals=0,
        ),
    )(place, taps, filters, wa, wb, *pieces)


def out_kernel(mirror, slots, chips, width, place_ref, v_ref, *refs):
    parts = refs[: len(refs) - 5]
    out_ref, left, right, total, sems = refs[len(refs) - 5 :]
    rows = out_ref.shape[0]
    core, dp = place_ref[0], place_ref[1]
    if mirror:
        core = 1 - core
    depth = slots * width
    groups = []
    if width == WIDE:
        for s in range(chips):
            group = []
            for r in range(slots):
                source = lax.bitwise_xor(dp, r) * chips + place_ref[2 + s]
                here = pl.ds((s * slots + r) * width, width)
                n = s * slots + r
                group.append(pltpu.make_async_copy(parts[n], left.at[here], sems.at[0, n]))
                group.append(pltpu.make_async_copy(v_ref.at[source], right.at[here], sems.at[1, n]))
            groups.append((group, s * depth, depth))
    else:
        group = [
            pltpu.make_async_copy(parts[0], left, sems.at[0, 0]),
            pltpu.make_async_copy(v_ref, right, sems.at[1, 0]),
        ]
        groups.append((group, 0, depth * chips))
    for group, _, _ in groups:
        for copy in group:
            copy.start()
    at = pl.multiple_of(core * rows, LANES)
    tile = 512
    for n, (group, start, size) in enumerate(groups):
        for copy in group:
            copy.wait()
        a = left[start : start + size, pl.ds(at, rows)].T
        for t in range(0, out_ref.shape[1], tile):
            here = slice(t, t + tile)
            value = dot(a, right[start : start + size, here])
            if n:
                value = value + total[:, here]
            if n + 1 < len(groups):
                total[:, here] = value
            else:
                out_ref[:, here] = value.astype(out_ref.dtype)


def project(mirror, slots, chips, width, place, v, parts, dtype):
    span, features = parts[0].shape[1], v.shape[-1]
    rows, depth = span // 2, slots * chips * width
    return pl.pallas_call(
        functools.partial(out_kernel, mirror, slots, chips, width),
        out_shape=jax.ShapeDtypeStruct((rows, features), dtype),
        in_specs=[SMEM, ANY] + [ANY] * len(parts),
        out_specs=VMEM,
        scratch_shapes=[
            pltpu.VMEM((depth, span), jnp.bfloat16),
            pltpu.VMEM((depth, features), jnp.bfloat16),
            pltpu.VMEM((rows, features), jnp.float32),
            pltpu.SemaphoreType.DMA((2, len(parts))),
        ],
        compiler_params=LIMIT,
        cost_estimate=pl.CostEstimate(
            flops=4 * rows * features * depth,
            bytes_accessed=2 * depth * (features + span),
            transcendentals=0,
        ),
    )(place, v, *parts)


def local_filters(chips, width, dp, core, short_taps, long_taps):
    part = short_taps.reshape(SHORT, 3, -1, 2, width)
    part = lax.dynamic_slice(
        part, (0, 0, dp * chips, core, 0), (SHORT, 3, chips, 1, width)
    ).reshape(SHORT, 3, chips, width)
    part = jnp.pad(part, ((0, 1), (0, 0), (0, 0), (0, WIDE - width)))
    part = jnp.transpose(part, (2, 0, 1, 3))
    taps = jnp.concatenate(
        [part[:, :, 0], part[:, :, 1], jnp.zeros_like(part[:, :, 0]), part[:, :, 2]], axis=2
    )
    groups = max(1, width // GSIZE)
    each = [
        lax.dynamic_slice_in_dim(
            long_taps, (2 * (dp * chips + i) + core) * width // GSIZE, groups, 0
        )
        for i in range(chips)
    ]
    filters = jnp.stack(each).astype(jnp.float32)
    return taps, jnp.pad(filters, ((0, 0), (0, WIDE // GSIZE - groups), (0, 0)))


def shards(chips, tokens, in_weight, short_taps, long_taps, out_weight):
    _, width, features = in_weight.shape
    rows = tokens.shape[0]
    slots = lax.axis_size("dp")
    dp = lax.axis_index("dp")
    z = lax.axis_index("z")
    core = lax.axis_index("core")
    ring = ring_of(chips)
    forward = lambda block: lax.ppermute(block, "z", ring)

    table = jnp.array(origins_of(chips), jnp.int32)
    origins = lax.dynamic_index_in_dim(table, z, 1, False)
    place = jnp.concatenate([jnp.stack([core, dp]).astype(jnp.int32), origins])
    taps, filters = local_filters(chips, width, dp, core, short_taps, long_taps)

    pairs = lambda c: [(2 * i + 1, 2 * (i + 1) + c) for i in range(chips - 1)]
    half = HALO // 2
    edge = lax.ppermute(tokens[rows - HALO : rows - half], ("z", "core"), pairs(0)) + lax.ppermute(
        tokens[rows - half :], ("z", "core"), pairs(1)
    )
    block = jnp.concatenate([tokens, edge])

    if slots == 4 and chips == 4 and width == WIDE:
        flat = in_weight.reshape(3 * width, features)
        cut = 3 * width // 2
        wa, wb = [flat[:cut]], [flat[cut:]]
        x, y, twin = across(block, 1), across(block, 2), swap(block)
        wa.append(forward(wa[0]))
        wb.append(forward(wb[0]))
        wa.append(forward(wa[1]))
        x, y, twin, wa[1], wa[2], wb[1], v_own = tie(x, y, twin, wa[1], wa[2], wb[1], out_weight)

        v = lax.all_gather(v_own, ("dp", "z"))
        mid = HALO
        x_far, y_far = across(y[:mid], 1), across(x[mid:], 2)
        x_twin, y_twin = swap(x), swap(y)
        wb.append(forward(wb[1]))
        wa.append(forward(wa[2]))
        x_far, y_far, x_twin, y_twin, wb[2], wa[3] = tie(x_far, y_far, x_twin, y_twin, wb[2], wa[3])

        wb.append(forward(wb[2]))
        parts = [(0, 0, 0), (0, 1, 0), (1, 0, 0), (1, 1, 0), (2, 0, 0), (2, 1, 0)]
        parts += [(3, 0, 0), (3, 0, mid), (3, 1, 0), (3, 1, mid)]
        pieces = [block, twin, x, x_twin, y, y_twin, x_far, y_far, swap(x_far), swap(y_far)]
    else:
        v = lax.all_gather(out_weight, ("dp", "z"))
        w, wa, wb = in_weight, [], []
        for s in range(chips):
            padded = jnp.pad(w, ((0, 0), (0, WIDE - width), (0, 0))).reshape(3 * WIDE, features)
            wa.append(padded[: 3 * WIDE // 2])
            wb.append(padded[3 * WIDE // 2 :])
            if s + 1 < chips:
                w = forward(w)
        pieces = [block] + [across(block, r) for r in range(1, slots)]
        pieces += [swap(piece) for piece in pieces]
        parts = [(r, side, 0) for side in range(2) for r in range(slots)]

    moved = []
    for s in range(chips):
        last = s + 1 == chips
        if last and s > 1:
            wb[s], moved[: s - 1] = tie(wb[s], moved[: s - 1])
        mixed = mix_chunk(s, rows, slots, place, taps, filters, wa[s], wb[s], parts, pieces)
        mixed = [m[:width] for m in mixed]
        moved.append([mixed[0]] + [across(mixed[r], r) for r in range(1, slots)])
    if width == WIDE:
        v = v.reshape(slots * chips, width, -1)
        together = [part for one in moved for part in one]
    else:
        order = lax.bitwise_xor(dp, jnp.arange(slots))
        v = v.reshape(slots, chips, width, -1)[order][:, origins].reshape(slots * chips * width, -1)
        together = [jnp.concatenate([one[r] for r in range(slots) for one in moved])]
    run = lambda mirror, dtype: project(mirror, slots, chips, width, place, v, together, dtype)
    theirs = swap(run(True, jnp.bfloat16))
    mine = run(False, jnp.float32)
    return (mine + theirs.astype(jnp.float32)).astype(jnp.bfloat16)


def solution(mesh):
    count = mesh.shape["dp"]
    chips = mesh.shape["ctx"] // 2
    fine = Mesh(mesh.devices.reshape(count, chips, 2), ("dp", "z", "core"))
    every = ("dp", "z", "core")
    in_specs = (P(every, None), P(None, every, None), P(), P(), P(every, None))
    return jax.shard_map(
        functools.partial(shards, chips),
        mesh=fine,
        in_specs=in_specs,
        out_specs=P(every, None),
        check_vma=False,
    )
```

```python
import functools

import jax
import jax.numpy as jnp
from jax import lax
from jax.experimental import pallas as pl
from jax.experimental.pallas import tpu as pltpu
from jax.sharding import Mesh
from jax.sharding import PartitionSpec as P

GSIZE = 16
SHORT = 7
TAPS = 128
LANES = 128
WIDE = 64
HALO = 160
SMEM = pl.BlockSpec(memory_space=pltpu.SMEM)
VMEM = pl.BlockSpec(memory_space=pltpu.VMEM)
LIMIT = pltpu.CompilerParams(vmem_limit_bytes=32 * 1024 * 1024)


def ring_of(count):
    order = [i for i in range(count) if i == 0 or i % 2 == 1]
    order += [i for i in reversed(range(1, count)) if i % 2 == 0]
    return [(order[i], order[(i + 1) % count]) for i in range(count)]


def origins_of(count):
    previous = dict((target, source) for source, target in ring_of(count))
    table = [list(range(count))]
    for _ in range(count - 1):
        table.append([previous[i] for i in table[-1]])
    return table


def swap(block):
    return lax.ppermute(block, "core", [(0, 1), (1, 0)])


def across(block, r):
    count = lax.axis_size("dp")
    return lax.ppermute(block, "dp", [(i, i ^ r) for i in range(count)])


def tie(*groups):
    return lax.optimization_barrier(groups)


def dot(a, b):
    return jnp.dot(a, b, preferred_element_type=jnp.float32)


def nt(a, b):
    return lax.dot_general(a, b, (((1,), (1,)), ((), ())), preferred_element_type=jnp.float32)


def mix_kernel(steps, slots, parts, place_ref, taps_ref, long_ref, *rest):
    weights, rest = rest[: 2 * len(steps)], rest[2 * len(steps) :]
    pieces, rest = rest[: len(parts)], rest[len(parts) :]
    outs, rest = rest[: len(slots)], rest[len(slots) :]
    w, first, second, packed, turned, tiles = rest
    span = first.shape[1] - HALO
    rows = span // 2
    core = place_ref[0]
    count = WIDE // GSIZE
    band = 64
    blocks = span // TAPS
    lower = lax.broadcasted_iota(jnp.int32, (band, LANES), 1) < WIDE
    taps = [taps_ref[place_ref[2 + step]] for step in steps]

    for c, step in enumerate(steps):
        wa, wb = weights[2 * c], weights[2 * c + 1]
        cut = wa.shape[0]
        w[c, :cut] = wa[...]
        w[c, cut : 2 * WIDE] = wb[: 2 * WIDE - cut]
        w[c, 2 * WIDE : 3 * WIDE] = jnp.zeros((WIDE, w.shape[2]), w.dtype)
        w[c, 3 * WIDE :] = wb[2 * WIDE - cut :]
        filters = long_ref[place_ref[2 + step]]
        for g in range(count):
            line = jnp.concatenate(
                [jnp.zeros((1, TAPS), jnp.float32), filters[g : g + 1, :]], axis=1
            )
            square = pltpu.roll(
                jnp.broadcast_to(line, (2 * TAPS, 2 * TAPS)), 0, 1, stride=1, stride_axis=0
            )
            tiles[c * count + g] = square[:, :TAPS].astype(jnp.bfloat16)

    def put(half, value, at):
        here = pl.ds(pl.multiple_of(at, 16), value.shape[0])
        first[half, here] = value[:, :LANES]
        second[half, here] = value[:, LANES:]

    def project_unit(n, c, i):
        for ref, (slot, side, start) in zip(pieces, parts):
            if slot != slots[i]:
                continue
            owner = core if side == 0 else 1 - core
            value = nt(ref[...], w[c]).astype(jnp.bfloat16).astype(jnp.float32)
            end = start + ref.shape[0]
            if start < rows:
                put(n % 2, value[: min(end, rows) - start], HALO + owner * rows + start)
            if end > rows:
                low = max(start, rows)
                put(n % 2, value[low - start :], owner * (HALO // 2) + low - rows)

    def feat(ref, n, at, c, lanes):
        total = None
        for j in range(SHORT):
            term = taps[c][j : j + 1, lanes] * ref[n % 2, at - j : at - j + band, :]
            total = term if total is None else total + term
        return total

    units = [(c, i) for c in range(len(steps)) for i in range(len(slots))]
    project_unit(0, *units[0])
    for n, (c, i) in enumerate(units):
        if n + 1 < len(units):
            project_unit(n + 1, *units[n + 1])
        for m in range((TAPS + span) // band):
            at = HALO - TAPS + m * band
            x = feat(first, n, at, c, slice(0, LANES))
            y = feat(second, n, at, c, slice(LANES, 2 * LANES))
            packed[n % 2, m * band : (m + 1) * band, :] = jnp.where(lower, x, x * y).astype(
                jnp.bfloat16
            )
        turned[n] = packed[n % 2].T

    for c in range(len(steps)):
        mine = [n for n in range(len(units)) if units[n][0] == c]
        for g in range(count):
            channels = slice(WIDE + g * GSIZE, WIDE + (g + 1) * GSIZE)
            window = jnp.concatenate(
                [
                    turned[n, channels, b * TAPS : (b + 2) * TAPS]
                    for n in mine
                    for b in range(blocks)
                ],
                axis=0,
            )
            conv = dot(window, tiles[c * count + g])
            for k, n in enumerate(mine):
                row = jnp.concatenate(
                    [
                        conv[(k * blocks + b) * GSIZE : (k * blocks + b + 1) * GSIZE]
                        for b in range(blocks)
                    ],
                    axis=1,
                )
                query = turned[n, g * GSIZE : (g + 1) * GSIZE, TAPS:].astype(jnp.float32)
                at = c * WIDE + g * GSIZE
                outs[units[n][1]][at : at + GSIZE, :] = (query * row).astype(jnp.bfloat16)


def mix_chunks(steps, slots, rows, place, taps, filters, wa, wb, parts, pieces):
    features = wa[0].shape[1]
    chosen = [n for n, part in enumerate(parts) if part[0] in slots]
    parts, pieces = [parts[n] for n in chosen], [pieces[n] for n in chosen]
    weights = [half[s] for s in steps for half in (wa, wb)]
    units = len(steps) * len(slots)
    return pl.pallas_call(
        functools.partial(mix_kernel, steps, slots, parts),
        out_shape=[jax.ShapeDtypeStruct((len(steps) * WIDE, 2 * rows), jnp.bfloat16)] * len(slots),
        in_specs=[SMEM] + [VMEM] * (2 + len(weights) + len(pieces)),
        out_specs=[VMEM] * len(slots),
        scratch_shapes=[
            pltpu.VMEM((len(steps), 4 * WIDE, features), jnp.bfloat16),
            pltpu.VMEM((2, HALO + 2 * rows, LANES), jnp.float32),
            pltpu.VMEM((2, HALO + 2 * rows, LANES), jnp.float32),
            pltpu.VMEM((2, TAPS + 2 * rows, LANES), jnp.bfloat16),
            pltpu.VMEM((units, LANES, TAPS + 2 * rows), jnp.bfloat16),
            pltpu.VMEM((len(steps) * WIDE // GSIZE, 2 * TAPS, TAPS), jnp.bfloat16),
        ],
        compiler_params=LIMIT,
        cost_estimate=pl.CostEstimate(
            flops=4 * units * 2 * rows * 4 * WIDE * features,
            bytes_accessed=2 * units * 2 * rows * features,
            transcendentals=0,
        ),
    )(place, taps, filters, *weights, *pieces)


def out_kernel(mirror, order, chips, width, place_ref, v_ref, *refs):
    parts = refs[: len(refs) - 4]
    out_ref, left, right, total = refs[len(refs) - 4 :]
    rows = out_ref.shape[0]
    core, dp = place_ref[0], place_ref[1]
    if mirror:
        core = 1 - core
    depth = left.shape[0]
    if order is None:
        left[...] = parts[0][...]
        right[...] = v_ref[...]
        size = depth
    else:
        for n, (r, s, k, row) in enumerate(order):
            here = slice(n * width, (n + 1) * width)
            left[here] = parts[k][row : row + width]
            right[here] = v_ref[lax.bitwise_xor(dp, r) * chips + place_ref[2 + s]]
        size = depth // 2
    at = pl.multiple_of(core * rows, LANES)
    tile = 512
    for start in range(0, depth, size):
        a = left[start : start + size, pl.ds(at, rows)].T
        for t in range(0, out_ref.shape[1], tile):
            here = slice(t, t + tile)
            value = dot(a, right[start : start + size, here])
            if start:
                value = value + total[:, here]
            if start + size < depth:
                total[:, here] = value
            else:
                out_ref[:, here] = value.astype(out_ref.dtype)


def project(mirror, order, chips, width, depth, place, v, parts, dtype):
    span, features = parts[0].shape[1], v.shape[-1]
    rows = span // 2
    return pl.pallas_call(
        functools.partial(out_kernel, mirror, order, chips, width),
        out_shape=jax.ShapeDtypeStruct((rows, features), dtype),
        in_specs=[SMEM, VMEM] + [VMEM] * len(parts),
        out_specs=VMEM,
        scratch_shapes=[
            pltpu.VMEM((depth, span), jnp.bfloat16),
            pltpu.VMEM((depth, features), jnp.bfloat16),
            pltpu.VMEM((rows, features), jnp.float32),
        ],
        compiler_params=LIMIT,
        cost_estimate=pl.CostEstimate(
            flops=4 * rows * features * depth,
            bytes_accessed=2 * depth * (features + span),
            transcendentals=0,
        ),
    )(place, v, *parts)


def local_filters(chips, width, dp, core, short_taps, long_taps):
    part = short_taps.reshape(SHORT, 3, -1, 2, width)
    part = lax.dynamic_slice(
        part, (0, 0, dp * chips, core, 0), (SHORT, 3, chips, 1, width)
    ).reshape(SHORT, 3, chips, width)
    part = jnp.pad(part, ((0, 1), (0, 0), (0, 0), (0, WIDE - width)))
    part = jnp.transpose(part, (2, 0, 1, 3))
    taps = jnp.concatenate(
        [part[:, :, 0], part[:, :, 1], jnp.zeros_like(part[:, :, 0]), part[:, :, 2]], axis=2
    )
    groups = max(1, width // GSIZE)
    each = [
        lax.dynamic_slice_in_dim(
            long_taps, (2 * (dp * chips + i) + core) * width // GSIZE, groups, 0
        )
        for i in range(chips)
    ]
    filters = jnp.stack(each).astype(jnp.float32)
    return taps, jnp.pad(filters, ((0, 0), (0, WIDE // GSIZE - groups), (0, 0)))


def shards(chips, tokens, in_weight, short_taps, long_taps, out_weight):
    _, width, features = in_weight.shape
    rows = tokens.shape[0]
    slots = lax.axis_size("dp")
    dp = lax.axis_index("dp")
    z = lax.axis_index("z")
    core = lax.axis_index("core")
    ring = ring_of(chips)
    forward = lambda block: lax.ppermute(block, "z", ring)

    table = jnp.array(origins_of(chips), jnp.int32)
    origins = lax.dynamic_index_in_dim(table, z, 1, False)
    place = jnp.concatenate([jnp.stack([core, dp]).astype(jnp.int32), origins])
    taps, filters = local_filters(chips, width, dp, core, short_taps, long_taps)

    pairs = lambda c: [(2 * i + 1, 2 * (i + 1) + c) for i in range(chips - 1)]
    half = HALO // 2
    edge = lax.ppermute(tokens[rows - HALO : rows - half], ("z", "core"), pairs(0)) + lax.ppermute(
        tokens[rows - half :], ("z", "core"), pairs(1)
    )
    v = lax.all_gather(out_weight, ("dp", "z"))
    run_mix = lambda steps, which: mix_chunks(
        steps, which, rows, place, taps, filters, wa, wb, parts, pieces
    )

    if slots == 4 and chips == 4 and width == WIDE:
        flat = in_weight.reshape(3 * width, features)
        cut = 3 * width // 2
        wa, wb = [flat[:cut]], [flat[cut:]]
        wa.append(forward(wa[0]))
        edge, wa[1] = tie(edge, wa[1])

        block = jnp.concatenate([tokens, edge])
        x, y, twin = across(block, 1), across(block, 2), swap(block)
        wb.append(forward(wb[0]))
        wa.append(forward(wa[1]))
        wb.append(forward(wb[1]))
        x, y, twin, wa, wb, taps, filters, place = tie(x, y, twin, wa, wb, taps, filters, place)
        wa, wb = list(wa), list(wb)

        mid = HALO
        x_twin, y_twin = swap(x), swap(y)
        wa.append(forward(wa[2]))
        wb.append(forward(wb[2]))
        x_far, y_far = across(y[:mid], 1), across(x[mid:], 2)
        parts = [(0, 0, 0), (0, 1, 0), (1, 0, 0), (1, 1, 0), (2, 0, 0), (2, 1, 0)]
        pieces = [block, twin, x, x_twin, y, y_twin]
        early = run_mix((0, 1, 2), (0, 1, 2))
        early, x_far, y_far, wa, wb = tie(early, x_far, y_far, wa, wb)

        parts += [(3, 0, 0), (3, 0, mid), (3, 1, 0), (3, 1, mid)]
        pieces += [x_far, y_far, swap(x_far), swap(y_far)]
        late = run_mix((3,), (0, 1, 2))
        (far,) = run_mix((0, 1, 2, 3), (3,))
        together = [early[0], late[0]]
        for r in (1, 2):
            together += [across(early[r], r), across(late[r], r)]
        together.append(across(far, 3))
        v = v.reshape(slots * chips, width, -1)
        order = [(r, s, 2 * r, s * width) for s in range(3) for r in range(3)]
        order += [(r, 3, 2 * r + 1, 0) for r in range(3)]
        order += [(3, s, 6, s * width) for s in range(chips)]
    else:
        block = jnp.concatenate([tokens, edge])
        w, wa, wb = in_weight, [], []
        for s in range(chips):
            padded = jnp.pad(w, ((0, 0), (0, WIDE - width), (0, 0))).reshape(3 * WIDE, features)
            wa.append(padded[: 3 * WIDE // 2])
            wb.append(padded[3 * WIDE // 2 :])
            if s + 1 < chips:
                w = forward(w)
        pieces = [block] + [across(block, r) for r in range(1, slots)]
        pieces += [swap(piece) for piece in pieces]
        parts = [(r, side, 0) for side in range(2) for r in range(slots)]
        moved = []
        for s in range(chips):
            mixed = []
            for r in range(0, slots, 4):
                mixed += run_mix((s,), tuple(range(r, min(r + 4, slots))))
            mixed = [m[:width] for m in mixed]
            moved.append([mixed[0]] + [across(mixed[r], r) for r in range(1, slots)])
        turn = lax.bitwise_xor(dp, jnp.arange(slots))
        v = v.reshape(slots, chips, width, -1)[turn][:, origins].reshape(slots * chips * width, -1)
        together = [jnp.concatenate([one[r] for r in range(slots) for one in moved])]
        order = None
    depth = slots * chips * width
    run = lambda mirror, dtype: project(
        mirror, order, chips, width, depth, place, v, together, dtype
    )
    theirs = swap(run(True, jnp.bfloat16))
    mine = run(False, jnp.float32)
    return (mine + theirs.astype(jnp.float32)).astype(jnp.bfloat16)


def solution(mesh):
    count = mesh.shape["dp"]
    chips = mesh.shape["ctx"] // 2
    fine = Mesh(mesh.devices.reshape(count, chips, 2), ("dp", "z", "core"))
    every = ("dp", "z", "core")
    in_specs = (P(every, None), P(None, every, None), P(), P(), P(every, None))
    return jax.shard_map(
        functools.partial(shards, chips),
        mesh=fine,
        in_specs=in_specs,
        out_specs=P(every, None),
        check_vma=False,
    )
```

```python
import functools

import jax
import jax.numpy as jnp
from jax import lax
from jax.experimental import pallas as pl
from jax.experimental.pallas import tpu as pltpu
from jax.sharding import Mesh
from jax.sharding import PartitionSpec as P

GSIZE = 16
SHORT = 7
TAPS = 128
LANES = 128
WIDE = 64
HALO = 160
SMEM = pl.BlockSpec(memory_space=pltpu.SMEM)
VMEM = pl.BlockSpec(memory_space=pltpu.VMEM)
LIMIT = pltpu.CompilerParams(vmem_limit_bytes=24 * 1024 * 1024)


def ring_of(count):
    order = [i for i in range(count) if i == 0 or i % 2 == 1]
    order += [i for i in reversed(range(1, count)) if i % 2 == 0]
    return [(order[i], order[(i + 1) % count]) for i in range(count)]


def origins_of(count):
    previous = dict((target, source) for source, target in ring_of(count))
    table = [list(range(count))]
    for _ in range(count - 1):
        table.append([previous[i] for i in table[-1]])
    return table


def swap(block):
    return lax.ppermute(block, "core", [(0, 1), (1, 0)])


def across(block, r):
    count = lax.axis_size("dp")
    return lax.ppermute(block, "dp", [(i, i ^ r) for i in range(count)])


def tie(*groups):
    return lax.optimization_barrier(groups)


def dot(a, b):
    return jnp.dot(a, b, preferred_element_type=jnp.float32)


def nt(a, b):
    return lax.dot_general(a, b, (((1,), (1,)), ((), ())), preferred_element_type=jnp.float32)


def mix_kernel(steps, slots, parts, place_ref, taps_ref, long_ref, *rest):
    weights, rest = rest[: 2 * len(steps)], rest[2 * len(steps) :]
    pieces, rest = rest[: len(parts)], rest[len(parts) :]
    outs, rest = rest[: len(slots)], rest[len(slots) :]
    w, first, second, packed, turned, tiles = rest
    span = first.shape[1] - HALO
    rows = span // 2
    core = place_ref[0]
    count = WIDE // GSIZE
    band = 64
    blocks = span // TAPS
    lower = lax.broadcasted_iota(jnp.int32, (band, LANES), 1) < WIDE
    taps = [taps_ref[place_ref[2 + step]] for step in steps]

    for c, step in enumerate(steps):
        wa, wb = weights[2 * c], weights[2 * c + 1]
        cut = wa.shape[0]
        w[c, :cut] = wa[...]
        w[c, cut : 2 * WIDE] = wb[: 2 * WIDE - cut]
        w[c, 2 * WIDE : 3 * WIDE] = jnp.zeros((WIDE, w.shape[2]), w.dtype)
        w[c, 3 * WIDE :] = wb[2 * WIDE - cut :]
        filters = long_ref[place_ref[2 + step]]
        for g in range(count):
            line = jnp.concatenate(
                [jnp.zeros((1, TAPS), jnp.float32), filters[g : g + 1, :]], axis=1
            )
            square = pltpu.roll(
                jnp.broadcast_to(line, (2 * TAPS, 2 * TAPS)), 0, 1, stride=1, stride_axis=0
            )
            tiles[c * count + g] = square[:, :TAPS].astype(jnp.bfloat16)

    def put(half, value, at):
        here = pl.ds(pl.multiple_of(at, 16), value.shape[0])
        first[half, here] = value[:, :LANES]
        second[half, here] = value[:, LANES:]

    def project_unit(n, c, i):
        for ref, (slot, side, start) in zip(pieces, parts):
            if slot != slots[i]:
                continue
            owner = core if side == 0 else 1 - core
            value = nt(ref[...], w[c]).astype(jnp.bfloat16).astype(jnp.float32)
            end = start + ref.shape[0]
            if start < rows:
                put(n % 2, value[: min(end, rows) - start], HALO + owner * rows + start)
            if end > rows:
                low = max(start, rows)
                put(n % 2, value[low - start :], owner * (HALO // 2) + low - rows)

    def feat(ref, n, at, c, lanes):
        total = None
        for j in range(SHORT):
            term = taps[c][j : j + 1, lanes] * ref[n % 2, at - j : at - j + band, :]
            total = term if total is None else total + term
        return total

    units = [(c, i) for c in range(len(steps)) for i in range(len(slots))]
    project_unit(0, *units[0])
    for n, (c, i) in enumerate(units):
        if n + 1 < len(units):
            project_unit(n + 1, *units[n + 1])
        for m in range((TAPS + span) // band):
            at = HALO - TAPS + m * band
            x = feat(first, n, at, c, slice(0, LANES))
            y = feat(second, n, at, c, slice(LANES, 2 * LANES))
            packed[n % 2, m * band : (m + 1) * band, :] = jnp.where(lower, x, x * y).astype(
                jnp.bfloat16
            )
        turned[n] = packed[n % 2].T

    for c in range(len(steps)):
        mine = [n for n in range(len(units)) if units[n][0] == c]
        for g in range(count):
            channels = slice(WIDE + g * GSIZE, WIDE + (g + 1) * GSIZE)
            window = jnp.concatenate(
                [
                    turned[n, channels, b * TAPS : (b + 2) * TAPS]
                    for n in mine
                    for b in range(blocks)
                ],
                axis=0,
            )
            conv = dot(window, tiles[c * count + g])
            for k, n in enumerate(mine):
                row = jnp.concatenate(
                    [
                        conv[(k * blocks + b) * GSIZE : (k * blocks + b + 1) * GSIZE]
                        for b in range(blocks)
                    ],
                    axis=1,
                )
                query = turned[n, g * GSIZE : (g + 1) * GSIZE, TAPS:].astype(jnp.float32)
                at = c * WIDE + g * GSIZE
                outs[units[n][1]][at : at + GSIZE, :] = (query * row).astype(jnp.bfloat16)


def mix_chunks(steps, slots, rows, place, taps, filters, wa, wb, parts, pieces):
    features = wa[0].shape[1]
    chosen = [n for n, part in enumerate(parts) if part[0] in slots]
    parts, pieces = [parts[n] for n in chosen], [pieces[n] for n in chosen]
    weights = [half[s] for s in steps for half in (wa, wb)]
    units = len(steps) * len(slots)
    return pl.pallas_call(
        functools.partial(mix_kernel, steps, slots, parts),
        out_shape=[jax.ShapeDtypeStruct((len(steps) * WIDE, 2 * rows), jnp.bfloat16)] * len(slots),
        in_specs=[SMEM] + [VMEM] * (2 + len(weights) + len(pieces)),
        out_specs=[VMEM] * len(slots),
        scratch_shapes=[
            pltpu.VMEM((len(steps), 4 * WIDE, features), jnp.bfloat16),
            pltpu.VMEM((2, HALO + 2 * rows, LANES), jnp.float32),
            pltpu.VMEM((2, HALO + 2 * rows, LANES), jnp.float32),
            pltpu.VMEM((2, TAPS + 2 * rows, LANES), jnp.bfloat16),
            pltpu.VMEM((units, LANES, TAPS + 2 * rows), jnp.bfloat16),
            pltpu.VMEM((len(steps) * WIDE // GSIZE, 2 * TAPS, TAPS), jnp.bfloat16),
        ],
        compiler_params=LIMIT,
        cost_estimate=pl.CostEstimate(
            flops=4 * units * 2 * rows * 4 * WIDE * features,
            bytes_accessed=2 * units * 2 * rows * features,
            transcendentals=0,
        ),
    )(place, taps, filters, *weights, *pieces)


def out_kernel(mirror, order, chips, width, place_ref, v_ref, *refs):
    parts = refs[: len(refs) - 4]
    out_ref, left, right, total = refs[len(refs) - 4 :]
    rows = out_ref.shape[0]
    core, dp = place_ref[0], place_ref[1]
    if mirror:
        core = 1 - core
    depth = left.shape[0]
    if order is None:
        left[...] = parts[0][...]
        right[...] = v_ref[...]
        size = depth
    else:
        for n, (r, s, k, row) in enumerate(order):
            here = slice(n * width, (n + 1) * width)
            left[here] = parts[k][row : row + width]
            right[here] = v_ref[lax.bitwise_xor(dp, r) * chips + place_ref[2 + s]]
        size = depth // 2
    at = pl.multiple_of(core * rows, LANES)
    tile = 512
    for start in range(0, depth, size):
        a = left[start : start + size, pl.ds(at, rows)].T
        for t in range(0, out_ref.shape[1], tile):
            here = slice(t, t + tile)
            value = dot(a, right[start : start + size, here])
            if start:
                value = value + total[:, here]
            if start + size < depth:
                total[:, here] = value
            else:
                out_ref[:, here] = value.astype(out_ref.dtype)


def project(mirror, order, chips, width, depth, place, v, parts, dtype):
    span, features = parts[0].shape[1], v.shape[-1]
    rows = span // 2
    return pl.pallas_call(
        functools.partial(out_kernel, mirror, order, chips, width),
        out_shape=jax.ShapeDtypeStruct((rows, features), dtype),
        in_specs=[SMEM, VMEM] + [VMEM] * len(parts),
        out_specs=VMEM,
        scratch_shapes=[
            pltpu.VMEM((depth, span), jnp.bfloat16),
            pltpu.VMEM((depth, features), jnp.bfloat16),
            pltpu.VMEM((rows, features), jnp.float32),
        ],
        compiler_params=LIMIT,
        cost_estimate=pl.CostEstimate(
            flops=4 * rows * features * depth,
            bytes_accessed=2 * depth * (features + span),
            transcendentals=0,
        ),
    )(place, v, *parts)


def local_filters(chips, width, dp, core, short_taps, long_taps):
    part = short_taps.reshape(SHORT, 3, -1, 2, width)
    part = lax.dynamic_slice(
        part, (0, 0, dp * chips, core, 0), (SHORT, 3, chips, 1, width)
    ).reshape(SHORT, 3, chips, width)
    part = jnp.pad(part, ((0, 1), (0, 0), (0, 0), (0, WIDE - width)))
    part = jnp.transpose(part, (2, 0, 1, 3))
    taps = jnp.concatenate(
        [part[:, :, 0], part[:, :, 1], jnp.zeros_like(part[:, :, 0]), part[:, :, 2]], axis=2
    )
    groups = max(1, width // GSIZE)
    each = [
        lax.dynamic_slice_in_dim(
            long_taps, (2 * (dp * chips + i) + core) * width // GSIZE, groups, 0
        )
        for i in range(chips)
    ]
    filters = jnp.stack(each).astype(jnp.float32)
    return taps, jnp.pad(filters, ((0, 0), (0, WIDE // GSIZE - groups), (0, 0)))


def shards(chips, tokens, in_weight, short_taps, long_taps, out_weight):
    _, width, features = in_weight.shape
    rows = tokens.shape[0]
    slots = lax.axis_size("dp")
    dp = lax.axis_index("dp")
    z = lax.axis_index("z")
    core = lax.axis_index("core")
    ring = ring_of(chips)
    forward = lambda block: lax.ppermute(block, "z", ring)

    table = jnp.array(origins_of(chips), jnp.int32)
    origins = lax.dynamic_index_in_dim(table, z, 1, False)
    place = jnp.concatenate([jnp.stack([core, dp]).astype(jnp.int32), origins])
    taps, filters = local_filters(chips, width, dp, core, short_taps, long_taps)

    pairs = lambda c: [(2 * i + 1, 2 * (i + 1) + c) for i in range(chips - 1)]
    half = HALO // 2
    edge = lax.ppermute(tokens[rows - HALO : rows - half], ("z", "core"), pairs(0)) + lax.ppermute(
        tokens[rows - half :], ("z", "core"), pairs(1)
    )
    run_mix = lambda steps, which: mix_chunks(
        steps, which, rows, place, taps, filters, wa, wb, parts, pieces
    )

    if slots == 4 and chips == 4 and width == WIDE:
        flat = in_weight.reshape(3 * width, features)
        cut = 3 * width // 2
        mid = HALO
        wa, wb = [flat[:cut]], [flat[cut:]]
        v = lax.all_gather(out_weight, "z")

        low = tokens[:mid]
        low_x, low_y, low_twin = across(low, 1), across(low, 2), swap(low)
        wa.append(forward(wa[0]))
        edge, wa[1], low_x, low_y, low_twin = tie(edge, wa[1], low_x, low_y, low_twin)

        high = jnp.concatenate([tokens[mid:], edge])
        high_x, high_y, high_twin = across(high, 1), across(high, 2), swap(high)
        low_x_twin, low_y_twin = swap(low_x), swap(low_y)
        wb.append(forward(wb[0]))
        wa.append(forward(wa[1]))
        (high_x, high_y, high_twin, low_x_twin, low_y_twin, wa, wb, taps, filters, place, v) = tie(
            high_x, high_y, high_twin, low_x_twin, low_y_twin, wa, wb, taps, filters, place, v
        )
        wa, wb = list(wa), list(wb)

        v = lax.all_gather(v, "dp")
        wb.append(forward(wb[1]))
        wa.append(forward(wa[2]))
        far_x, far_y = across(low_y, 1), across(high_x, 2)
        parts = [(r, side, at) for r in range(3) for side in range(2) for at in (0, mid)]
        pieces = [low, high, low_twin, high_twin]
        pieces += [low_x, high_x, low_x_twin, swap(high_x)]
        pieces += [low_y, high_y, low_y_twin, swap(high_y)]
        early = run_mix((0, 1), (0, 1, 2))
        early, far_x, far_y, wa, wb = tie(early, far_x, far_y, wa, wb)
        wa, wb = list(wa), list(wb)

        wb.append(forward(wb[2]))
        parts += [(3, 0, 0), (3, 0, mid), (3, 1, 0), (3, 1, mid)]
        pieces += [far_x, far_y, swap(far_x), swap(far_y)]
        (far,) = run_mix((0, 1, 2), (3,))
        late = run_mix((2, 3), (0, 1, 2))
        (last,) = run_mix((3,), (3,))
        together = [early[0], late[0]]
        for r in (1, 2):
            together += [across(early[r], r), across(late[r], r)]
        together += [across(far, 3), across(last, 3)]
        v = v.reshape(slots * chips, width, -1)
        order = [(r, s, 2 * r + s // 2, s % 2 * width) for s in range(chips) for r in range(3)]
        order += [(3, s, 6 + s // 3, s % 3 * width) for s in range(chips)]
    else:
        v = lax.all_gather(out_weight, ("dp", "z"))
        block = jnp.concatenate([tokens, edge])
        w, wa, wb = in_weight, [], []
        for s in range(chips):
            padded = jnp.pad(w, ((0, 0), (0, WIDE - width), (0, 0))).reshape(3 * WIDE, features)
            wa.append(padded[: 3 * WIDE // 2])
            wb.append(padded[3 * WIDE // 2 :])
            if s + 1 < chips:
                w = forward(w)
        pieces = [block] + [across(block, r) for r in range(1, slots)]
        pieces += [swap(piece) for piece in pieces]
        parts = [(r, side, 0) for side in range(2) for r in range(slots)]
        moved = []
        for s in range(chips):
            mixed = []
            for r in range(0, slots, 4):
                mixed += run_mix((s,), tuple(range(r, min(r + 4, slots))))
            mixed = [m[:width] for m in mixed]
            moved.append([mixed[0]] + [across(mixed[r], r) for r in range(1, slots)])
        turn = lax.bitwise_xor(dp, jnp.arange(slots))
        v = v.reshape(slots, chips, width, -1)[turn][:, origins].reshape(slots * chips * width, -1)
        together = [jnp.concatenate([one[r] for r in range(slots) for one in moved])]
        order = None
    depth = slots * chips * width
    run = lambda mirror, dtype: project(
        mirror, order, chips, width, depth, place, v, together, dtype
    )
    theirs = swap(run(True, jnp.bfloat16))
    mine = run(False, jnp.float32)
    return (mine + theirs.astype(jnp.float32)).astype(jnp.bfloat16)


def solution(mesh):
    count = mesh.shape["dp"]
    chips = mesh.shape["ctx"] // 2
    fine = Mesh(mesh.devices.reshape(count, chips, 2), ("dp", "z", "core"))
    every = ("dp", "z", "core")
    in_specs = (P(every, None), P(None, every, None), P(), P(), P(every, None))
    return jax.shard_map(
        functools.partial(shards, chips),
        mesh=fine,
        in_specs=in_specs,
        out_specs=P(every, None),
        check_vma=False,
    )
```

```python
import functools

import jax
import jax.numpy as jnp
from jax import lax
from jax.experimental import pallas as pl
from jax.experimental.pallas import tpu as pltpu
from jax.sharding import Mesh
from jax.sharding import PartitionSpec as P

GSIZE = 16
SHORT = 7
TAPS = 128
LANES = 128
WIDE = 64
HALO = 160
SMEM = pl.BlockSpec(memory_space=pltpu.SMEM)
VMEM = pl.BlockSpec(memory_space=pltpu.VMEM)
LIMIT = pltpu.CompilerParams(vmem_limit_bytes=24 * 1024 * 1024)


def ring_of(count):
    order = [i for i in range(count) if i == 0 or i % 2 == 1]
    order += [i for i in reversed(range(1, count)) if i % 2 == 0]
    return [(order[i], order[(i + 1) % count]) for i in range(count)]


def origins_of(count):
    previous = dict((target, source) for source, target in ring_of(count))
    table = [list(range(count))]
    for _ in range(count - 1):
        table.append([previous[i] for i in table[-1]])
    return table


def swap(block):
    return lax.ppermute(block, "core", [(0, 1), (1, 0)])


def across(block, r):
    count = lax.axis_size("dp")
    return lax.ppermute(block, "dp", [(i, i ^ r) for i in range(count)])


def tie(*groups):
    return lax.optimization_barrier(groups)


def dot(a, b):
    return jnp.dot(a, b, preferred_element_type=jnp.float32)


def nt(a, b):
    return lax.dot_general(a, b, (((1,), (1,)), ((), ())), preferred_element_type=jnp.float32)


def mix_kernel(steps, slots, parts, place_ref, taps_ref, long_ref, *rest):
    weights, rest = rest[: len(steps)], rest[len(steps) :]
    pieces, rest = rest[: len(parts)], rest[len(parts) :]
    outs, rest = rest[: len(slots)], rest[len(slots) :]
    w, first, second, packed, turned, tiles = rest
    span = first.shape[1] - HALO
    rows = span // 2
    core = place_ref[0]
    count = WIDE // GSIZE
    band = 64
    blocks = span // TAPS
    lower = lax.broadcasted_iota(jnp.int32, (band, LANES), 1) < WIDE
    taps = [taps_ref[place_ref[2 + step]] for step in steps]

    for c, step in enumerate(steps):
        w[c, : 2 * WIDE] = weights[c][: 2 * WIDE]
        w[c, 2 * WIDE : 3 * WIDE] = jnp.zeros((WIDE, w.shape[2]), w.dtype)
        w[c, 3 * WIDE :] = weights[c][2 * WIDE :]
        filters = long_ref[place_ref[2 + step]]
        for g in range(count):
            line = jnp.concatenate(
                [jnp.zeros((1, TAPS), jnp.float32), filters[g : g + 1, :]], axis=1
            )
            square = pltpu.roll(
                jnp.broadcast_to(line, (2 * TAPS, 2 * TAPS)), 0, 1, stride=1, stride_axis=0
            )
            tiles[c * count + g] = square[:, :TAPS].astype(jnp.bfloat16)

    def put(half, value, at):
        here = pl.ds(pl.multiple_of(at, 16), value.shape[0])
        first[half, here] = value[:, :LANES]
        second[half, here] = value[:, LANES:]

    def project_unit(n, c, i):
        for ref, (slot, side, start) in zip(pieces, parts):
            if slot != slots[i]:
                continue
            owner = core if side == 0 else 1 - core
            value = nt(ref[...], w[c]).astype(jnp.bfloat16).astype(jnp.float32)
            end = start + ref.shape[0]
            if start < rows:
                put(n % 2, value[: min(end, rows) - start], HALO + owner * rows + start)
            if end > rows:
                low = max(start, rows)
                put(n % 2, value[low - start :], owner * (HALO // 2) + low - rows)

    def feat(ref, n, at, c, lanes):
        total = None
        for j in range(SHORT):
            term = taps[c][j : j + 1, lanes] * ref[n % 2, at - j : at - j + band, :]
            total = term if total is None else total + term
        return total

    units = [(c, i) for c in range(len(steps)) for i in range(len(slots))]
    project_unit(0, *units[0])
    for n, (c, i) in enumerate(units):
        if n + 1 < len(units):
            project_unit(n + 1, *units[n + 1])
        for m in range((TAPS + span) // band):
            at = HALO - TAPS + m * band
            x = feat(first, n, at, c, slice(0, LANES))
            y = feat(second, n, at, c, slice(LANES, 2 * LANES))
            packed[n % 2, m * band : (m + 1) * band, :] = jnp.where(lower, x, x * y).astype(
                jnp.bfloat16
            )
        turned[n] = packed[n % 2].T

    for c in range(len(steps)):
        mine = [n for n in range(len(units)) if units[n][0] == c]
        for g in range(count):
            channels = slice(WIDE + g * GSIZE, WIDE + (g + 1) * GSIZE)
            window = jnp.concatenate(
                [
                    turned[n, channels, b * TAPS : (b + 2) * TAPS]
                    for n in mine
                    for b in range(blocks)
                ],
                axis=0,
            )
            conv = dot(window, tiles[c * count + g])
            for k, n in enumerate(mine):
                row = jnp.concatenate(
                    [
                        conv[(k * blocks + b) * GSIZE : (k * blocks + b + 1) * GSIZE]
                        for b in range(blocks)
                    ],
                    axis=1,
                )
                query = turned[n, g * GSIZE : (g + 1) * GSIZE, TAPS:].astype(jnp.float32)
                at = c * WIDE + g * GSIZE
                outs[units[n][1]][at : at + GSIZE, :] = (query * row).astype(jnp.bfloat16)


def mix_chunks(steps, slots, rows, place, taps, filters, ws, parts, pieces):
    features = ws[0].shape[1]
    chosen = [n for n, part in enumerate(parts) if part[0] in slots]
    parts, pieces = [parts[n] for n in chosen], [pieces[n] for n in chosen]
    weights = [ws[s] for s in steps]
    units = len(steps) * len(slots)
    return pl.pallas_call(
        functools.partial(mix_kernel, steps, slots, parts),
        out_shape=[jax.ShapeDtypeStruct((len(steps) * WIDE, 2 * rows), jnp.bfloat16)] * len(slots),
        in_specs=[SMEM] + [VMEM] * (2 + len(weights) + len(pieces)),
        out_specs=[VMEM] * len(slots),
        scratch_shapes=[
            pltpu.VMEM((len(steps), 4 * WIDE, features), jnp.bfloat16),
            pltpu.VMEM((2, HALO + 2 * rows, LANES), jnp.float32),
            pltpu.VMEM((2, HALO + 2 * rows, LANES), jnp.float32),
            pltpu.VMEM((2, TAPS + 2 * rows, LANES), jnp.bfloat16),
            pltpu.VMEM((units, LANES, TAPS + 2 * rows), jnp.bfloat16),
            pltpu.VMEM((len(steps) * WIDE // GSIZE, 2 * TAPS, TAPS), jnp.bfloat16),
        ],
        compiler_params=LIMIT,
        cost_estimate=pl.CostEstimate(
            flops=4 * units * 2 * rows * 4 * WIDE * features,
            bytes_accessed=2 * units * 2 * rows * features,
            transcendentals=0,
        ),
    )(place, taps, filters, *weights, *pieces)


def out_kernel(mirror, order, chips, width, counts, place_ref, *refs):
    weights, refs = refs[: counts[0]], refs[counts[0] :]
    parts, refs = refs[: counts[1]], refs[counts[1] :]
    out_ref, left, right, total = refs
    rows = out_ref.shape[0]
    core = place_ref[0]
    if mirror:
        core = 1 - core
    depth = left.shape[0]
    if order is None:
        left[...] = parts[0][...]
    else:
        for n, (k, row) in enumerate(order):
            at = pl.multiple_of((n // chips * chips + place_ref[2 + n % chips]) * width, width)
            left[pl.ds(at, width)] = parts[k][row : row + width]
    at = 0
    for ref in weights:
        right[at : at + ref.shape[0]] = ref[...]
        at += ref.shape[0]
    size = depth // 2
    at = pl.multiple_of(core * rows, LANES)
    tile = 512
    for start in range(0, depth, size):
        a = left[start : start + size, pl.ds(at, rows)].T
        for t in range(0, out_ref.shape[1], tile):
            here = slice(t, t + tile)
            value = dot(a, right[start : start + size, here])
            if start:
                value = value + total[:, here]
            if start + size < depth:
                total[:, here] = value
            else:
                out_ref[:, here] = value.astype(out_ref.dtype)


def project(mirror, order, chips, width, depth, place, v, parts, dtype):
    span, features = parts[0].shape[1], v[0].shape[-1]
    rows = span // 2
    counts = (len(v), len(parts))
    return pl.pallas_call(
        functools.partial(out_kernel, mirror, order, chips, width, counts),
        out_shape=jax.ShapeDtypeStruct((rows, features), dtype),
        in_specs=[SMEM] + [VMEM] * sum(counts),
        out_specs=VMEM,
        scratch_shapes=[
            pltpu.VMEM((depth, span), jnp.bfloat16),
            pltpu.VMEM((depth, features), jnp.bfloat16),
            pltpu.VMEM((rows, features), jnp.float32),
        ],
        compiler_params=LIMIT,
        cost_estimate=pl.CostEstimate(
            flops=4 * rows * features * depth,
            bytes_accessed=2 * depth * (features + span),
            transcendentals=0,
        ),
    )(place, *v, *parts)


def local_filters(chips, width, dp, core, short_taps, long_taps):
    part = short_taps.reshape(SHORT, 3, -1, 2, width)
    part = lax.dynamic_slice(
        part, (0, 0, dp * chips, core, 0), (SHORT, 3, chips, 1, width)
    ).reshape(SHORT, 3, chips, width)
    part = jnp.pad(part, ((0, 1), (0, 0), (0, 0), (0, WIDE - width)))
    part = jnp.transpose(part, (2, 0, 1, 3))
    taps = jnp.concatenate(
        [part[:, :, 0], part[:, :, 1], jnp.zeros_like(part[:, :, 0]), part[:, :, 2]], axis=2
    )
    groups = max(1, width // GSIZE)
    each = [
        lax.dynamic_slice_in_dim(
            long_taps, (2 * (dp * chips + i) + core) * width // GSIZE, groups, 0
        )
        for i in range(chips)
    ]
    filters = jnp.stack(each).astype(jnp.float32)
    return taps, jnp.pad(filters, ((0, 0), (0, WIDE // GSIZE - groups), (0, 0)))


def shards(chips, tokens, in_weight, short_taps, long_taps, out_weight):
    _, width, features = in_weight.shape
    rows = tokens.shape[0]
    slots = lax.axis_size("dp")
    dp = lax.axis_index("dp")
    z = lax.axis_index("z")
    core = lax.axis_index("core")
    ring = ring_of(chips)
    forward = lambda block: lax.ppermute(block, "z", ring)

    table = jnp.array(origins_of(chips), jnp.int32)
    origins = lax.dynamic_index_in_dim(table, z, 1, False)
    place = jnp.concatenate([jnp.stack([core, dp]).astype(jnp.int32), origins])
    taps, filters = local_filters(chips, width, dp, core, short_taps, long_taps)

    pairs = lambda c: [(2 * i + 1, 2 * (i + 1) + c) for i in range(chips - 1)]
    half = HALO // 2
    edge = lax.ppermute(tokens[rows - HALO : rows - half], ("z", "core"), pairs(0)) + lax.ppermute(
        tokens[rows - half :], ("z", "core"), pairs(1)
    )
    run_mix = lambda steps, which: mix_chunks(
        steps, which, rows, place, taps, filters, ws, parts, pieces
    )

    if slots == 4 and chips == 4 and width == WIDE:
        mid = HALO
        ws = [in_weight.reshape(3 * width, features)]
        low = tokens[:mid]
        low_x, low_y = across(low, 1), across(low, 2)
        edge, low, low_x, low_y, v, ws[0] = tie(edge, low, low_x, low_y, out_weight, ws[0])

        v = lax.all_gather(v, "z")
        high = jnp.concatenate([tokens[mid:], edge])
        high_x, high_y, high_twin = across(high, 1), across(high, 2), swap(high)
        low_twin, low_x_twin, low_y_twin = swap(low), swap(low_x), swap(low_y)
        ws.append(forward(ws[0]))
        (high_x, high_y, high_twin, low_twin, low_x_twin, low_y_twin, ws, taps, filters, place, v) = tie(
            high_x, high_y, high_twin, low_twin, low_x_twin, low_y_twin, ws, taps, filters, place, v
        )

        ws = list(ws) + [forward(ws[1])]
        far_x, far_y = across(low_y, 1), across(high_x, 2)
        parts = [(r, side, at) for r in range(3) for side in range(2) for at in (0, mid)]
        pieces = [low, high, low_twin, high_twin]
        pieces += [low_x, high_x, low_x_twin, swap(high_x)]
        pieces += [low_y, high_y, low_y_twin, swap(high_y)]
        early = run_mix((0, 1), (0, 1, 2))
        v = v.reshape(chips * width, -1)
        v_x, v_y = across(v, 1), across(v, 2)
        early, far_x, far_y, ws = tie(early, far_x, far_y, ws)

        ws = list(ws) + [forward(ws[2])]
        parts += [(3, 0, 0), (3, 0, mid), (3, 1, 0), (3, 1, mid)]
        pieces += [far_x, far_y, swap(far_x), swap(far_y)]
        (far,) = run_mix((0, 1, 2), (3,))
        late = run_mix((2,), (0, 1, 2))
        late, far, v_x, v_y = tie(late, far, v_x, v_y)
        cut = v.shape[0] // 2
        v = [v, v_x, v_y, across(v_y[:cut], 1), across(v_x[cut:], 2)]
        last = run_mix((3,), (0, 1, 2, 3))
        together = [early[0], late[0], last[0]]
        for r in (1, 2):
            together += [across(early[r], r), across(late[r], r), across(last[r], r)]
        together += [across(far, 3), across(last[3], 3)]
        order = [
            (3 * r + max(0, s - 1), s * width if s < 2 else 0)
            for r in range(3)
            for s in range(chips)
        ]
        order += [(9 + s // 3, s % 3 * width) for s in range(chips)]
    else:
        v = lax.all_gather(out_weight, ("dp", "z"))
        block = jnp.concatenate([tokens, edge])
        w, ws = in_weight, []
        for s in range(chips):
            padded = jnp.pad(w, ((0, 0), (0, WIDE - width), (0, 0)))
            ws.append(padded.reshape(3 * WIDE, features))
            if s + 1 < chips:
                w = forward(w)
        pieces = [block] + [across(block, r) for r in range(1, slots)]
        pieces += [swap(piece) for piece in pieces]
        parts = [(r, side, 0) for side in range(2) for r in range(slots)]
        moved = []
        for s in range(chips):
            mixed = []
            for r in range(0, slots, 4):
                mixed += run_mix((s,), tuple(range(r, min(r + 4, slots))))
            mixed = [m[:width] for m in mixed]
            moved.append([mixed[0]] + [across(mixed[r], r) for r in range(1, slots)])
        turn = lax.bitwise_xor(dp, jnp.arange(slots))
        v = [v.reshape(slots, chips, width, -1)[turn][:, origins].reshape(slots * chips * width, -1)]
        together = [jnp.concatenate([one[r] for r in range(slots) for one in moved])]
        order = None
    depth = slots * chips * width
    run = lambda mirror, dtype: project(
        mirror, order, chips, width, depth, place, v, together, dtype
    )
    theirs = swap(run(True, jnp.bfloat16))
    mine = run(False, jnp.float32)
    return (mine + theirs.astype(jnp.float32)).astype(jnp.bfloat16)


def solution(mesh):
    count = mesh.shape["dp"]
    chips = mesh.shape["ctx"] // 2
    fine = Mesh(mesh.devices.reshape(count, chips, 2), ("dp", "z", "core"))
    every = ("dp", "z", "core")
    in_specs = (P(every, None), P(None, every, None), P(), P(), P(every, None))
    return jax.shard_map(
        functools.partial(shards, chips),
        mesh=fine,
        in_specs=in_specs,
        out_specs=P(every, None),
        check_vma=False,
    )
```

```python
import functools

import jax
import jax.numpy as jnp
from jax import lax
from jax.experimental import pallas as pl
from jax.experimental.pallas import tpu as pltpu
from jax.sharding import Mesh
from jax.sharding import PartitionSpec as P

GSIZE = 16
SHORT = 7
TAPS = 128
LANES = 128
WIDE = 64
HALO = 160
SMEM = pl.BlockSpec(memory_space=pltpu.SMEM)
VMEM = pl.BlockSpec(memory_space=pltpu.VMEM)
LIMIT = pltpu.CompilerParams(vmem_limit_bytes=24 * 1024 * 1024)


def ring_of(count):
    order = [i for i in range(count) if i == 0 or i % 2 == 1]
    order += [i for i in reversed(range(1, count)) if i % 2 == 0]
    return [(order[i], order[(i + 1) % count]) for i in range(count)]


def origins_of(count):
    previous = dict((target, source) for source, target in ring_of(count))
    table = [list(range(count))]
    for _ in range(count - 1):
        table.append([previous[i] for i in table[-1]])
    return table


def swap(block):
    return lax.ppermute(block, "core", [(0, 1), (1, 0)])


def across(block, r):
    count = lax.axis_size("dp")
    return lax.ppermute(block, "dp", [(i, i ^ r) for i in range(count)])


def tie(*groups):
    return lax.optimization_barrier(groups)


def dot(a, b):
    return jnp.dot(a, b, preferred_element_type=jnp.float32)


def nt(a, b):
    return lax.dot_general(a, b, (((1,), (1,)), ((), ())), preferred_element_type=jnp.float32)


def lay_kernel(parts, place_ref, *refs):
    pieces, (out_ref, sems) = refs[: len(parts)], refs[len(parts) :]
    rows = (out_ref.shape[0] - HALO) // 2
    core = place_ref[0]
    copies = []
    for ref, (side, start) in zip(pieces, parts):
        owner = core if side == 0 else 1 - core
        end = start + ref.shape[0]
        bounds = []
        if start < rows:
            bounds.append((start, min(end, rows), HALO + owner * rows + start))
        if end > rows:
            low = max(start, rows)
            bounds.append((low, end, owner * (HALO // 2) + low - rows))
        for low, high, at in bounds:
            copies.append(
                pltpu.make_async_copy(
                    ref.at[pl.ds(low - start, high - low)],
                    out_ref.at[pl.ds(pl.multiple_of(at, 16), high - low)],
                    sems.at[len(copies)],
                )
            )
    for copy in copies:
        copy.start()
    for copy in copies:
        copy.wait()


def lay(place, rows, parts, pieces):
    features = pieces[0].shape[1]
    return pl.pallas_call(
        functools.partial(lay_kernel, parts),
        out_shape=jax.ShapeDtypeStruct((HALO + 2 * rows, features), jnp.bfloat16),
        in_specs=[SMEM] + [pl.BlockSpec(memory_space=pl.ANY)] * len(pieces),
        out_specs=VMEM,
        scratch_shapes=[pltpu.SemaphoreType.DMA((2 * len(pieces),))],
        compiler_params=LIMIT,
        cost_estimate=pl.CostEstimate(
            flops=0, bytes_accessed=4 * (HALO + 2 * rows) * features, transcendentals=0
        ),
    )(place, *pieces)


def mix_kernel(steps, slots, place_ref, taps_ref, long_ref, *rest):
    weights, rest = rest[: len(steps)], rest[len(steps) :]
    tokens, rest = rest[:slots], rest[slots:]
    outs, rest = rest[:slots], rest[slots:]
    w, first, second, packed, turned, tiles = rest
    span = first.shape[1] - HALO
    count = WIDE // GSIZE
    band = 64
    blocks = span // TAPS
    lower = lax.broadcasted_iota(jnp.int32, (band, LANES), 1) < WIDE
    taps = [taps_ref[place_ref[2 + step]] for step in steps]

    for c, step in enumerate(steps):
        w[c, : 2 * WIDE] = weights[c][: 2 * WIDE]
        w[c, 2 * WIDE : 3 * WIDE] = jnp.zeros((WIDE, w.shape[2]), w.dtype)
        w[c, 3 * WIDE :] = weights[c][2 * WIDE :]
        filters = long_ref[place_ref[2 + step]]
        for g in range(count):
            line = jnp.concatenate(
                [jnp.zeros((1, TAPS), jnp.float32), filters[g : g + 1, :]], axis=1
            )
            square = pltpu.roll(
                jnp.broadcast_to(line, (2 * TAPS, 2 * TAPS)), 0, 1, stride=1, stride_axis=0
            )
            tiles[c * count + g] = square[:, :TAPS].astype(jnp.bfloat16)

    def project_unit(n, c, i):
        value = nt(tokens[i][...], w[c]).astype(jnp.bfloat16).astype(jnp.float32)
        first[n % 2] = value[:, :LANES]
        second[n % 2] = value[:, LANES:]

    def feat(ref, n, at, c, lanes):
        total = None
        for j in range(SHORT):
            term = taps[c][j : j + 1, lanes] * ref[n % 2, at - j : at - j + band, :]
            total = term if total is None else total + term
        return total

    units = [(c, i) for c in range(len(steps)) for i in range(slots)]
    project_unit(0, *units[0])
    for n, (c, i) in enumerate(units):
        if n + 1 < len(units):
            project_unit(n + 1, *units[n + 1])
        for m in range((TAPS + span) // band):
            at = HALO - TAPS + m * band
            x = feat(first, n, at, c, slice(0, LANES))
            y = feat(second, n, at, c, slice(LANES, 2 * LANES))
            packed[n % 2, m * band : (m + 1) * band, :] = jnp.where(lower, x, x * y).astype(
                jnp.bfloat16
            )
        turned[n] = packed[n % 2].T

    for c in range(len(steps)):
        mine = [n for n in range(len(units)) if units[n][0] == c]
        for g in range(count):
            channels = slice(WIDE + g * GSIZE, WIDE + (g + 1) * GSIZE)
            window = jnp.concatenate(
                [
                    turned[n, channels, b * TAPS : (b + 2) * TAPS]
                    for n in mine
                    for b in range(blocks)
                ],
                axis=0,
            )
            conv = dot(window, tiles[c * count + g])
            for k, n in enumerate(mine):
                row = jnp.concatenate(
                    [
                        conv[(k * blocks + b) * GSIZE : (k * blocks + b + 1) * GSIZE]
                        for b in range(blocks)
                    ],
                    axis=1,
                )
                query = turned[n, g * GSIZE : (g + 1) * GSIZE, TAPS:].astype(jnp.float32)
                at = c * WIDE + g * GSIZE
                outs[units[n][1]][at : at + GSIZE, :] = (query * row).astype(jnp.bfloat16)


def mix_chunks(steps, place, taps, filters, ws, tokens):
    features = ws[0].shape[1]
    slots, rows = len(tokens), (tokens[0].shape[0] - HALO) // 2
    weights = [ws[s] for s in steps]
    units = len(steps) * slots
    return pl.pallas_call(
        functools.partial(mix_kernel, steps, slots),
        out_shape=[jax.ShapeDtypeStruct((len(steps) * WIDE, 2 * rows), jnp.bfloat16)] * slots,
        in_specs=[SMEM] + [VMEM] * (2 + len(weights) + slots),
        out_specs=[VMEM] * slots,
        scratch_shapes=[
            pltpu.VMEM((len(steps), 4 * WIDE, features), jnp.bfloat16),
            pltpu.VMEM((2, HALO + 2 * rows, LANES), jnp.float32),
            pltpu.VMEM((2, HALO + 2 * rows, LANES), jnp.float32),
            pltpu.VMEM((2, TAPS + 2 * rows, LANES), jnp.bfloat16),
            pltpu.VMEM((units, LANES, TAPS + 2 * rows), jnp.bfloat16),
            pltpu.VMEM((len(steps) * WIDE // GSIZE, 2 * TAPS, TAPS), jnp.bfloat16),
        ],
        compiler_params=LIMIT,
        cost_estimate=pl.CostEstimate(
            flops=4 * units * 2 * rows * 4 * WIDE * features,
            bytes_accessed=2 * units * 2 * rows * features,
            transcendentals=0,
        ),
    )(place, taps, filters, *weights, *tokens)


def out_kernel(mirror, order, chips, width, counts, place_ref, *refs):
    weights, refs = refs[: counts[0]], refs[counts[0] :]
    parts, refs = refs[: counts[1]], refs[counts[1] :]
    out_ref, left, right, total = refs
    rows = out_ref.shape[0]
    core = place_ref[0]
    if mirror:
        core = 1 - core
    depth = left.shape[0]
    if order is None:
        left[...] = parts[0][...]
    else:
        for n, (k, row) in enumerate(order):
            at = pl.multiple_of((n // chips * chips + place_ref[2 + n % chips]) * width, width)
            left[pl.ds(at, width)] = parts[k][row : row + width]
    at = 0
    for ref in weights:
        right[at : at + ref.shape[0]] = ref[...]
        at += ref.shape[0]
    size = depth // 2
    at = pl.multiple_of(core * rows, LANES)
    tile = 512
    for start in range(0, depth, size):
        a = left[start : start + size, pl.ds(at, rows)].T
        for t in range(0, out_ref.shape[1], tile):
            here = slice(t, t + tile)
            value = dot(a, right[start : start + size, here])
            if start:
                value = value + total[:, here]
            if start + size < depth:
                total[:, here] = value
            else:
                out_ref[:, here] = value.astype(out_ref.dtype)


def project(mirror, order, chips, width, depth, place, v, parts, dtype):
    span, features = parts[0].shape[1], v[0].shape[-1]
    rows = span // 2
    counts = (len(v), len(parts))
    return pl.pallas_call(
        functools.partial(out_kernel, mirror, order, chips, width, counts),
        out_shape=jax.ShapeDtypeStruct((rows, features), dtype),
        in_specs=[SMEM] + [VMEM] * sum(counts),
        out_specs=VMEM,
        scratch_shapes=[
            pltpu.VMEM((depth, span), jnp.bfloat16),
            pltpu.VMEM((depth, features), jnp.bfloat16),
            pltpu.VMEM((rows, features), jnp.float32),
        ],
        compiler_params=LIMIT,
        cost_estimate=pl.CostEstimate(
            flops=4 * rows * features * depth,
            bytes_accessed=2 * depth * (features + span),
            transcendentals=0,
        ),
    )(place, *v, *parts)


def local_filters(chips, width, dp, core, short_taps, long_taps):
    part = short_taps.reshape(SHORT, 3, -1, 2, width)
    part = lax.dynamic_slice(
        part, (0, 0, dp * chips, core, 0), (SHORT, 3, chips, 1, width)
    ).reshape(SHORT, 3, chips, width)
    part = jnp.pad(part, ((0, 1), (0, 0), (0, 0), (0, WIDE - width)))
    part = jnp.transpose(part, (2, 0, 1, 3))
    taps = jnp.concatenate(
        [part[:, :, 0], part[:, :, 1], jnp.zeros_like(part[:, :, 0]), part[:, :, 2]], axis=2
    )
    groups = max(1, width // GSIZE)
    each = [
        lax.dynamic_slice_in_dim(
            long_taps, (2 * (dp * chips + i) + core) * width // GSIZE, groups, 0
        )
        for i in range(chips)
    ]
    filters = jnp.stack(each).astype(jnp.float32)
    return taps, jnp.pad(filters, ((0, 0), (0, WIDE // GSIZE - groups), (0, 0)))


def shards(chips, tokens, in_weight, short_taps, long_taps, out_weight):
    _, width, features = in_weight.shape
    rows = tokens.shape[0]
    slots = lax.axis_size("dp")
    dp = lax.axis_index("dp")
    z = lax.axis_index("z")
    core = lax.axis_index("core")
    ring = ring_of(chips)
    forward = lambda block: lax.ppermute(block, "z", ring)

    table = jnp.array(origins_of(chips), jnp.int32)
    origins = lax.dynamic_index_in_dim(table, z, 1, False)
    place = jnp.concatenate([jnp.stack([core, dp]).astype(jnp.int32), origins])
    taps, filters = local_filters(chips, width, dp, core, short_taps, long_taps)

    pairs = lambda c: [(2 * i + 1, 2 * (i + 1) + c) for i in range(chips - 1)]
    half = HALO // 2
    edge = lax.ppermute(tokens[rows - HALO : rows - half], ("z", "core"), pairs(0)) + lax.ppermute(
        tokens[rows - half :], ("z", "core"), pairs(1)
    )
    run_mix = lambda steps, which: mix_chunks(steps, place, taps, filters, ws, which)

    if slots == 4 and chips == 4 and width == WIDE:
        mid = HALO
        parts = [(0, 0), (0, mid), (1, 0), (1, mid)]
        ws = [in_weight.reshape(3 * width, features)]
        low = tokens[:mid]
        low_x, low_y = across(low, 1), across(low, 2)
        edge, low, low_x, low_y, v, ws[0] = tie(edge, low, low_x, low_y, out_weight, ws[0])

        v = lax.all_gather(v, "z")
        high = jnp.concatenate([tokens[mid:], edge])
        high_x, high_y = across(high, 1), across(high, 2)
        x0 = lay(place, rows, parts, [low, high, swap(low), swap(high)])
        low_x_twin, low_y_twin = swap(low_x), swap(low_y)
        (x0, high_x, high_y, low_x_twin, low_y_twin, ws, taps, filters, place, v) = tie(
            x0, high_x, high_y, low_x_twin, low_y_twin, ws, taps, filters, place, v
        )

        ws = list(ws) + [forward(ws[0])]
        far_x, far_y = across(low_y, 1), across(high_x, 2)
        x1 = lay(place, rows, parts, [low_x, high_x, low_x_twin, swap(high_x)])
        x2 = lay(place, rows, parts, [low_y, high_y, low_y_twin, swap(high_y)])
        mix0 = run_mix((0,), (x0, x1, x2))
        v = v.reshape(chips * width, -1)
        v_x, v_y = across(v, 1), across(v, 2)
        mix0, far_x, far_y, ws = tie(mix0, far_x, far_y, ws)

        ws = list(ws) + [forward(ws[1])]
        x3 = lay(place, rows, parts, [far_x, far_y, swap(far_x), swap(far_y)])
        mix1 = run_mix((1,), (x0, x1, x2))
        far01 = run_mix((0, 1), (x3,))
        mix1, far01, ws, v_x, v_y = tie(mix1, far01, ws, v_x, v_y)

        ws = list(ws) + [forward(ws[2])]
        cut = v.shape[0] // 2
        v_far = (across(v_y[:cut], 1), across(v_x[cut:], 2))
        moved = [[across(mix0[r], r), across(mix1[r], r)] for r in (1, 2)]
        moved.append([across(far01[0], 3)])
        mix2 = run_mix((2,), (x0, x1, x2, x3))
        mix2, moved, ws = tie(mix2, moved, ws)

        mix3 = run_mix((3,), (x0, x1, x2, x3))
        v = [v, v_x, v_y, *v_far]
        together = [mix0[0], mix1[0], mix2[0], mix3[0]]
        for r in (1, 2, 3):
            together += list(moved[r - 1]) + [across(mix2[r], r), across(mix3[r], r)]
        order = [(4 * r + s, 0) for r in range(3) for s in range(chips)]
        order += [(12, 0), (12, width), (13, 0), (14, 0)]
    else:
        v = lax.all_gather(out_weight, ("dp", "z"))
        block = jnp.concatenate([tokens, edge])
        w, ws = in_weight, []
        for s in range(chips):
            padded = jnp.pad(w, ((0, 0), (0, WIDE - width), (0, 0)))
            ws.append(padded.reshape(3 * WIDE, features))
            if s + 1 < chips:
                w = forward(w)
        blocks = [block] + [across(block, r) for r in range(1, slots)]
        xs = [lay(place, rows, [(0, 0), (1, 0)], [one, swap(one)]) for one in blocks]
        moved = []
        for s in range(chips):
            mixed = []
            for r in range(0, slots, 4):
                mixed += run_mix((s,), xs[r : r + 4])
            mixed = [m[:width] for m in mixed]
            moved.append([mixed[0]] + [across(mixed[r], r) for r in range(1, slots)])
        turn = lax.bitwise_xor(dp, jnp.arange(slots))
        v = [v.reshape(slots, chips, width, -1)[turn][:, origins].reshape(slots * chips * width, -1)]
        together = [jnp.concatenate([one[r] for r in range(slots) for one in moved])]
        order = None
    depth = slots * chips * width
    run = lambda mirror, dtype: project(
        mirror, order, chips, width, depth, place, v, together, dtype
    )
    theirs = swap(run(True, jnp.bfloat16))
    mine = run(False, jnp.float32)
    return (mine + theirs.astype(jnp.float32)).astype(jnp.bfloat16)


def solution(mesh):
    count = mesh.shape["dp"]
    chips = mesh.shape["ctx"] // 2
    fine = Mesh(mesh.devices.reshape(count, chips, 2), ("dp", "z", "core"))
    every = ("dp", "z", "core")
    in_specs = (P(every, None), P(None, every, None), P(), P(), P(every, None))
    return jax.shard_map(
        functools.partial(shards, chips),
        mesh=fine,
        in_specs=in_specs,
        out_specs=P(every, None),
        check_vma=False,
    )
```

```python
import functools

import jax
import jax.numpy as jnp
from jax import lax
from jax.experimental import pallas as pl
from jax.experimental.pallas import tpu as pltpu
from jax.sharding import Mesh
from jax.sharding import PartitionSpec as P

GSIZE = 16
SHORT = 7
TAPS = 128
LANES = 128
WIDE = 64
HALO = 160
SMEM = pl.BlockSpec(memory_space=pltpu.SMEM)
VMEM = pl.BlockSpec(memory_space=pltpu.VMEM)
LIMIT = pltpu.CompilerParams(vmem_limit_bytes=24 * 1024 * 1024)


def ring_of(count):
    order = [i for i in range(count) if i == 0 or i % 2 == 1]
    order += [i for i in reversed(range(1, count)) if i % 2 == 0]
    return [(order[i], order[(i + 1) % count]) for i in range(count)]


def origins_of(count):
    previous = dict((target, source) for source, target in ring_of(count))
    table = [list(range(count))]
    for _ in range(count - 1):
        table.append([previous[i] for i in table[-1]])
    return table


def swap(block):
    return lax.ppermute(block, "core", [(0, 1), (1, 0)])


def across(block, r):
    count = lax.axis_size("dp")
    return lax.ppermute(block, "dp", [(i, i ^ r) for i in range(count)])


def tie(*groups):
    return lax.optimization_barrier(groups)


def dot(a, b):
    return jnp.dot(a, b, preferred_element_type=jnp.float32)


def nt(a, b):
    return lax.dot_general(a, b, (((1,), (1,)), ((), ())), preferred_element_type=jnp.float32)


def lay_kernel(parts, place_ref, *refs):
    pieces, (out_ref, sems) = refs[: len(parts)], refs[len(parts) :]
    rows = (out_ref.shape[0] - HALO) // 2
    core = place_ref[0]
    copies = []
    for ref, (side, start) in zip(pieces, parts):
        owner = core if side == 0 else 1 - core
        end = start + ref.shape[0]
        bounds = []
        if start < rows:
            bounds.append((start, min(end, rows), HALO + owner * rows + start))
        if end > rows:
            low = max(start, rows)
            bounds.append((low, end, owner * (HALO // 2) + low - rows))
        for low, high, at in bounds:
            copies.append(
                pltpu.make_async_copy(
                    ref.at[pl.ds(low - start, high - low)],
                    out_ref.at[pl.ds(pl.multiple_of(at, 16), high - low)],
                    sems.at[len(copies)],
                )
            )
    for copy in copies:
        copy.start()
    for copy in copies:
        copy.wait()


def lay(place, rows, parts, pieces):
    features = pieces[0].shape[1]
    return pl.pallas_call(
        functools.partial(lay_kernel, parts),
        out_shape=jax.ShapeDtypeStruct((HALO + 2 * rows, features), jnp.bfloat16),
        in_specs=[SMEM] + [pl.BlockSpec(memory_space=pl.ANY)] * len(pieces),
        out_specs=VMEM,
        scratch_shapes=[pltpu.SemaphoreType.DMA((2 * len(pieces),))],
        compiler_params=LIMIT,
        cost_estimate=pl.CostEstimate(
            flops=0, bytes_accessed=4 * (HALO + 2 * rows) * features, transcendentals=0
        ),
    )(place, *pieces)


def mix_kernel(steps, slots, place_ref, taps_ref, long_ref, *rest):
    weights, rest = rest[: len(steps)], rest[len(steps) :]
    tokens, rest = rest[:slots], rest[slots:]
    outs, rest = rest[:slots], rest[slots:]
    w, first, second, packed, turned, tiles = rest
    span = first.shape[1] - HALO
    count = WIDE // GSIZE
    band = 64
    blocks = span // TAPS
    lower = lax.broadcasted_iota(jnp.int32, (band, LANES), 1) < WIDE
    taps = [taps_ref[place_ref[2 + step]] for step in steps]

    for c, step in enumerate(steps):
        w[c, : 2 * WIDE] = weights[c][: 2 * WIDE]
        w[c, 2 * WIDE : 3 * WIDE] = jnp.zeros((WIDE, w.shape[2]), w.dtype)
        w[c, 3 * WIDE :] = weights[c][2 * WIDE : 3 * WIDE]
        filters = long_ref[place_ref[2 + step]]
        for g in range(count):
            line = jnp.concatenate(
                [jnp.zeros((1, TAPS), jnp.float32), filters[g : g + 1, :]], axis=1
            )
            square = pltpu.roll(
                jnp.broadcast_to(line, (2 * TAPS, 2 * TAPS)), 0, 1, stride=1, stride_axis=0
            )
            tiles[c * count + g] = square[:, :TAPS].astype(jnp.bfloat16)

    def project_unit(n, c, i):
        value = nt(tokens[i][...], w[c]).astype(jnp.bfloat16).astype(jnp.float32)
        first[n % 2] = value[:, :LANES]
        second[n % 2] = value[:, LANES:]

    def feat(ref, n, at, c, lanes):
        total = None
        for j in range(SHORT):
            term = taps[c][j : j + 1, lanes] * ref[n % 2, at - j : at - j + band, :]
            total = term if total is None else total + term
        return total

    units = [(c, i) for c in range(len(steps)) for i in range(slots)]
    project_unit(0, *units[0])
    for n, (c, i) in enumerate(units):
        if n + 1 < len(units):
            project_unit(n + 1, *units[n + 1])
        for m in range((TAPS + span) // band):
            at = HALO - TAPS + m * band
            x = feat(first, n, at, c, slice(0, LANES))
            y = feat(second, n, at, c, slice(LANES, 2 * LANES))
            packed[n % 2, m * band : (m + 1) * band, :] = jnp.where(lower, x, x * y).astype(
                jnp.bfloat16
            )
        turned[n] = packed[n % 2].T

    for c in range(len(steps)):
        mine = [n for n in range(len(units)) if units[n][0] == c]
        for g in range(count):
            channels = slice(WIDE + g * GSIZE, WIDE + (g + 1) * GSIZE)
            window = jnp.concatenate(
                [
                    turned[n, channels, b * TAPS : (b + 2) * TAPS]
                    for n in mine
                    for b in range(blocks)
                ],
                axis=0,
            )
            conv = dot(window, tiles[c * count + g])
            for k, n in enumerate(mine):
                row = jnp.concatenate(
                    [
                        conv[(k * blocks + b) * GSIZE : (k * blocks + b + 1) * GSIZE]
                        for b in range(blocks)
                    ],
                    axis=1,
                )
                query = turned[n, g * GSIZE : (g + 1) * GSIZE, TAPS:].astype(jnp.float32)
                at = c * WIDE + g * GSIZE
                outs[units[n][1]][at : at + GSIZE, :] = (query * row).astype(jnp.bfloat16)


def mix_chunks(steps, place, taps, filters, ws, tokens):
    features = ws[0].shape[1]
    slots, rows = len(tokens), (tokens[0].shape[0] - HALO) // 2
    weights = [ws[s] for s in steps]
    units = len(steps) * slots
    return pl.pallas_call(
        functools.partial(mix_kernel, steps, slots),
        out_shape=[jax.ShapeDtypeStruct((len(steps) * WIDE, 2 * rows), jnp.bfloat16)] * slots,
        in_specs=[SMEM] + [VMEM] * (2 + len(weights) + slots),
        out_specs=[VMEM] * slots,
        scratch_shapes=[
            pltpu.VMEM((len(steps), 4 * WIDE, features), jnp.bfloat16),
            pltpu.VMEM((2, HALO + 2 * rows, LANES), jnp.float32),
            pltpu.VMEM((2, HALO + 2 * rows, LANES), jnp.float32),
            pltpu.VMEM((2, TAPS + 2 * rows, LANES), jnp.bfloat16),
            pltpu.VMEM((units, LANES, TAPS + 2 * rows), jnp.bfloat16),
            pltpu.VMEM((len(steps) * WIDE // GSIZE, 2 * TAPS, TAPS), jnp.bfloat16),
        ],
        compiler_params=LIMIT,
        cost_estimate=pl.CostEstimate(
            flops=4 * units * 2 * rows * 4 * WIDE * features,
            bytes_accessed=2 * units * 2 * rows * features,
            transcendentals=0,
        ),
    )(place, taps, filters, *weights, *tokens)


def out_kernel(mirror, order, width, counts, place_ref, *refs):
    weights, refs = refs[: counts[0]], refs[counts[0] :]
    parts, refs = refs[: counts[1]], refs[counts[1] :]
    out_ref, left, right, total = refs
    rows = out_ref.shape[0]
    core = place_ref[0]
    if mirror:
        core = 1 - core
    depth = left.shape[0]
    if order is None:
        left[...] = parts[0][...]
    else:
        for n, (k, row) in enumerate(order):
            left[n * width : (n + 1) * width] = parts[k][row : row + width]
    at = 0
    for ref in weights:
        right[at : at + ref.shape[0]] = ref[...]
        at += ref.shape[0]
    size = depth // 2
    at = pl.multiple_of(core * rows, LANES)
    tile = 512
    for start in range(0, depth, size):
        a = left[start : start + size, pl.ds(at, rows)].T
        for t in range(0, out_ref.shape[1], tile):
            here = slice(t, t + tile)
            value = dot(a, right[start : start + size, here])
            if start:
                value = value + total[:, here]
            if start + size < depth:
                total[:, here] = value
            else:
                out_ref[:, here] = value.astype(out_ref.dtype)


def project(mirror, order, width, depth, place, v, parts, dtype):
    span, features = parts[0].shape[1], v[0].shape[-1]
    rows = span // 2
    counts = (len(v), len(parts))
    return pl.pallas_call(
        functools.partial(out_kernel, mirror, order, width, counts),
        out_shape=jax.ShapeDtypeStruct((rows, features), dtype),
        in_specs=[SMEM] + [VMEM] * sum(counts),
        out_specs=VMEM,
        scratch_shapes=[
            pltpu.VMEM((depth, span), jnp.bfloat16),
            pltpu.VMEM((depth, features), jnp.bfloat16),
            pltpu.VMEM((rows, features), jnp.float32),
        ],
        compiler_params=LIMIT,
        cost_estimate=pl.CostEstimate(
            flops=4 * rows * features * depth,
            bytes_accessed=2 * depth * (features + span),
            transcendentals=0,
        ),
    )(place, *v, *parts)


def local_filters(chips, width, dp, core, short_taps, long_taps):
    part = short_taps.reshape(SHORT, 3, -1, 2, width)
    part = lax.dynamic_slice(
        part, (0, 0, dp * chips, core, 0), (SHORT, 3, chips, 1, width)
    ).reshape(SHORT, 3, chips, width)
    part = jnp.pad(part, ((0, 1), (0, 0), (0, 0), (0, WIDE - width)))
    part = jnp.transpose(part, (2, 0, 1, 3))
    taps = jnp.concatenate(
        [part[:, :, 0], part[:, :, 1], jnp.zeros_like(part[:, :, 0]), part[:, :, 2]], axis=2
    )
    groups = max(1, width // GSIZE)
    each = [
        lax.dynamic_slice_in_dim(
            long_taps, (2 * (dp * chips + i) + core) * width // GSIZE, groups, 0
        )
        for i in range(chips)
    ]
    filters = jnp.stack(each).astype(jnp.float32)
    return taps, jnp.pad(filters, ((0, 0), (0, WIDE // GSIZE - groups), (0, 0)))


def shards(chips, tokens, in_weight, short_taps, long_taps, out_weight):
    _, width, features = in_weight.shape
    rows = tokens.shape[0]
    slots = lax.axis_size("dp")
    dp = lax.axis_index("dp")
    z = lax.axis_index("z")
    core = lax.axis_index("core")
    ring = ring_of(chips)
    forward = lambda block: lax.ppermute(block, "z", ring)

    table = jnp.array(origins_of(chips), jnp.int32)
    origins = lax.dynamic_index_in_dim(table, z, 1, False)
    place = jnp.concatenate([jnp.stack([core, dp]).astype(jnp.int32), origins])
    taps, filters = local_filters(chips, width, dp, core, short_taps, long_taps)

    pairs = lambda c: [(2 * i + 1, 2 * (i + 1) + c) for i in range(chips - 1)]
    half = HALO // 2
    edge = lax.ppermute(tokens[rows - HALO : rows - half], ("z", "core"), pairs(0)) + lax.ppermute(
        tokens[rows - half :], ("z", "core"), pairs(1)
    )
    run_mix = lambda steps, which: mix_chunks(steps, place, taps, filters, ws, which)

    if slots == 4 and chips == 4 and width == WIDE:
        mid = HALO
        parts = [(0, 0), (0, mid), (1, 0), (1, mid)]
        spread = lambda one: [one] + [across(one, r) for r in range(1, slots)]
        ws = [jnp.concatenate([in_weight.reshape(3 * width, features), out_weight])]
        out_rows = lambda s: ws[s][3 * width :]
        low, high = tokens[:mid], tokens[mid:]
        low_x, low_y = across(low, 1), across(low, 2)
        edge, low, high, low_x, low_y, ws = tie(edge, low, high, low_x, low_y, ws)

        high = jnp.concatenate([high, edge])
        high_x, high_y = across(high, 1), across(high, 2)
        ws = [ws[0], forward(ws[0])]
        x0 = lay(place, rows, parts, [low, high, swap(low), swap(high)])
        low_x_twin, low_y_twin = swap(low_x), swap(low_y)
        (x0, high_x, high_y, low_x, low_y, low_x_twin, low_y_twin, ws, taps, filters, place) = tie(
            x0, high_x, high_y, low_x, low_y, low_x_twin, low_y_twin, ws, taps, filters, place
        )

        ws = [*ws, forward(ws[1])]
        far_x, far_y = across(low_y, 1), across(high_x, 2)
        x1 = lay(place, rows, parts, [low_x, high_x, low_x_twin, swap(high_x)])
        x2 = lay(place, rows, parts, [low_y, high_y, low_y_twin, swap(high_y)])
        mix0 = run_mix((0,), (x0, x1, x2))
        wide0 = spread(out_rows(0))
        mix0, far_x, far_y, ws, wide0 = tie(mix0, far_x, far_y, ws, wide0)

        ws = [*ws, forward(ws[2])]
        wide12 = spread(jnp.concatenate([out_rows(1), out_rows(2)]))
        x3 = lay(place, rows, parts, [far_x, far_y, swap(far_x), swap(far_y)])
        far = run_mix((0, 1, 2), (x3,))
        mix12 = run_mix((1, 2), (x0, x1, x2))
        moved = [[across(mix0[r], r), across(mix12[r], r)] for r in (1, 2)] + [[across(far[0], 3)]]
        moved, ws, wide12 = tie(moved, ws, wide12)

        wide3 = spread(out_rows(3))
        mix3 = run_mix((3,), (x0, x1, x2, x3))
        v = [one for r in range(slots) for one in (wide0[r], wide12[r], wide3[r])]
        together = [mix0[0], mix12[0], mix3[0]]
        for r in (1, 2, 3):
            together += [*moved[r - 1], across(mix3[r], r)]
        order = []
        for r in range(3):
            order += [(3 * r, 0), (3 * r + 1, 0), (3 * r + 1, width), (3 * r + 2, 0)]
        order += [(9, 0), (9, width), (9, 2 * width), (10, 0)]
    else:
        v = lax.all_gather(out_weight, ("dp", "z"))
        block = jnp.concatenate([tokens, edge])
        w, ws = in_weight, []
        for s in range(chips):
            padded = jnp.pad(w, ((0, 0), (0, WIDE - width), (0, 0)))
            ws.append(padded.reshape(3 * WIDE, features))
            if s + 1 < chips:
                w = forward(w)
        blocks = [block] + [across(block, r) for r in range(1, slots)]
        xs = [lay(place, rows, [(0, 0), (1, 0)], [one, swap(one)]) for one in blocks]
        moved = []
        for s in range(chips):
            mixed = []
            for r in range(0, slots, 4):
                mixed += run_mix((s,), xs[r : r + 4])
            mixed = [m[:width] for m in mixed]
            moved.append([mixed[0]] + [across(mixed[r], r) for r in range(1, slots)])
        turn = lax.bitwise_xor(dp, jnp.arange(slots))
        v = [v.reshape(slots, chips, width, -1)[turn][:, origins].reshape(slots * chips * width, -1)]
        together = [jnp.concatenate([one[r] for r in range(slots) for one in moved])]
        order = None
    depth = slots * chips * width
    run = lambda mirror, dtype: project(
        mirror, order, width, depth, place, v, together, dtype
    )
    theirs = swap(run(True, jnp.bfloat16))
    mine = run(False, jnp.float32)
    return (mine + theirs.astype(jnp.float32)).astype(jnp.bfloat16)


def solution(mesh):
    count = mesh.shape["dp"]
    chips = mesh.shape["ctx"] // 2
    fine = Mesh(mesh.devices.reshape(count, chips, 2), ("dp", "z", "core"))
    every = ("dp", "z", "core")
    in_specs = (P(every, None), P(None, every, None), P(), P(), P(every, None))
    return jax.shard_map(
        functools.partial(shards, chips),
        mesh=fine,
        in_specs=in_specs,
        out_specs=P(every, None),
        check_vma=False,
    )
```

```python
import functools

import jax
import jax.numpy as jnp
from jax import lax
from jax.experimental import pallas as pl
from jax.experimental.pallas import tpu as pltpu
from jax.sharding import Mesh
from jax.sharding import PartitionSpec as P

GSIZE = 16
SHORT = 7
TAPS = 128
LANES = 128
WIDE = 64
HALO = 160
SMEM = pl.BlockSpec(memory_space=pltpu.SMEM)
VMEM = pl.BlockSpec(memory_space=pltpu.VMEM)
LIMIT = pltpu.CompilerParams(vmem_limit_bytes=24 * 1024 * 1024)


def ring_of(count):
    order = [i for i in range(count) if i == 0 or i % 2 == 1]
    order += [i for i in reversed(range(1, count)) if i % 2 == 0]
    return [(order[i], order[(i + 1) % count]) for i in range(count)]


def origins_of(count):
    previous = dict((target, source) for source, target in ring_of(count))
    table = [list(range(count))]
    for _ in range(count - 1):
        table.append([previous[i] for i in table[-1]])
    return table


def swap(block):
    return lax.ppermute(block, "core", [(0, 1), (1, 0)])


def across(block, r):
    count = lax.axis_size("dp")
    return lax.ppermute(block, "dp", [(i, i ^ r) for i in range(count)])


def tie(*groups):
    return lax.optimization_barrier(groups)


def dot(a, b):
    return jnp.dot(a, b, preferred_element_type=jnp.float32)


def nt(a, b):
    return lax.dot_general(a, b, (((1,), (1,)), ((), ())), preferred_element_type=jnp.float32)


def lay_kernel(parts, place_ref, *refs):
    pieces, (out_ref, sems) = refs[: len(parts)], refs[len(parts) :]
    rows = (out_ref.shape[0] - HALO) // 2
    core = place_ref[0]
    copies = []
    for ref, (side, start) in zip(pieces, parts):
        owner = core if side == 0 else 1 - core
        end = start + ref.shape[0]
        bounds = []
        if start < rows:
            bounds.append((start, min(end, rows), HALO + owner * rows + start))
        if end > rows:
            low = max(start, rows)
            bounds.append((low, end, owner * (HALO // 2) + low - rows))
        for low, high, at in bounds:
            copies.append(
                pltpu.make_async_copy(
                    ref.at[pl.ds(low - start, high - low)],
                    out_ref.at[pl.ds(pl.multiple_of(at, 16), high - low)],
                    sems.at[len(copies)],
                )
            )
    for copy in copies:
        copy.start()
    for copy in copies:
        copy.wait()


def lay(place, rows, parts, pieces):
    features = pieces[0].shape[1]
    return pl.pallas_call(
        functools.partial(lay_kernel, parts),
        out_shape=jax.ShapeDtypeStruct((HALO + 2 * rows, features), jnp.bfloat16),
        in_specs=[SMEM] + [pl.BlockSpec(memory_space=pl.ANY)] * len(pieces),
        out_specs=VMEM,
        scratch_shapes=[pltpu.SemaphoreType.DMA((2 * len(pieces),))],
        compiler_params=LIMIT,
        cost_estimate=pl.CostEstimate(
            flops=0, bytes_accessed=4 * (HALO + 2 * rows) * features, transcendentals=0
        ),
    )(place, *pieces)


def mix_kernel(steps, slots, place_ref, taps_ref, long_ref, *rest):
    weights, rest = rest[: len(steps)], rest[len(steps) :]
    tokens, rest = rest[:slots], rest[slots:]
    outs, rest = rest[:slots], rest[slots:]
    w, first, second, packed, turned, tiles = rest
    span = first.shape[1] - HALO
    count = WIDE // GSIZE
    band = 64
    blocks = span // TAPS
    lower = lax.broadcasted_iota(jnp.int32, (band, LANES), 1) < WIDE
    taps = [taps_ref[place_ref[2 + step]] for step in steps]

    for c, step in enumerate(steps):
        w[c, : 2 * WIDE] = weights[c][: 2 * WIDE]
        w[c, 2 * WIDE : 3 * WIDE] = jnp.zeros((WIDE, w.shape[2]), w.dtype)
        w[c, 3 * WIDE :] = weights[c][2 * WIDE : 3 * WIDE]
        filters = long_ref[place_ref[2 + step]]
        for g in range(count):
            line = jnp.concatenate(
                [jnp.zeros((1, TAPS), jnp.float32), filters[g : g + 1, :]], axis=1
            )
            square = pltpu.roll(
                jnp.broadcast_to(line, (2 * TAPS, 2 * TAPS)), 0, 1, stride=1, stride_axis=0
            )
            tiles[c * count + g] = square[:, :TAPS].astype(jnp.bfloat16)

    def project_unit(n, c, i):
        value = nt(tokens[i][...], w[c]).astype(jnp.bfloat16).astype(jnp.float32)
        first[n % 2] = value[:, :LANES]
        second[n % 2] = value[:, LANES:]

    def feat(ref, n, at, c, lanes):
        total = None
        for j in range(SHORT):
            term = taps[c][j : j + 1, lanes] * ref[n % 2, at - j : at - j + band, :]
            total = term if total is None else total + term
        return total

    units = [(c, i) for c in range(len(steps)) for i in range(slots)]
    project_unit(0, *units[0])
    for n, (c, i) in enumerate(units):
        if n + 1 < len(units):
            project_unit(n + 1, *units[n + 1])
        for m in range((TAPS + span) // band):
            at = HALO - TAPS + m * band
            x = feat(first, n, at, c, slice(0, LANES))
            y = feat(second, n, at, c, slice(LANES, 2 * LANES))
            packed[n % 2, m * band : (m + 1) * band, :] = jnp.where(lower, x, x * y).astype(
                jnp.bfloat16
            )
        turned[n] = packed[n % 2].T

    for c in range(len(steps)):
        mine = [n for n in range(len(units)) if units[n][0] == c]
        for g in range(count):
            channels = slice(WIDE + g * GSIZE, WIDE + (g + 1) * GSIZE)
            window = jnp.concatenate(
                [
                    turned[n, channels, b * TAPS : (b + 2) * TAPS]
                    for n in mine
                    for b in range(blocks)
                ],
                axis=0,
            )
            conv = dot(window, tiles[c * count + g])
            for k, n in enumerate(mine):
                row = jnp.concatenate(
                    [
                        conv[(k * blocks + b) * GSIZE : (k * blocks + b + 1) * GSIZE]
                        for b in range(blocks)
                    ],
                    axis=1,
                )
                query = turned[n, g * GSIZE : (g + 1) * GSIZE, TAPS:].astype(jnp.float32)
                at = c * WIDE + g * GSIZE
                outs[units[n][1]][at : at + GSIZE, :] = (query * row).astype(jnp.bfloat16)


def mix_chunks(steps, place, taps, filters, ws, tokens):
    features = ws[0].shape[1]
    slots, rows = len(tokens), (tokens[0].shape[0] - HALO) // 2
    weights = [ws[s] for s in steps]
    units = len(steps) * slots
    return pl.pallas_call(
        functools.partial(mix_kernel, steps, slots),
        out_shape=[jax.ShapeDtypeStruct((len(steps) * WIDE, 2 * rows), jnp.bfloat16)] * slots,
        in_specs=[SMEM] + [VMEM] * (2 + len(weights) + slots),
        out_specs=[VMEM] * slots,
        scratch_shapes=[
            pltpu.VMEM((len(steps), 4 * WIDE, features), jnp.bfloat16),
            pltpu.VMEM((2, HALO + 2 * rows, LANES), jnp.float32),
            pltpu.VMEM((2, HALO + 2 * rows, LANES), jnp.float32),
            pltpu.VMEM((2, TAPS + 2 * rows, LANES), jnp.bfloat16),
            pltpu.VMEM((units, LANES, TAPS + 2 * rows), jnp.bfloat16),
            pltpu.VMEM((len(steps) * WIDE // GSIZE, 2 * TAPS, TAPS), jnp.bfloat16),
        ],
        compiler_params=LIMIT,
        cost_estimate=pl.CostEstimate(
            flops=4 * units * 2 * rows * 4 * WIDE * features,
            bytes_accessed=2 * units * 2 * rows * features,
            transcendentals=0,
        ),
    )(place, taps, filters, *weights, *tokens)


def out_kernel(mirror, order, width, counts, place_ref, *refs):
    weights, refs = refs[: counts[0]], refs[counts[0] :]
    parts, refs = refs[: counts[1]], refs[counts[1] :]
    out_ref, left, right, total = refs
    rows = out_ref.shape[0]
    core = place_ref[0]
    if mirror:
        core = 1 - core
    depth = left.shape[0]
    if order is None:
        left[...] = parts[0][...]
    else:
        for n, (k, row) in enumerate(order):
            left[n * width : (n + 1) * width] = parts[k][row : row + width]
    at = 0
    for ref in weights:
        right[at : at + ref.shape[0]] = ref[...]
        at += ref.shape[0]
    size = depth // 2
    at = pl.multiple_of(core * rows, LANES)
    tile = 512
    for start in range(0, depth, size):
        a = left[start : start + size, pl.ds(at, rows)].T
        for t in range(0, out_ref.shape[1], tile):
            here = slice(t, t + tile)
            value = dot(a, right[start : start + size, here])
            if start:
                value = value + total[:, here]
            if start + size < depth:
                total[:, here] = value
            else:
                out_ref[:, here] = value.astype(out_ref.dtype)


def project(mirror, order, width, depth, place, v, parts, dtype):
    span, features = parts[0].shape[1], v[0].shape[-1]
    rows = span // 2
    counts = (len(v), len(parts))
    return pl.pallas_call(
        functools.partial(out_kernel, mirror, order, width, counts),
        out_shape=jax.ShapeDtypeStruct((rows, features), dtype),
        in_specs=[SMEM] + [VMEM] * sum(counts),
        out_specs=VMEM,
        scratch_shapes=[
            pltpu.VMEM((depth, span), jnp.bfloat16),
            pltpu.VMEM((depth, features), jnp.bfloat16),
            pltpu.VMEM((rows, features), jnp.float32),
        ],
        compiler_params=LIMIT,
        cost_estimate=pl.CostEstimate(
            flops=4 * rows * features * depth,
            bytes_accessed=2 * depth * (features + span),
            transcendentals=0,
        ),
    )(place, *v, *parts)


def local_filters(chips, width, dp, core, short_taps, long_taps):
    part = short_taps.reshape(SHORT, 3, -1, 2, width)
    part = lax.dynamic_slice(
        part, (0, 0, dp * chips, core, 0), (SHORT, 3, chips, 1, width)
    ).reshape(SHORT, 3, chips, width)
    part = jnp.pad(part, ((0, 1), (0, 0), (0, 0), (0, WIDE - width)))
    part = jnp.transpose(part, (2, 0, 1, 3))
    taps = jnp.concatenate(
        [part[:, :, 0], part[:, :, 1], jnp.zeros_like(part[:, :, 0]), part[:, :, 2]], axis=2
    )
    groups = max(1, width // GSIZE)
    each = [
        lax.dynamic_slice_in_dim(
            long_taps, (2 * (dp * chips + i) + core) * width // GSIZE, groups, 0
        )
        for i in range(chips)
    ]
    filters = jnp.stack(each).astype(jnp.float32)
    return taps, jnp.pad(filters, ((0, 0), (0, WIDE // GSIZE - groups), (0, 0)))


def shards(chips, tokens, in_weight, short_taps, long_taps, out_weight):
    _, width, features = in_weight.shape
    rows = tokens.shape[0]
    slots = lax.axis_size("dp")
    dp = lax.axis_index("dp")
    z = lax.axis_index("z")
    core = lax.axis_index("core")
    ring = ring_of(chips)
    forward = lambda block: lax.ppermute(block, "z", ring)

    table = jnp.array(origins_of(chips), jnp.int32)
    origins = lax.dynamic_index_in_dim(table, z, 1, False)
    place = jnp.concatenate([jnp.stack([core, dp]).astype(jnp.int32), origins])
    taps, filters = local_filters(chips, width, dp, core, short_taps, long_taps)

    pairs = lambda c: [(2 * i + 1, 2 * (i + 1) + c) for i in range(chips - 1)]
    half = HALO // 2
    edge = lax.ppermute(tokens[rows - HALO : rows - half], ("z", "core"), pairs(0)) + lax.ppermute(
        tokens[rows - half :], ("z", "core"), pairs(1)
    )
    run_mix = lambda steps, which: mix_chunks(steps, place, taps, filters, ws, which)

    if slots == 4 and chips == 4 and width == WIDE:
        mid = HALO
        parts = [(0, 0), (0, mid), (1, 0), (1, mid)]
        ws, vs = [in_weight.reshape(3 * width, features)], [out_weight, forward(out_weight)]
        low, high = tokens[:mid], tokens[mid:]
        low_x, low_y = across(low, 1), across(low, 2)
        edge, low, high, low_x, low_y, ws, vs = tie(edge, low, high, low_x, low_y, ws, vs)

        high = jnp.concatenate([high, edge])
        high_x, high_y = across(high, 1), across(high, 2)
        ws, vs = [ws[0], forward(ws[0])], [*vs, forward(vs[1])]
        x0 = lay(place, rows, parts, [low, high, swap(low), swap(high)])
        low_x_twin, low_y_twin = swap(low_x), swap(low_y)
        both = lambda one: [one, across(one, 1), across(one, 2)]
        (x0, high_x, high_y, low_x, low_y, low_x_twin, low_y_twin, ws, vs, taps, filters, place) = tie(
            x0, high_x, high_y, low_x, low_y, low_x_twin, low_y_twin, ws, vs, taps, filters, place
        )

        ws, vs = [*ws, forward(ws[1])], [*vs, forward(vs[2])]
        far_x, far_y = across(low_y, 1), across(high_x, 2)
        v1 = both(jnp.concatenate([vs[0], vs[1]]))
        x1 = lay(place, rows, parts, [low_x, high_x, low_x_twin, swap(high_x)])
        x2 = lay(place, rows, parts, [low_y, high_y, low_y_twin, swap(high_y)])
        mix01 = run_mix((0, 1), (x0, x1, x2))
        mix01, far_x, far_y, ws, vs, v1 = tie(mix01, far_x, far_y, ws, vs, v1)

        ws = [*ws, forward(ws[2])]
        v0, v1 = across(v1[2][:width], 1), [*v1, across(v1[1][width:], 2)]
        v2, v3 = both(vs[2]), both(vs[3])
        moved = [[across(mix01[r], r)] for r in (1, 2)]
        x3 = lay(place, rows, parts, [far_x, far_y, swap(far_x), swap(far_y)])
        mix2 = run_mix((2,), (x0, x1, x2))
        far = run_mix((0, 1, 2), (x3,))
        mix2, far, moved, ws, v0, v1, v2, v3 = tie(mix2, far, moved, ws, v0, v1, v2, v3)

        v2, v3 = [*v2, across(v2[2], 1)], [*v3, across(v3[1], 2)]
        mix3 = run_mix((3,), (x0, x1, x2, x3))
        v = [one[r] for r in range(slots) for one in (v1, v2, v3)]
        v.insert(9, v0)
        together = [mix01[0], mix2[0], mix3[0]]
        for r in (1, 2):
            together += [*moved[r - 1], across(mix2[r], r), across(mix3[r], r)]
        together += [across(far[0], 3), across(mix3[3], 3)]
        order = []
        for r in range(3):
            order += [(3 * r, 0), (3 * r, width), (3 * r + 1, 0), (3 * r + 2, 0)]
        order += [(9, 0), (9, width), (9, 2 * width), (10, 0)]
    else:
        v = lax.all_gather(out_weight, ("dp", "z"))
        block = jnp.concatenate([tokens, edge])
        w, ws = in_weight, []
        for s in range(chips):
            padded = jnp.pad(w, ((0, 0), (0, WIDE - width), (0, 0)))
            ws.append(padded.reshape(3 * WIDE, features))
            if s + 1 < chips:
                w = forward(w)
        blocks = [block] + [across(block, r) for r in range(1, slots)]
        xs = [lay(place, rows, [(0, 0), (1, 0)], [one, swap(one)]) for one in blocks]
        moved = []
        for s in range(chips):
            mixed = []
            for r in range(0, slots, 4):
                mixed += run_mix((s,), xs[r : r + 4])
            mixed = [m[:width] for m in mixed]
            moved.append([mixed[0]] + [across(mixed[r], r) for r in range(1, slots)])
        turn = lax.bitwise_xor(dp, jnp.arange(slots))
        v = [v.reshape(slots, chips, width, -1)[turn][:, origins].reshape(slots * chips * width, -1)]
        together = [jnp.concatenate([one[r] for r in range(slots) for one in moved])]
        order = None
    depth = slots * chips * width
    run = lambda mirror, dtype: project(
        mirror, order, width, depth, place, v, together, dtype
    )
    theirs = swap(run(True, jnp.bfloat16))
    mine = run(False, jnp.float32)
    return (mine + theirs.astype(jnp.float32)).astype(jnp.bfloat16)


def solution(mesh):
    count = mesh.shape["dp"]
    chips = mesh.shape["ctx"] // 2
    fine = Mesh(mesh.devices.reshape(count, chips, 2), ("dp", "z", "core"))
    every = ("dp", "z", "core")
    in_specs = (P(every, None), P(None, every, None), P(), P(), P(every, None))
    return jax.shard_map(
        functools.partial(shards, chips),
        mesh=fine,
        in_specs=in_specs,
        out_specs=P(every, None),
        check_vma=False,
    )
```

```python
import functools

import jax
import jax.numpy as jnp
from jax import lax
from jax.experimental import pallas as pl
from jax.experimental.pallas import tpu as pltpu
from jax.sharding import Mesh
from jax.sharding import PartitionSpec as P

GSIZE = 16
SHORT = 7
TAPS = 128
LANES = 128
WIDE = 64
HALO = 160
SMEM = pl.BlockSpec(memory_space=pltpu.SMEM)
VMEM = pl.BlockSpec(memory_space=pltpu.VMEM)
LIMIT = pltpu.CompilerParams(vmem_limit_bytes=24 * 1024 * 1024)


def ring_of(count):
    order = [i for i in range(count) if i == 0 or i % 2 == 1]
    order += [i for i in reversed(range(1, count)) if i % 2 == 0]
    return [(order[i], order[(i + 1) % count]) for i in range(count)]


def origins_of(count):
    previous = dict((target, source) for source, target in ring_of(count))
    table = [list(range(count))]
    for _ in range(count - 1):
        table.append([previous[i] for i in table[-1]])
    return table


def swap(block):
    return lax.ppermute(block, "core", [(0, 1), (1, 0)])


def across(block, r):
    count = lax.axis_size("dp")
    return lax.ppermute(block, "dp", [(i, i ^ r) for i in range(count)])


def tie(*groups):
    return lax.optimization_barrier(groups)


def dot(a, b):
    return jnp.dot(a, b, preferred_element_type=jnp.float32)


def nt(a, b):
    return lax.dot_general(a, b, (((1,), (1,)), ((), ())), preferred_element_type=jnp.float32)


def lay_kernel(parts, place_ref, *refs):
    pieces, (out_ref, sems) = refs[: len(parts)], refs[len(parts) :]
    rows = (out_ref.shape[0] - HALO) // 2
    core = place_ref[0]
    copies = []
    for ref, (side, start) in zip(pieces, parts):
        owner = core if side == 0 else 1 - core
        end = start + ref.shape[0]
        bounds = []
        if start < rows:
            bounds.append((start, min(end, rows), HALO + owner * rows + start))
        if end > rows:
            low = max(start, rows)
            bounds.append((low, end, owner * (HALO // 2) + low - rows))
        for low, high, at in bounds:
            copies.append(
                pltpu.make_async_copy(
                    ref.at[pl.ds(low - start, high - low)],
                    out_ref.at[pl.ds(pl.multiple_of(at, 16), high - low)],
                    sems.at[len(copies)],
                )
            )
    for copy in copies:
        copy.start()
    for copy in copies:
        copy.wait()


def lay(place, rows, parts, pieces):
    features = pieces[0].shape[1]
    return pl.pallas_call(
        functools.partial(lay_kernel, parts),
        out_shape=jax.ShapeDtypeStruct((HALO + 2 * rows, features), jnp.bfloat16),
        in_specs=[SMEM] + [pl.BlockSpec(memory_space=pl.ANY)] * len(pieces),
        out_specs=VMEM,
        scratch_shapes=[pltpu.SemaphoreType.DMA((2 * len(pieces),))],
        compiler_params=LIMIT,
        cost_estimate=pl.CostEstimate(
            flops=0, bytes_accessed=4 * (HALO + 2 * rows) * features, transcendentals=0
        ),
    )(place, *pieces)


def mix_kernel(steps, slots, place_ref, taps_ref, long_ref, *rest):
    weights, rest = rest[: len(steps)], rest[len(steps) :]
    tokens, rest = rest[:slots], rest[slots:]
    outs, rest = rest[:slots], rest[slots:]
    w, first, second, packed, turned, tiles = rest
    span = first.shape[1] - HALO
    count = WIDE // GSIZE
    band = 64
    blocks = span // TAPS
    lower = lax.broadcasted_iota(jnp.int32, (band, LANES), 1) < WIDE
    taps = [taps_ref[place_ref[2 + step]] for step in steps]

    for c, step in enumerate(steps):
        w[c, : 2 * WIDE] = weights[c][: 2 * WIDE]
        w[c, 2 * WIDE : 3 * WIDE] = jnp.zeros((WIDE, w.shape[2]), w.dtype)
        w[c, 3 * WIDE :] = weights[c][2 * WIDE : 3 * WIDE]
        filters = long_ref[place_ref[2 + step]]
        for g in range(count):
            line = jnp.concatenate(
                [jnp.zeros((1, TAPS), jnp.float32), filters[g : g + 1, :]], axis=1
            )
            square = pltpu.roll(
                jnp.broadcast_to(line, (2 * TAPS, 2 * TAPS)), 0, 1, stride=1, stride_axis=0
            )
            tiles[c * count + g] = square[:, :TAPS].astype(jnp.bfloat16)

    def project_unit(n, c, i):
        value = nt(tokens[i][...], w[c]).astype(jnp.bfloat16).astype(jnp.float32)
        first[n % 2] = value[:, :LANES]
        second[n % 2] = value[:, LANES:]

    def feat(ref, n, at, c, lanes):
        total = None
        for j in range(SHORT):
            term = taps[c][j : j + 1, lanes] * ref[n % 2, at - j : at - j + band, :]
            total = term if total is None else total + term
        return total

    units = [(c, i) for c in range(len(steps)) for i in range(slots)]
    project_unit(0, *units[0])
    for n, (c, i) in enumerate(units):
        if n + 1 < len(units):
            project_unit(n + 1, *units[n + 1])
        for m in range((TAPS + span) // band):
            at = HALO - TAPS + m * band
            x = feat(first, n, at, c, slice(0, LANES))
            y = feat(second, n, at, c, slice(LANES, 2 * LANES))
            packed[n % 2, m * band : (m + 1) * band, :] = jnp.where(lower, x, x * y).astype(
                jnp.bfloat16
            )
        turned[n] = packed[n % 2].T

    for c in range(len(steps)):
        mine = [n for n in range(len(units)) if units[n][0] == c]
        for g in range(count):
            channels = slice(WIDE + g * GSIZE, WIDE + (g + 1) * GSIZE)
            window = jnp.concatenate(
                [
                    turned[n, channels, b * TAPS : (b + 2) * TAPS]
                    for n in mine
                    for b in range(blocks)
                ],
                axis=0,
            )
            conv = dot(window, tiles[c * count + g])
            for k, n in enumerate(mine):
                row = jnp.concatenate(
                    [
                        conv[(k * blocks + b) * GSIZE : (k * blocks + b + 1) * GSIZE]
                        for b in range(blocks)
                    ],
                    axis=1,
                )
                query = turned[n, g * GSIZE : (g + 1) * GSIZE, TAPS:].astype(jnp.float32)
                at = c * WIDE + g * GSIZE
                outs[units[n][1]][at : at + GSIZE, :] = (query * row).astype(jnp.bfloat16)


def mix_chunks(steps, place, taps, filters, ws, tokens):
    features = ws[0].shape[1]
    slots, rows = len(tokens), (tokens[0].shape[0] - HALO) // 2
    weights = [ws[s] for s in steps]
    units = len(steps) * slots
    return pl.pallas_call(
        functools.partial(mix_kernel, steps, slots),
        out_shape=[jax.ShapeDtypeStruct((len(steps) * WIDE, 2 * rows), jnp.bfloat16)] * slots,
        in_specs=[SMEM] + [VMEM] * (2 + len(weights) + slots),
        out_specs=[VMEM] * slots,
        scratch_shapes=[
            pltpu.VMEM((len(steps), 4 * WIDE, features), jnp.bfloat16),
            pltpu.VMEM((2, HALO + 2 * rows, LANES), jnp.float32),
            pltpu.VMEM((2, HALO + 2 * rows, LANES), jnp.float32),
            pltpu.VMEM((2, TAPS + 2 * rows, LANES), jnp.bfloat16),
            pltpu.VMEM((units, LANES, TAPS + 2 * rows), jnp.bfloat16),
            pltpu.VMEM((len(steps) * WIDE // GSIZE, 2 * TAPS, TAPS), jnp.bfloat16),
        ],
        compiler_params=LIMIT,
        cost_estimate=pl.CostEstimate(
            flops=4 * units * 2 * rows * 4 * WIDE * features,
            bytes_accessed=2 * units * 2 * rows * features,
            transcendentals=0,
        ),
    )(place, taps, filters, *weights, *tokens)


def out_kernel(mirror, order, width, counts, place_ref, *refs):
    weights, refs = refs[: counts[0]], refs[counts[0] :]
    parts, refs = refs[: counts[1]], refs[counts[1] :]
    out_ref, left, right, total = refs
    rows = out_ref.shape[0]
    core = place_ref[0]
    if mirror:
        core = 1 - core
    depth = left.shape[0]
    if order is None:
        left[...] = parts[0][...]
    else:
        for n, (k, row) in enumerate(order):
            left[n * width : (n + 1) * width] = parts[k][row : row + width]
    at = 0
    for ref in weights:
        right[at : at + ref.shape[0]] = ref[...]
        at += ref.shape[0]
    size = depth // 2
    at = pl.multiple_of(core * rows, LANES)
    tile = 512
    for start in range(0, depth, size):
        a = left[start : start + size, pl.ds(at, rows)].T
        for t in range(0, out_ref.shape[1], tile):
            here = slice(t, t + tile)
            value = dot(a, right[start : start + size, here])
            if start:
                value = value + total[:, here]
            if start + size < depth:
                total[:, here] = value
            else:
                out_ref[:, here] = value.astype(out_ref.dtype)


def project(mirror, order, width, depth, place, v, parts, dtype):
    span, features = parts[0].shape[1], v[0].shape[-1]
    rows = span // 2
    counts = (len(v), len(parts))
    return pl.pallas_call(
        functools.partial(out_kernel, mirror, order, width, counts),
        out_shape=jax.ShapeDtypeStruct((rows, features), dtype),
        in_specs=[SMEM] + [VMEM] * sum(counts),
        out_specs=VMEM,
        scratch_shapes=[
            pltpu.VMEM((depth, span), jnp.bfloat16),
            pltpu.VMEM((depth, features), jnp.bfloat16),
            pltpu.VMEM((rows, features), jnp.float32),
        ],
        compiler_params=LIMIT,
        cost_estimate=pl.CostEstimate(
            flops=4 * rows * features * depth,
            bytes_accessed=2 * depth * (features + span),
            transcendentals=0,
        ),
    )(place, *v, *parts)


def local_filters(chips, width, dp, core, short_taps, long_taps):
    part = short_taps.reshape(SHORT, 3, -1, 2, width)
    part = lax.dynamic_slice(
        part, (0, 0, dp * chips, core, 0), (SHORT, 3, chips, 1, width)
    ).reshape(SHORT, 3, chips, width)
    part = jnp.pad(part, ((0, 1), (0, 0), (0, 0), (0, WIDE - width)))
    part = jnp.transpose(part, (2, 0, 1, 3))
    taps = jnp.concatenate(
        [part[:, :, 0], part[:, :, 1], jnp.zeros_like(part[:, :, 0]), part[:, :, 2]], axis=2
    )
    groups = max(1, width // GSIZE)
    each = [
        lax.dynamic_slice_in_dim(
            long_taps, (2 * (dp * chips + i) + core) * width // GSIZE, groups, 0
        )
        for i in range(chips)
    ]
    filters = jnp.stack(each).astype(jnp.float32)
    return taps, jnp.pad(filters, ((0, 0), (0, WIDE // GSIZE - groups), (0, 0)))


def shards(chips, tokens, in_weight, short_taps, long_taps, out_weight):
    _, width, features = in_weight.shape
    rows = tokens.shape[0]
    slots = lax.axis_size("dp")
    dp = lax.axis_index("dp")
    z = lax.axis_index("z")
    core = lax.axis_index("core")
    ring = ring_of(chips)
    forward = lambda block: lax.ppermute(block, "z", ring)

    table = jnp.array(origins_of(chips), jnp.int32)
    origins = lax.dynamic_index_in_dim(table, z, 1, False)
    place = jnp.concatenate([jnp.stack([core, dp]).astype(jnp.int32), origins])
    taps, filters = local_filters(chips, width, dp, core, short_taps, long_taps)

    pairs = lambda c: [(2 * i + 1, 2 * (i + 1) + c) for i in range(chips - 1)]
    half = HALO // 2
    edge = lax.ppermute(tokens[rows - HALO : rows - half], ("z", "core"), pairs(0)) + lax.ppermute(
        tokens[rows - half :], ("z", "core"), pairs(1)
    )
    run_mix = lambda steps, which: mix_chunks(steps, place, taps, filters, ws, which)

    if slots == 4 and chips == 4 and width == WIDE:
        mid = HALO
        parts = [(0, 0), (0, mid), (1, 0), (1, mid)]
        ws, vs = [in_weight.reshape(3 * width, features)], [out_weight, forward(out_weight)]
        low, high = tokens[:mid], tokens[mid:]
        low_x, low_y = across(low, 1), across(low, 2)
        edge, low, high, low_x, low_y, ws, vs, taps, filters, place = tie(
            edge, low, high, low_x, low_y, ws, vs, taps, filters, place
        )

        high = jnp.concatenate([high, edge])
        high_x, high_y = across(high, 1), across(high, 2)
        ws = [ws[0], forward(ws[0])]
        x0 = lay(place, rows, parts, [low, high, swap(low), swap(high)])
        low_x_twin, low_y_twin = swap(low_x), swap(low_y)
        both = lambda one: [one, across(one, 1), across(one, 2)]
        x0, vs = tie(x0, vs)
        vs = [*vs, forward(vs[1])]
        v0 = both(vs[0])
        (x0, high_x, high_y, low_x, low_y, low_x_twin, low_y_twin, ws, vs, v0) = tie(
            x0, high_x, high_y, low_x, low_y, low_x_twin, low_y_twin, ws, vs, v0
        )

        ws, vs = [*ws, forward(ws[1])], [*vs, forward(vs[2])]
        far_x, far_y = across(low_y, 1), across(high_x, 2)
        v1 = both(vs[1])
        x1 = lay(place, rows, parts, [low_x, high_x, low_x_twin, swap(high_x)])
        x2 = lay(place, rows, parts, [low_y, high_y, low_y_twin, swap(high_y)])
        mix01 = run_mix((0, 1), (x0, x1, x2))
        mix01, far_x, far_y, ws, vs, v1 = tie(mix01, far_x, far_y, ws, vs, v1)

        ws = [*ws, forward(ws[2])]
        v0, v1 = [*v0, across(v0[2], 1)], [*v1, across(v1[1], 2)]
        v2, v3 = both(vs[2]), both(vs[3])
        x3 = lay(place, rows, parts, [far_x, far_y, swap(far_x), swap(far_y)])
        mix2 = run_mix((2,), (x0, x1, x2))
        far = run_mix((0, 1, 2), (x3,))
        moved = [[across(mix01[r], r), across(mix2[r], r)] for r in (1, 2)] + [across(far[0], 3)]
        mix2, far, moved, ws, v0, v1, v2, v3 = tie(mix2, far, moved, ws, v0, v1, v2, v3)

        v2, v3 = [*v2, across(v2[2], 1)], [*v3, across(v3[1], 2)]
        mix3 = run_mix((3,), (x0, x1, x2, x3))
        v = [one[r] for r in range(slots) for one in (v0, v1, v2, v3)]
        together = [mix01[0], mix2[0], mix3[0]]
        for r in (1, 2):
            together += [*moved[r - 1], across(mix3[r], r)]
        together += [moved[2], across(mix3[3], 3)]
        order = []
        for r in range(3):
            order += [(3 * r, 0), (3 * r, width), (3 * r + 1, 0), (3 * r + 2, 0)]
        order += [(9, 0), (9, width), (9, 2 * width), (10, 0)]
    else:
        v = lax.all_gather(out_weight, ("dp", "z"))
        block = jnp.concatenate([tokens, edge])
        w, ws = in_weight, []
        for s in range(chips):
            padded = jnp.pad(w, ((0, 0), (0, WIDE - width), (0, 0)))
            ws.append(padded.reshape(3 * WIDE, features))
            if s + 1 < chips:
                w = forward(w)
        blocks = [block] + [across(block, r) for r in range(1, slots)]
        xs = [lay(place, rows, [(0, 0), (1, 0)], [one, swap(one)]) for one in blocks]
        moved = []
        for s in range(chips):
            mixed = []
            for r in range(0, slots, 4):
                mixed += run_mix((s,), xs[r : r + 4])
            mixed = [m[:width] for m in mixed]
            moved.append([mixed[0]] + [across(mixed[r], r) for r in range(1, slots)])
        turn = lax.bitwise_xor(dp, jnp.arange(slots))
        v = [v.reshape(slots, chips, width, -1)[turn][:, origins].reshape(slots * chips * width, -1)]
        together = [jnp.concatenate([one[r] for r in range(slots) for one in moved])]
        order = None
    depth = slots * chips * width
    run = lambda mirror, dtype: project(
        mirror, order, width, depth, place, v, together, dtype
    )
    theirs = swap(run(True, jnp.bfloat16))
    mine = run(False, jnp.float32)
    return (mine + theirs.astype(jnp.float32)).astype(jnp.bfloat16)


def solution(mesh):
    count = mesh.shape["dp"]
    chips = mesh.shape["ctx"] // 2
    fine = Mesh(mesh.devices.reshape(count, chips, 2), ("dp", "z", "core"))
    every = ("dp", "z", "core")
    in_specs = (P(every, None), P(None, every, None), P(), P(), P(every, None))
    return jax.shard_map(
        functools.partial(shards, chips),
        mesh=fine,
        in_specs=in_specs,
        out_specs=P(every, None),
        check_vma=False,
    )
```

```python
import functools

import jax
import jax.numpy as jnp
from jax import lax
from jax.experimental import pallas as pl
from jax.experimental.pallas import tpu as pltpu
from jax.sharding import Mesh
from jax.sharding import PartitionSpec as P

GSIZE = 16
SHORT = 7
TAPS = 128
LANES = 128
WIDE = 64
HALO = 160
SMEM = pl.BlockSpec(memory_space=pltpu.SMEM)
VMEM = pl.BlockSpec(memory_space=pltpu.VMEM)
LIMIT = pltpu.CompilerParams(vmem_limit_bytes=24 * 1024 * 1024)


def ring_of(count):
    order = [i for i in range(count) if i == 0 or i % 2 == 1]
    order += [i for i in reversed(range(1, count)) if i % 2 == 0]
    return [(order[i], order[(i + 1) % count]) for i in range(count)]


def origins_of(count):
    previous = dict((target, source) for source, target in ring_of(count))
    table = [list(range(count))]
    for _ in range(count - 1):
        table.append([previous[i] for i in table[-1]])
    return table


def swap(block):
    return lax.ppermute(block, "core", [(0, 1), (1, 0)])


def across(block, r):
    count = lax.axis_size("dp")
    return lax.ppermute(block, "dp", [(i, i ^ r) for i in range(count)])


def tie(*groups):
    return lax.optimization_barrier(groups)


def dot(a, b):
    return jnp.dot(a, b, preferred_element_type=jnp.float32)


def nt(a, b):
    return lax.dot_general(a, b, (((1,), (1,)), ((), ())), preferred_element_type=jnp.float32)


def lay_kernel(parts, place_ref, *refs):
    pieces, (out_ref, sems) = refs[: len(parts)], refs[len(parts) :]
    rows = (out_ref.shape[0] - HALO) // 2
    core = place_ref[0]
    copies = []
    for ref, (side, start) in zip(pieces, parts):
        owner = core if side == 0 else 1 - core
        end = start + ref.shape[0]
        bounds = []
        if start < rows:
            bounds.append((start, min(end, rows), HALO + owner * rows + start))
        if end > rows:
            low = max(start, rows)
            bounds.append((low, end, owner * (HALO // 2) + low - rows))
        for low, high, at in bounds:
            copies.append(
                pltpu.make_async_copy(
                    ref.at[pl.ds(low - start, high - low)],
                    out_ref.at[pl.ds(pl.multiple_of(at, 16), high - low)],
                    sems.at[len(copies)],
                )
            )
    for copy in copies:
        copy.start()
    for copy in copies:
        copy.wait()


def lay(place, rows, parts, pieces):
    features = pieces[0].shape[1]
    return pl.pallas_call(
        functools.partial(lay_kernel, parts),
        out_shape=jax.ShapeDtypeStruct((HALO + 2 * rows, features), jnp.bfloat16),
        in_specs=[SMEM] + [pl.BlockSpec(memory_space=pl.ANY)] * len(pieces),
        out_specs=VMEM,
        scratch_shapes=[pltpu.SemaphoreType.DMA((2 * len(pieces),))],
        compiler_params=LIMIT,
        cost_estimate=pl.CostEstimate(
            flops=0, bytes_accessed=4 * (HALO + 2 * rows) * features, transcendentals=0
        ),
    )(place, *pieces)


def mix_kernel(steps, slots, place_ref, taps_ref, long_ref, *rest):
    weights, rest = rest[: len(steps)], rest[len(steps) :]
    tokens, rest = rest[:slots], rest[slots:]
    outs, rest = rest[:slots], rest[slots:]
    w, first, second, packed, turned, tiles = rest
    span = first.shape[1] - HALO
    count = WIDE // GSIZE
    band = 64
    blocks = span // TAPS
    lower = lax.broadcasted_iota(jnp.int32, (band, LANES), 1) < WIDE
    taps = [taps_ref[place_ref[2 + step]] for step in steps]

    for c, step in enumerate(steps):
        w[c, : 2 * WIDE] = weights[c][: 2 * WIDE]
        w[c, 2 * WIDE : 3 * WIDE] = jnp.zeros((WIDE, w.shape[2]), w.dtype)
        w[c, 3 * WIDE :] = weights[c][2 * WIDE : 3 * WIDE]
        filters = long_ref[place_ref[2 + step]]
        for g in range(count):
            line = jnp.concatenate(
                [jnp.zeros((1, TAPS), jnp.float32), filters[g : g + 1, :]], axis=1
            )
            square = pltpu.roll(
                jnp.broadcast_to(line, (2 * TAPS, 2 * TAPS)), 0, 1, stride=1, stride_axis=0
            )
            tiles[c * count + g] = square[:, :TAPS].astype(jnp.bfloat16)

    def project_unit(n, c, i):
        value = nt(tokens[i][...], w[c]).astype(jnp.bfloat16).astype(jnp.float32)
        first[n % 2] = value[:, :LANES]
        second[n % 2] = value[:, LANES:]

    def feat(ref, n, at, c, lanes):
        total = None
        for j in range(SHORT):
            term = taps[c][j : j + 1, lanes] * ref[n % 2, at - j : at - j + band, :]
            total = term if total is None else total + term
        return total

    units = [(c, i) for c in range(len(steps)) for i in range(slots)]
    project_unit(0, *units[0])
    for n, (c, i) in enumerate(units):
        if n + 1 < len(units):
            project_unit(n + 1, *units[n + 1])
        for m in range((TAPS + span) // band):
            at = HALO - TAPS + m * band
            x = feat(first, n, at, c, slice(0, LANES))
            y = feat(second, n, at, c, slice(LANES, 2 * LANES))
            packed[n % 2, m * band : (m + 1) * band, :] = jnp.where(lower, x, x * y).astype(
                jnp.bfloat16
            )
        turned[n] = packed[n % 2].T

    for c in range(len(steps)):
        mine = [n for n in range(len(units)) if units[n][0] == c]
        for g in range(count):
            channels = slice(WIDE + g * GSIZE, WIDE + (g + 1) * GSIZE)
            window = jnp.concatenate(
                [
                    turned[n, channels, b * TAPS : (b + 2) * TAPS]
                    for n in mine
                    for b in range(blocks)
                ],
                axis=0,
            )
            conv = dot(window, tiles[c * count + g])
            for k, n in enumerate(mine):
                row = jnp.concatenate(
                    [
                        conv[(k * blocks + b) * GSIZE : (k * blocks + b + 1) * GSIZE]
                        for b in range(blocks)
                    ],
                    axis=1,
                )
                query = turned[n, g * GSIZE : (g + 1) * GSIZE, TAPS:].astype(jnp.float32)
                at = c * WIDE + g * GSIZE
                outs[units[n][1]][at : at + GSIZE, :] = (query * row).astype(jnp.bfloat16)


def mix_chunks(steps, place, taps, filters, ws, tokens):
    features = ws[0].shape[1]
    slots, rows = len(tokens), (tokens[0].shape[0] - HALO) // 2
    weights = [ws[s] for s in steps]
    units = len(steps) * slots
    return pl.pallas_call(
        functools.partial(mix_kernel, steps, slots),
        out_shape=[jax.ShapeDtypeStruct((len(steps) * WIDE, 2 * rows), jnp.bfloat16)] * slots,
        in_specs=[SMEM] + [VMEM] * (2 + len(weights) + slots),
        out_specs=[VMEM] * slots,
        scratch_shapes=[
            pltpu.VMEM((len(steps), 4 * WIDE, features), jnp.bfloat16),
            pltpu.VMEM((2, HALO + 2 * rows, LANES), jnp.float32),
            pltpu.VMEM((2, HALO + 2 * rows, LANES), jnp.float32),
            pltpu.VMEM((2, TAPS + 2 * rows, LANES), jnp.bfloat16),
            pltpu.VMEM((units, LANES, TAPS + 2 * rows), jnp.bfloat16),
            pltpu.VMEM((len(steps) * WIDE // GSIZE, 2 * TAPS, TAPS), jnp.bfloat16),
        ],
        compiler_params=LIMIT,
        cost_estimate=pl.CostEstimate(
            flops=4 * units * 2 * rows * 4 * WIDE * features,
            bytes_accessed=2 * units * 2 * rows * features,
            transcendentals=0,
        ),
    )(place, taps, filters, *weights, *tokens)


def out_kernel(mirror, order, width, counts, place_ref, *refs):
    weights, refs = refs[: counts[0]], refs[counts[0] :]
    parts, refs = refs[: counts[1]], refs[counts[1] :]
    out_ref, left, right, total = refs
    rows = out_ref.shape[0]
    core = place_ref[0]
    if mirror:
        core = 1 - core
    depth = left.shape[0]
    if order is None:
        left[...] = parts[0][...]
    else:
        for n, (k, row) in enumerate(order):
            left[n * width : (n + 1) * width] = parts[k][row : row + width]
    at = 0
    for ref in weights:
        right[at : at + ref.shape[0]] = ref[...]
        at += ref.shape[0]
    size = depth // 2
    at = pl.multiple_of(core * rows, LANES)
    tile = 512
    for start in range(0, depth, size):
        a = left[start : start + size, pl.ds(at, rows)].T
        for t in range(0, out_ref.shape[1], tile):
            here = slice(t, t + tile)
            value = dot(a, right[start : start + size, here])
            if start:
                value = value + total[:, here]
            if start + size < depth:
                total[:, here] = value
            else:
                out_ref[:, here] = value.astype(out_ref.dtype)


def project(mirror, order, width, depth, place, v, parts, dtype):
    span, features = parts[0].shape[1], v[0].shape[-1]
    rows = span // 2
    counts = (len(v), len(parts))
    return pl.pallas_call(
        functools.partial(out_kernel, mirror, order, width, counts),
        out_shape=jax.ShapeDtypeStruct((rows, features), dtype),
        in_specs=[SMEM] + [VMEM] * sum(counts),
        out_specs=VMEM,
        scratch_shapes=[
            pltpu.VMEM((depth, span), jnp.bfloat16),
            pltpu.VMEM((depth, features), jnp.bfloat16),
            pltpu.VMEM((rows, features), jnp.float32),
        ],
        compiler_params=LIMIT,
        cost_estimate=pl.CostEstimate(
            flops=4 * rows * features * depth,
            bytes_accessed=2 * depth * (features + span),
            transcendentals=0,
        ),
    )(place, *v, *parts)


def local_filters(chips, width, dp, core, short_taps, long_taps):
    part = short_taps.reshape(SHORT, 3, -1, 2, width)
    part = lax.dynamic_slice(
        part, (0, 0, dp * chips, core, 0), (SHORT, 3, chips, 1, width)
    ).reshape(SHORT, 3, chips, width)
    part = jnp.pad(part, ((0, 1), (0, 0), (0, 0), (0, WIDE - width)))
    part = jnp.transpose(part, (2, 0, 1, 3))
    taps = jnp.concatenate(
        [part[:, :, 0], part[:, :, 1], jnp.zeros_like(part[:, :, 0]), part[:, :, 2]], axis=2
    )
    groups = max(1, width // GSIZE)
    each = [
        lax.dynamic_slice_in_dim(
            long_taps, (2 * (dp * chips + i) + core) * width // GSIZE, groups, 0
        )
        for i in range(chips)
    ]
    filters = jnp.stack(each).astype(jnp.float32)
    return taps, jnp.pad(filters, ((0, 0), (0, WIDE // GSIZE - groups), (0, 0)))


def shards(chips, tokens, in_weight, short_taps, long_taps, out_weight):
    _, width, features = in_weight.shape
    rows = tokens.shape[0]
    slots = lax.axis_size("dp")
    dp = lax.axis_index("dp")
    z = lax.axis_index("z")
    core = lax.axis_index("core")
    ring = ring_of(chips)
    forward = lambda block: lax.ppermute(block, "z", ring)

    table = jnp.array(origins_of(chips), jnp.int32)
    origins = lax.dynamic_index_in_dim(table, z, 1, False)
    place = jnp.concatenate([jnp.stack([core, dp]).astype(jnp.int32), origins])
    taps, filters = local_filters(chips, width, dp, core, short_taps, long_taps)

    pairs = lambda c: [(2 * i + 1, 2 * (i + 1) + c) for i in range(chips - 1)]
    half = HALO // 2
    edge = lax.ppermute(tokens[rows - HALO : rows - half], ("z", "core"), pairs(0)) + lax.ppermute(
        tokens[rows - half :], ("z", "core"), pairs(1)
    )
    run_mix = lambda steps, which: mix_chunks(steps, place, taps, filters, ws, which)

    if slots == 4 and chips == 4 and width == WIDE:
        mid = HALO
        parts = [(0, 0), (0, mid), (1, 0), (1, mid)]
        ws, vs = [in_weight.reshape(3 * width, features)], [out_weight, forward(out_weight)]
        low, high = tokens[:mid], tokens[mid:]
        low_x, low_y = across(low, 1), across(low, 2)
        edge, low, high, low_x, low_y, ws, vs, taps, filters, place = tie(
            edge, low, high, low_x, low_y, ws, vs, taps, filters, place
        )

        high = jnp.concatenate([high, edge])
        high_x, high_y = across(high, 1), across(high, 2)
        ws = [ws[0], forward(ws[0])]
        x0 = lay(place, rows, parts, [low, high, swap(low), swap(high)])
        low_x_twin, low_y_twin = swap(low_x), swap(low_y)
        both = lambda one: [one, across(one, 1), across(one, 2)]
        x0, vs = tie(x0, vs)
        vs = [*vs, forward(vs[1])]
        v0 = both(vs[0])
        (x0, high_x, high_y, low_x, low_y, low_x_twin, low_y_twin, ws, vs, v0) = tie(
            x0, high_x, high_y, low_x, low_y, low_x_twin, low_y_twin, ws, vs, v0
        )

        ws, vs = [*ws, forward(ws[1])], [*vs, forward(vs[2])]
        far_x, far_y = across(low_y, 1), across(high_x, 2)
        v1 = both(vs[1])
        x1 = lay(place, rows, parts, [low_x, high_x, low_x_twin, swap(high_x)])
        x2 = lay(place, rows, parts, [low_y, high_y, low_y_twin, swap(high_y)])
        mix01 = run_mix((0, 1), (x0, x1, x2))
        moved = [[across(mix01[r], r)] for r in (1, 2)]
        mix01, moved, far_x, far_y, ws, vs, v1 = tie(mix01, moved, far_x, far_y, ws, vs, v1)

        ws = [*ws, forward(ws[2])]
        v0, v1 = [*v0, across(v0[2], 1)], [*v1, across(v1[1], 2)]
        v2, v3 = both(vs[2]), both(vs[3])
        x3 = lay(place, rows, parts, [far_x, far_y, swap(far_x), swap(far_y)])
        mix2 = run_mix((2,), (x0, x1, x2))
        far = run_mix((0, 1, 2), (x3,))
        moved = [[*moved[r - 1], across(mix2[r], r)] for r in (1, 2)] + [across(far[0], 3)]
        mix2, far, moved, ws, v0, v1 = tie(mix2, far, moved, ws, v0, v1)

        v2, v3 = [*v2, across(v2[2], 1)], [*v3, across(v3[1], 2)]
        mix3 = run_mix((3,), (x0, x1, x2, x3))
        v = [one[r] for r in range(slots) for one in (v0, v1, v2, v3)]
        together = [mix01[0], mix2[0], mix3[0]]
        for r in (1, 2):
            together += [*moved[r - 1], across(mix3[r], r)]
        together += [moved[2], across(mix3[3], 3)]
        order = []
        for r in range(3):
            order += [(3 * r, 0), (3 * r, width), (3 * r + 1, 0), (3 * r + 2, 0)]
        order += [(9, 0), (9, width), (9, 2 * width), (10, 0)]
    else:
        v = lax.all_gather(out_weight, ("dp", "z"))
        block = jnp.concatenate([tokens, edge])
        w, ws = in_weight, []
        for s in range(chips):
            padded = jnp.pad(w, ((0, 0), (0, WIDE - width), (0, 0)))
            ws.append(padded.reshape(3 * WIDE, features))
            if s + 1 < chips:
                w = forward(w)
        blocks = [block] + [across(block, r) for r in range(1, slots)]
        xs = [lay(place, rows, [(0, 0), (1, 0)], [one, swap(one)]) for one in blocks]
        moved = []
        for s in range(chips):
            mixed = []
            for r in range(0, slots, 4):
                mixed += run_mix((s,), xs[r : r + 4])
            mixed = [m[:width] for m in mixed]
            moved.append([mixed[0]] + [across(mixed[r], r) for r in range(1, slots)])
        turn = lax.bitwise_xor(dp, jnp.arange(slots))
        v = [v.reshape(slots, chips, width, -1)[turn][:, origins].reshape(slots * chips * width, -1)]
        together = [jnp.concatenate([one[r] for r in range(slots) for one in moved])]
        order = None
    depth = slots * chips * width
    run = lambda mirror, dtype: project(
        mirror, order, width, depth, place, v, together, dtype
    )
    theirs = swap(run(True, jnp.bfloat16))
    mine = run(False, jnp.float32)
    return (mine + theirs.astype(jnp.float32)).astype(jnp.bfloat16)


def solution(mesh):
    count = mesh.shape["dp"]
    chips = mesh.shape["ctx"] // 2
    fine = Mesh(mesh.devices.reshape(count, chips, 2), ("dp", "z", "core"))
    every = ("dp", "z", "core")
    in_specs = (P(every, None), P(None, every, None), P(), P(), P(every, None))
    return jax.shard_map(
        functools.partial(shards, chips),
        mesh=fine,
        in_specs=in_specs,
        out_specs=P(every, None),
        check_vma=False,
    )
```

```python
import functools

import jax
import jax.numpy as jnp
from jax import lax
from jax.experimental import pallas as pl
from jax.experimental.pallas import tpu as pltpu
from jax.sharding import Mesh
from jax.sharding import PartitionSpec as P

GSIZE = 16
SHORT = 7
TAPS = 128
LANES = 128
WIDE = 64
HALO = 160
SMEM = pl.BlockSpec(memory_space=pltpu.SMEM)
VMEM = pl.BlockSpec(memory_space=pltpu.VMEM)
LIMIT = pltpu.CompilerParams(vmem_limit_bytes=24 * 1024 * 1024)


def ring_of(count):
    order = [i for i in range(count) if i == 0 or i % 2 == 1]
    order += [i for i in reversed(range(1, count)) if i % 2 == 0]
    return [(order[i], order[(i + 1) % count]) for i in range(count)]


def origins_of(count):
    previous = dict((target, source) for source, target in ring_of(count))
    table = [list(range(count))]
    for _ in range(count - 1):
        table.append([previous[i] for i in table[-1]])
    return table


def swap(block):
    return lax.ppermute(block, "core", [(0, 1), (1, 0)])


def across(block, r):
    count = lax.axis_size("dp")
    return lax.ppermute(block, "dp", [(i, i ^ r) for i in range(count)])


def tie(*groups):
    return lax.optimization_barrier(groups)


def dot(a, b):
    return jnp.dot(a, b, preferred_element_type=jnp.float32)


def nt(a, b):
    return lax.dot_general(a, b, (((1,), (1,)), ((), ())), preferred_element_type=jnp.float32)


def lay_kernel(parts, place_ref, *refs):
    pieces, (out_ref, sems) = refs[: len(parts)], refs[len(parts) :]
    rows = (out_ref.shape[0] - HALO) // 2
    core = place_ref[0]
    copies = []
    for ref, (side, start) in zip(pieces, parts):
        owner = core if side == 0 else 1 - core
        end = start + ref.shape[0]
        bounds = []
        if start < rows:
            bounds.append((start, min(end, rows), HALO + owner * rows + start))
        if end > rows:
            low = max(start, rows)
            bounds.append((low, end, owner * (HALO // 2) + low - rows))
        for low, high, at in bounds:
            copies.append(
                pltpu.make_async_copy(
                    ref.at[pl.ds(low - start, high - low)],
                    out_ref.at[pl.ds(pl.multiple_of(at, 16), high - low)],
                    sems.at[len(copies)],
                )
            )
    for copy in copies:
        copy.start()
    for copy in copies:
        copy.wait()


def lay(place, rows, parts, pieces):
    features = pieces[0].shape[1]
    return pl.pallas_call(
        functools.partial(lay_kernel, parts),
        out_shape=jax.ShapeDtypeStruct((HALO + 2 * rows, features), jnp.bfloat16),
        in_specs=[SMEM] + [pl.BlockSpec(memory_space=pl.ANY)] * len(pieces),
        out_specs=VMEM,
        scratch_shapes=[pltpu.SemaphoreType.DMA((2 * len(pieces),))],
        compiler_params=LIMIT,
        cost_estimate=pl.CostEstimate(
            flops=0, bytes_accessed=4 * (HALO + 2 * rows) * features, transcendentals=0
        ),
    )(place, *pieces)


def mix_kernel(steps, slots, place_ref, taps_ref, long_ref, *rest):
    weights, rest = rest[: len(steps)], rest[len(steps) :]
    tokens, rest = rest[:slots], rest[slots:]
    outs, rest = rest[:slots], rest[slots:]
    w, first, second, packed, turned, tiles = rest
    span = first.shape[1] - HALO
    count = WIDE // GSIZE
    band = 64
    blocks = span // TAPS
    lower = lax.broadcasted_iota(jnp.int32, (band, LANES), 1) < WIDE
    taps = [taps_ref[place_ref[2 + step]] for step in steps]

    for c, step in enumerate(steps):
        w[c, : 2 * WIDE] = weights[c][: 2 * WIDE]
        w[c, 2 * WIDE : 3 * WIDE] = jnp.zeros((WIDE, w.shape[2]), w.dtype)
        w[c, 3 * WIDE :] = weights[c][2 * WIDE : 3 * WIDE]
        filters = long_ref[place_ref[2 + step]]
        for g in range(count):
            line = jnp.concatenate(
                [jnp.zeros((1, TAPS), jnp.float32), filters[g : g + 1, :]], axis=1
            )
            square = pltpu.roll(
                jnp.broadcast_to(line, (2 * TAPS, 2 * TAPS)), 0, 1, stride=1, stride_axis=0
            )
            tiles[c * count + g] = square[:, :TAPS].astype(jnp.bfloat16)

    def project_unit(n, c, i):
        value = nt(tokens[i][...], w[c]).astype(jnp.bfloat16).astype(jnp.float32)
        first[n % 2] = value[:, :LANES]
        second[n % 2] = value[:, LANES:]

    def feat(ref, n, at, c, lanes):
        total = None
        for j in range(SHORT):
            term = taps[c][j : j + 1, lanes] * ref[n % 2, at - j : at - j + band, :]
            total = term if total is None else total + term
        return total

    units = [(c, i) for c in range(len(steps)) for i in range(slots)]
    project_unit(0, *units[0])
    for n, (c, i) in enumerate(units):
        if n + 1 < len(units):
            project_unit(n + 1, *units[n + 1])
        for m in range((TAPS + span) // band):
            at = HALO - TAPS + m * band
            x = feat(first, n, at, c, slice(0, LANES))
            y = feat(second, n, at, c, slice(LANES, 2 * LANES))
            packed[n % 2, m * band : (m + 1) * band, :] = jnp.where(lower, x, x * y).astype(
                jnp.bfloat16
            )
        turned[n] = packed[n % 2].T

    for c in range(len(steps)):
        mine = [n for n in range(len(units)) if units[n][0] == c]
        for g in range(count):
            channels = slice(WIDE + g * GSIZE, WIDE + (g + 1) * GSIZE)
            window = jnp.concatenate(
                [
                    turned[n, channels, b * TAPS : (b + 2) * TAPS]
                    for n in mine
                    for b in range(blocks)
                ],
                axis=0,
            )
            conv = dot(window, tiles[c * count + g])
            for k, n in enumerate(mine):
                row = jnp.concatenate(
                    [
                        conv[(k * blocks + b) * GSIZE : (k * blocks + b + 1) * GSIZE]
                        for b in range(blocks)
                    ],
                    axis=1,
                )
                query = turned[n, g * GSIZE : (g + 1) * GSIZE, TAPS:].astype(jnp.float32)
                at = c * WIDE + g * GSIZE
                outs[units[n][1]][at : at + GSIZE, :] = (query * row).astype(jnp.bfloat16)


def mix_chunks(steps, place, taps, filters, ws, tokens):
    features = ws[0].shape[1]
    slots, rows = len(tokens), (tokens[0].shape[0] - HALO) // 2
    weights = [ws[s] for s in steps]
    units = len(steps) * slots
    return pl.pallas_call(
        functools.partial(mix_kernel, steps, slots),
        out_shape=[jax.ShapeDtypeStruct((len(steps) * WIDE, 2 * rows), jnp.bfloat16)] * slots,
        in_specs=[SMEM] + [VMEM] * (2 + len(weights) + slots),
        out_specs=[VMEM] * slots,
        scratch_shapes=[
            pltpu.VMEM((len(steps), 4 * WIDE, features), jnp.bfloat16),
            pltpu.VMEM((2, HALO + 2 * rows, LANES), jnp.float32),
            pltpu.VMEM((2, HALO + 2 * rows, LANES), jnp.float32),
            pltpu.VMEM((2, TAPS + 2 * rows, LANES), jnp.bfloat16),
            pltpu.VMEM((units, LANES, TAPS + 2 * rows), jnp.bfloat16),
            pltpu.VMEM((len(steps) * WIDE // GSIZE, 2 * TAPS, TAPS), jnp.bfloat16),
        ],
        compiler_params=LIMIT,
        cost_estimate=pl.CostEstimate(
            flops=4 * units * 2 * rows * 4 * WIDE * features,
            bytes_accessed=2 * units * 2 * rows * features,
            transcendentals=0,
        ),
    )(place, taps, filters, *weights, *tokens)


def out_kernel(mirror, order, width, counts, place_ref, *refs):
    weights, refs = refs[: counts[0]], refs[counts[0] :]
    parts, refs = refs[: counts[1]], refs[counts[1] :]
    out_ref, left, right, total = refs
    rows = out_ref.shape[0]
    core = place_ref[0]
    if mirror:
        core = 1 - core
    depth = left.shape[0]
    if order is None:
        left[...] = parts[0][...]
    else:
        for n, (k, row) in enumerate(order):
            left[n * width : (n + 1) * width] = parts[k][row : row + width]
    at = 0
    for ref in weights:
        right[at : at + ref.shape[0]] = ref[...]
        at += ref.shape[0]
    size = depth // 2
    at = pl.multiple_of(core * rows, LANES)
    tile = 512
    for start in range(0, depth, size):
        a = left[start : start + size, pl.ds(at, rows)].T
        for t in range(0, out_ref.shape[1], tile):
            here = slice(t, t + tile)
            value = dot(a, right[start : start + size, here])
            if start:
                value = value + total[:, here]
            if start + size < depth:
                total[:, here] = value
            else:
                out_ref[:, here] = value.astype(out_ref.dtype)


def project(mirror, order, width, depth, place, v, parts, dtype):
    span, features = parts[0].shape[1], v[0].shape[-1]
    rows = span // 2
    counts = (len(v), len(parts))
    return pl.pallas_call(
        functools.partial(out_kernel, mirror, order, width, counts),
        out_shape=jax.ShapeDtypeStruct((rows, features), dtype),
        in_specs=[SMEM] + [VMEM] * sum(counts),
        out_specs=VMEM,
        scratch_shapes=[
            pltpu.VMEM((depth, span), jnp.bfloat16),
            pltpu.VMEM((depth, features), jnp.bfloat16),
            pltpu.VMEM((rows, features), jnp.float32),
        ],
        compiler_params=LIMIT,
        cost_estimate=pl.CostEstimate(
            flops=4 * rows * features * depth,
            bytes_accessed=2 * depth * (features + span),
            transcendentals=0,
        ),
    )(place, *v, *parts)


def local_filters(chips, width, dp, core, short_taps, long_taps):
    part = short_taps.reshape(SHORT, 3, -1, 2, width)
    part = lax.dynamic_slice(
        part, (0, 0, dp * chips, core, 0), (SHORT, 3, chips, 1, width)
    ).reshape(SHORT, 3, chips, width)
    part = jnp.pad(part, ((0, 1), (0, 0), (0, 0), (0, WIDE - width)))
    part = jnp.transpose(part, (2, 0, 1, 3))
    taps = jnp.concatenate(
        [part[:, :, 0], part[:, :, 1], jnp.zeros_like(part[:, :, 0]), part[:, :, 2]], axis=2
    )
    groups = max(1, width // GSIZE)
    each = [
        lax.dynamic_slice_in_dim(
            long_taps, (2 * (dp * chips + i) + core) * width // GSIZE, groups, 0
        )
        for i in range(chips)
    ]
    filters = jnp.stack(each).astype(jnp.float32)
    return taps, jnp.pad(filters, ((0, 0), (0, WIDE // GSIZE - groups), (0, 0)))


def shards(chips, tokens, in_weight, short_taps, long_taps, out_weight):
    _, width, features = in_weight.shape
    rows = tokens.shape[0]
    slots = lax.axis_size("dp")
    dp = lax.axis_index("dp")
    z = lax.axis_index("z")
    core = lax.axis_index("core")
    ring = ring_of(chips)
    forward = lambda block: lax.ppermute(block, "z", ring)

    table = jnp.array(origins_of(chips), jnp.int32)
    origins = lax.dynamic_index_in_dim(table, z, 1, False)
    place = jnp.concatenate([jnp.stack([core, dp]).astype(jnp.int32), origins])
    taps, filters = local_filters(chips, width, dp, core, short_taps, long_taps)

    pairs = lambda c: [(2 * i + 1, 2 * (i + 1) + c) for i in range(chips - 1)]
    half = HALO // 2
    edge = lax.ppermute(tokens[rows - HALO : rows - half], ("z", "core"), pairs(0)) + lax.ppermute(
        tokens[rows - half :], ("z", "core"), pairs(1)
    )
    run_mix = lambda steps, which: mix_chunks(steps, place, taps, filters, ws, which)

    if slots == 4 and chips == 4 and width == WIDE:
        mid = HALO
        parts = [(0, 0), (0, mid), (1, 0), (1, mid)]
        ws, vs = [in_weight.reshape(3 * width, features)], [out_weight, forward(out_weight)]
        low, high = tokens[:mid], tokens[mid:]
        low_x, low_y = across(low, 1), across(low, 2)
        edge, low, high, low_x, low_y, ws, vs, taps, filters, place = tie(
            edge, low, high, low_x, low_y, ws, vs, taps, filters, place
        )

        high = jnp.concatenate([high, edge])
        high_x, high_y = across(high, 1), across(high, 2)
        ws = [ws[0], forward(ws[0])]
        x0 = lay(place, rows, parts, [low, high, swap(low), swap(high)])
        low_x_twin, low_y_twin = swap(low_x), swap(low_y)
        both = lambda one: [one, across(one, 1), across(one, 2)]
        x0, vs = tie(x0, vs)
        third = forward(vs[1])
        v0 = both(vs[0])
        (x0, high_x, high_y, low_x, low_y, low_x_twin, low_y_twin, ws, vs, v0) = tie(
            x0, high_x, high_y, low_x, low_y, low_x_twin, low_y_twin, ws, vs, v0
        )

        ws = [*ws, forward(ws[1])]
        far_x, far_y = across(low_y, 1), across(high_x, 2)
        v1 = both(vs[1])
        x1 = lay(place, rows, parts, [low_x, high_x, low_x_twin, swap(high_x)])
        x2 = lay(place, rows, parts, [low_y, high_y, low_y_twin, swap(high_y)])
        x1, third = tie(x1, third)
        vs = [*vs, third, forward(third)]
        mix01 = run_mix((0, 1), (x0, x1, x2))
        moved = [[across(mix01[r], r)] for r in (1, 2)]
        mix01, moved, far_x, far_y, ws, vs[2], v1 = tie(mix01, moved, far_x, far_y, ws, vs[2], v1)

        ws = [*ws, forward(ws[2])]
        v0, v1 = [*v0, across(v0[2], 1)], [*v1, across(v1[1], 2)]
        v2, v3 = both(vs[2]), both(vs[3])
        x3 = lay(place, rows, parts, [far_x, far_y, swap(far_x), swap(far_y)])
        mix2 = run_mix((2,), (x0, x1, x2))
        far = run_mix((0, 1, 2), (x3,))
        moved = [[*moved[r - 1], across(mix2[r], r)] for r in (1, 2)] + [across(far[0], 3)]
        mix2, far, moved, ws, v0, v1 = tie(mix2, far, moved, ws, v0, v1)

        v2, v3 = [*v2, across(v2[2], 1)], [*v3, across(v3[1], 2)]
        mix3 = run_mix((3,), (x0, x1, x2, x3))
        v = [one[r] for r in range(slots) for one in (v0, v1, v2, v3)]
        together = [mix01[0], mix2[0], mix3[0]]
        for r in (1, 2):
            together += [*moved[r - 1], across(mix3[r], r)]
        together += [moved[2], across(mix3[3], 3)]
        order = []
        for r in range(3):
            order += [(3 * r, 0), (3 * r, width), (3 * r + 1, 0), (3 * r + 2, 0)]
        order += [(9, 0), (9, width), (9, 2 * width), (10, 0)]
    else:
        v = lax.all_gather(out_weight, ("dp", "z"))
        block = jnp.concatenate([tokens, edge])
        w, ws = in_weight, []
        for s in range(chips):
            padded = jnp.pad(w, ((0, 0), (0, WIDE - width), (0, 0)))
            ws.append(padded.reshape(3 * WIDE, features))
            if s + 1 < chips:
                w = forward(w)
        blocks = [block] + [across(block, r) for r in range(1, slots)]
        xs = [lay(place, rows, [(0, 0), (1, 0)], [one, swap(one)]) for one in blocks]
        moved = []
        for s in range(chips):
            mixed = []
            for r in range(0, slots, 4):
                mixed += run_mix((s,), xs[r : r + 4])
            mixed = [m[:width] for m in mixed]
            moved.append([mixed[0]] + [across(mixed[r], r) for r in range(1, slots)])
        turn = lax.bitwise_xor(dp, jnp.arange(slots))
        v = [v.reshape(slots, chips, width, -1)[turn][:, origins].reshape(slots * chips * width, -1)]
        together = [jnp.concatenate([one[r] for r in range(slots) for one in moved])]
        order = None
    depth = slots * chips * width
    run = lambda mirror, dtype: project(
        mirror, order, width, depth, place, v, together, dtype
    )
    theirs = swap(run(True, jnp.bfloat16))
    mine = run(False, jnp.float32)
    return (mine + theirs.astype(jnp.float32)).astype(jnp.bfloat16)


def solution(mesh):
    count = mesh.shape["dp"]
    chips = mesh.shape["ctx"] // 2
    fine = Mesh(mesh.devices.reshape(count, chips, 2), ("dp", "z", "core"))
    every = ("dp", "z", "core")
    in_specs = (P(every, None), P(None, every, None), P(), P(), P(every, None))
    return jax.shard_map(
        functools.partial(shards, chips),
        mesh=fine,
        in_specs=in_specs,
        out_specs=P(every, None),
        check_vma=False,
    )
```
